128 devices in a mesh: dp: 32 (over x, z, y_hi), seq: 4 (over y_lo, core).
Axes of the slice: x: 4, y: 4 (y_hi: 2, y_lo: 2; y = y_hi * 2 + y_lo), z: 4, core: 2. Of those that a mesh axis runs over, the one named last changes fastest.
Arguments:
- key_tokens: bfloat16 [32, 1024, 2048], P('dp', 'seq'), may hold values from -4 to 4
- value_tokens: bfloat16 [32, 1024, 2048], P('dp', 'seq'), may hold values from -6 to 6
- query_tokens: bfloat16 [32, 1024, 2048], P('dp', 'seq'), may hold values from -6 to 6
- cotangent: bfloat16 [32, 1024, 2048], P('dp', 'seq'), may hold values from -0.03125 to 0.03125
- base_weight: bfloat16 [2048, 2048], P('dp'), may hold values from -0.125 to 0.125
- factors: float32 [2, 2048, 128], replicated, may hold values from -0.375 to 0.375
Outputs:
- recalled: bfloat16 [32, 1024, 2048], P('dp', 'seq')
- base_grad: float32 [2048, 2048], P('dp')
The draws below stay inside these ranges and needn't reach their ends.
All inputs are finite; a program needn't handle non-finite values.
Results may differ from the reference program's by a relative error of at most 0.0012.
Values may be sent and summed in bfloat16 or wider, within the bound.
No kernel may reach another device: no remote copies, remote signals or barrier semaphores. Data moves between devices by JAX's collectives and lax.ppermute only.
A program may use at most 128 MiB of HBM per device.

```python
import jax
import jax.numpy as jnp
from jax import lax

D = 2048
R = 128
GROUP = 256
DOCS = 32
LENGTH = 1024


def draw_key_tokens(key, part):
    key = jax.random.fold_in(key, 11)
    fresh_key = jax.random.fold_in(key, 1)
    shared_key = jax.random.fold_in(key, 2)
    blocks = LENGTH // GROUP
    fresh = jax.random.normal(fresh_key, (DOCS, blocks, GROUP, D), jnp.float32)
    shared = jax.random.normal(shared_key, (DOCS, 1, GROUP, D), jnp.float32)
    mixed = 0.70710677 * fresh + 0.70710677 * shared
    mixed = jnp.clip(mixed, -4.0, 4.0)
    return mixed.reshape(DOCS, LENGTH, D).astype(jnp.bfloat16)


def levels(stream_key, shape, cuts, least, largest):
    def one(axis_at, parts):
        steps = jax.random.uniform(jax.random.fold_in(jax.random.fold_in(stream_key, 6), axis_at), (parts,), jnp.float32, least / len(cuts), largest / len(cuts))
        return jnp.repeat(jnp.exp(steps), shape[axis_at] // parts).reshape((-1,) + (1,) * (len(shape) - axis_at - 1))

    loudness = one(*cuts[0])
    for cut in cuts[1:]:
        loudness = loudness * one(*cut)
    return loudness


def gaussian(rng, extent, spread, bound, cuts=(), dtype=jnp.bfloat16):
    result = jax.random.normal(rng, extent, jnp.float32) * spread
    if len(cuts) > 0:
        result = levels(rng, extent, cuts, -0.22, 0.18) * result
    return jnp.clip(result, min=-bound, max=bound).astype(dtype)


def setup_inputs(seed: int = 0) -> dict:
    key_of = jax.random.split(jax.random.key(seed), 7)
    return {
        "key_tokens": draw_key_tokens(jax.random.fold_in(key_of[6], 71), 0),
        "value_tokens": gaussian(key_of[1], (DOCS, LENGTH, D), 1.0, 6.0, ((0, 32), (1, 4))),
        "query_tokens": gaussian(key_of[2], (DOCS, LENGTH, D), 1.0, 6.0, ((0, 32), (1, 4))),
        "cotangent": gaussian(key_of[3], (DOCS, LENGTH, D), (DOCS * LENGTH) ** -0.5, 0.03125, ((0, 32), (1, 4))),
        "base_weight": gaussian(key_of[4], (D, D), D ** -0.5, 0.125, ((0, 32),)),
        "factors": gaussian(key_of[5], (2, D, R), (2 * R) ** -0.5, 0.375, (), jnp.float32),
    }


learn_rate = 0.01
highest = lax.Precision.HIGHEST

def memory_step(memory, group_keys, group_values, group_queries, group_proj):
    left_factor = memory[:, 0]
    right_factor = memory[:, 1]
    key_left = jnp.einsum('btd,bdr->btr', group_keys, left_factor, precision=highest)
    query_left = jnp.einsum('btd,bdr->btr', group_queries, left_factor, precision=highest)
    lowrank = jnp.einsum('btr,bdr->btd', query_left, right_factor, precision=highest)
    residue = group_proj + jnp.einsum('btr,bdr->btd', key_left, right_factor, precision=highest) - group_values
    residue_right = jnp.einsum('btd,bdr->btr', residue, right_factor, precision=highest)
    step_left = jnp.einsum('btd,btr->bdr', group_keys, residue_right, precision=highest) / GROUP
    step_right = jnp.einsum('btd,btr->bdr', residue, key_left, precision=highest) / GROUP
    updated = jnp.stack([left_factor - learn_rate * step_left, right_factor - learn_rate * step_right], axis=1)
    return (updated, lowrank)

def run_document(key_proj, key_wide, value_wide, query_wide, factors):
    blocks = LENGTH // GROUP

    def advance(memory, inputs):
        proj_block, key_block, value_block, query_block = inputs
        return memory_step(memory, key_block, value_block, query_block, proj_block)

    def split(array):
        return array.reshape(blocks, 1, GROUP, D)
    _, lowrank = lax.scan(advance, factors[None], (split(key_proj), split(key_wide), split(value_wide), split(query_wide)))
    return lowrank.reshape(LENGTH, D)

def reference(key_tokens, value_tokens, query_tokens, cotangent, base_weight, factors):

    def per_document(running, inputs):
        key_doc, value_doc, query_doc, cot_doc = inputs
        key_proj = jnp.dot(key_doc, base_weight, preferred_element_type=jnp.float32)
        query_proj = jnp.dot(query_doc, base_weight, preferred_element_type=jnp.float32)
        key_wide = key_doc.astype(jnp.float32)
        value_wide = value_doc.astype(jnp.float32)
        query_wide = query_doc.astype(jnp.float32)

        def lowrank_of(proj):
            return run_document(proj, key_wide, value_wide, query_wide, factors)
        lowrank, pullback = jax.vjp(lowrank_of, key_proj)
        proj_grad, = pullback(cot_doc.astype(jnp.float32))
        recalled = (query_proj + lowrank).astype(jnp.bfloat16)
        grad_half = proj_grad.astype(jnp.bfloat16)
        contract = (((0,), (0,)), ((), ()))
        running = running + lax.dot_general(key_doc, grad_half, contract, preferred_element_type=jnp.float32)
        running = running + lax.dot_general(query_doc, cot_doc, contract, preferred_element_type=jnp.float32)
        return (running, recalled)
    start_grad = jnp.zeros((D, D), jnp.float32)
    base_grad, recalled = lax.scan(per_document, start_grad, (key_tokens, value_tokens, query_tokens, cotangent))
    return (recalled, base_grad)
```

```python
import jax
import jax.numpy as jnp
from jax import lax
from jax.sharding import Mesh, PartitionSpec as P

GROUP = 256
DP = ("x", "z", "yh")
SEQ = ("yl", "c")
CHIPS = ("x", "z", "yh", "yl")

learn_rate = 0.01
highest = lax.Precision.HIGHEST


def swap_cores(value):
    return lax.ppermute(value, "c", [(0, 1), (1, 0)])


def memory_step(memory, group_keys, group_values, group_queries, group_proj):
    left_factor = memory[:, 0]
    right_factor = memory[:, 1]
    key_left = jnp.einsum("btd,bdr->btr", group_keys, left_factor, precision=highest)
    query_left = jnp.einsum("btd,bdr->btr", group_queries, left_factor, precision=highest)
    lowrank = jnp.einsum("btr,bdr->btd", query_left, right_factor, precision=highest)
    residue = (
        group_proj
        + jnp.einsum("btr,bdr->btd", key_left, right_factor, precision=highest)
        - group_values
    )
    residue_right = jnp.einsum("btd,bdr->btr", residue, right_factor, precision=highest)
    step_left = jnp.einsum("btd,btr->bdr", group_keys, residue_right, precision=highest) / GROUP
    step_right = jnp.einsum("btd,btr->bdr", residue, key_left, precision=highest) / GROUP
    updated = jnp.stack(
        [left_factor - learn_rate * step_left, right_factor - learn_rate * step_right], axis=1
    )
    return (updated, lowrank)


def per_device(key_tokens, value_tokens, query_tokens, cotangent, base_weight, factors):
    _, slice_len, width = key_tokens.shape
    half = width // 2
    core = lax.axis_index("c")
    position = lax.axis_index("yl") * 2 + core
    seq_count = 4

    def own_half(array):
        return lax.dynamic_slice_in_dim(array, core * half, half, 1)

    def other_half(array):
        return lax.dynamic_slice_in_dim(array, (1 - core) * half, half, 1)

    def join_halves(own, other):
        return jnp.where(
            core == 0, jnp.concatenate([own, other], 1), jnp.concatenate([other, own], 1)
        )

    keys, values, queries, cot = (a[0] for a in (key_tokens, value_tokens, query_tokens, cotangent))
    stacked = jnp.concatenate([keys, queries], 0)
    stacked_sibling = swap_cores(stacked)
    cot_sibling = swap_cores(other_half(cot))

    rows = base_weight.shape[0]
    mine = own_half(base_weight)
    weight = lax.all_to_all(
        jnp.broadcast_to(mine[None], (width // rows, rows, half)), DP, 0, 0, tiled=True
    ).reshape(width, half)

    projected_sibling = jnp.dot(stacked_sibling, weight, preferred_element_type=jnp.float32)
    projected = jnp.dot(stacked, weight, preferred_element_type=jnp.float32)
    projected = join_halves(projected, swap_cores(projected_sibling))
    key_proj = projected[None, :slice_len]
    query_proj = projected[None, slice_len:]
    key_wide = key_tokens.astype(jnp.float32)
    value_wide = value_tokens.astype(jnp.float32)
    query_wide = query_tokens.astype(jnp.float32)

    def local_chain(proj, memory):
        memory, lowrank = memory_step(memory, key_wide, value_wide, query_wide, proj)
        return (lowrank, memory)

    memory = factors[None]
    for step in range(seq_count - 1):
        _, passed = local_chain(key_proj, memory)
        moved = lax.ppermute(passed, SEQ, [(step, step + 1)])
        memory = jnp.where(position == step + 1, moved, memory)
    (lowrank, final_memory), pullback = jax.vjp(local_chain, key_proj, memory)
    recalled = (query_proj + lowrank).astype(jnp.bfloat16)
    cot_wide = cotangent.astype(jnp.float32)
    memory_cot = jnp.zeros_like(final_memory)
    for step in reversed(range(seq_count - 1)):
        _, memory_grad = pullback((cot_wide, memory_cot))
        moved = lax.ppermute(memory_grad.astype(jnp.bfloat16), SEQ, [(step + 1, step)])
        memory_cot = jnp.where(position == step, moved.astype(memory_grad.dtype), memory_cot)
    proj_grad, _ = pullback((cot_wide, memory_cot))
    proj_grad = proj_grad[0].astype(jnp.bfloat16)
    proj_sibling = swap_cores(other_half(proj_grad))

    grad_left = jnp.concatenate([stacked, stacked_sibling], 0)
    grad_right = jnp.concatenate([own_half(proj_grad), own_half(cot), proj_sibling, cot_sibling], 0)
    partial = lax.dot_general(
        grad_left, grad_right, (((0,), (0,)), ((), ())), preferred_element_type=jnp.float32
    )
    peak = jnp.max(jnp.abs(partial), axis=1, keepdims=True)
    power = jnp.clip(jnp.ceil(jnp.log2(jnp.maximum(peak, 1e-30))), -100.0, 120.0)
    scaled = (partial * jnp.exp2(-power)).astype(jnp.float16)
    beside = jnp.broadcast_to(power, (width, 128)).astype(jnp.float16)
    sent = jnp.concatenate([scaled, beside], 1)
    got = lax.all_to_all(sent, CHIPS, 0, 0, tiled=True).reshape(64, rows // 2, half + 128)
    factor = jnp.exp2(got[:, :, half : half + 1].astype(jnp.float32))
    share = jnp.sum(got[:, :, :half].astype(jnp.float32) * factor, 0)
    share = join_halves(share, swap_cores(share))
    share_other = lax.ppermute(share, "yl", [(0, 1), (1, 0)])
    base_grad = jnp.where(
        lax.axis_index("yl") == 0,
        jnp.concatenate([share, share_other], 0),
        jnp.concatenate([share_other, share], 0),
    )
    return (recalled, base_grad)


def solution(mesh):
    fine = Mesh(mesh.devices.reshape(4, 4, 2, 2, 2), ("x", "z", "yh", "yl", "c"))
    tokens = P(DP, SEQ, None)
    in_specs = (tokens, tokens, tokens, tokens, P(DP, None), P())
    out_specs = (tokens, P(DP, None))
    return jax.shard_map(
        per_device, mesh=fine, in_specs=in_specs, out_specs=out_specs, check_vma=False
    )
```

```python
import jax
import jax.numpy as jnp
import numpy as np
from jax import lax
from jax.experimental import pallas as pl
from jax.experimental.pallas import tpu as pltpu
from jax.sharding import Mesh, PartitionSpec as P

GROUP = 256
RANK = 128
CHUNK = 512
RATE = 0.01 / GROUP
f32 = jnp.float32
bf16 = jnp.bfloat16


def nt(a, b):
    return lax.dot_general(a, b, (((1,), (1,)), ((), ())), preferred_element_type=f32)


def nn(a, b):
    return lax.dot_general(a, b, (((1,), (0,)), ((), ())), preferred_element_type=f32)


def split(x):
    high = x.astype(bf16)
    return high, (x - high.astype(f32)).astype(bf16)


def fold_lanes(x):
    return x[:, :RANK] + x[:, RANK:]


def fold_rows(x):
    return x[:RANK] + x[RANK:]


def small(x, y):
    xh, xl = split(x)
    yh, yl = split(y)
    return nn(xh, yh) + nn(xl, yh) + nn(xh, yl)


def stack_pair(x):
    return jnp.concatenate(split(x), 0)


def gram(pair_a, pair_b):
    return fold_lanes(fold_rows(nt(pair_a, pair_b)))


def chunks(width):
    return [pl.ds(j, CHUNK) for j in range(0, width, CHUNK)]


def split_state(state, left_pair, right_pair):
    for cols in chunks(state.shape[-1]):
        for part, pair in ((0, left_pair), (1, right_pair)):
            high, low = split(state[part, :, cols])
            pair[0:RANK, cols] = high
            pair[RANK:, cols] = low


def forward_block(keys, values, proj, state, left_pair, right_pair, err_high, err_low, update):
    width = keys.shape[-1]
    hidden = fold_lanes(nt(keys[...], left_pair[...]))
    high, low = split(hidden)
    twice = jnp.concatenate([high, high], 1)
    for cols in chunks(width):
        err = (
            proj[:, cols]
            - values[:, cols].astype(f32)
            + (nn(twice, right_pair[:, cols]) + nn(low, right_pair[0:RANK, cols]))
        )
        eh, el = split(err)
        err_high[:, cols] = eh
        err_low[:, cols] = el
    if not update:
        return hidden
    back = fold_lanes(nt(err_high[...], right_pair[...])) + nt(err_low[...], right_pair[0:RANK, :])
    back_pair = stack_pair((-RATE * back).T)
    hidden_pair = stack_pair((-RATE * hidden).T)
    for cols in chunks(width):
        state[0, :, cols] += fold_rows(nn(back_pair, keys[:, cols]))
        state[1, :, cols] += fold_rows(nn(hidden_pair, err_high[:, cols])) + nn(
            hidden_pair[0:RANK], err_low[:, cols]
        )
    return hidden


def backward_hidden(keys, right_pair, err_high, err_low, hidden, gram_right, cot_left, cot_right):
    back_cot = -RATE * fold_lanes(nt(keys[...], cot_left[...]))
    err_cot = fold_lanes(nt(err_high[...], cot_right[...])) + nt(err_low[...], cot_right[0:RANK, :])
    mixed = gram(cot_right[...], right_pair[...])
    hidden_cot = -RATE * (err_cot + small(hidden, mixed)) + small(back_cot, gram_right)
    return back_cot, hidden_cot


def backward_state(
    keys, right_pair, err_high, err_low, hidden, back_cot, hidden_cot, cot, cot_left, cot_right, given_left, given_right
):
    hidden_t = hidden.T
    back_t = back_cot.T
    own = -RATE * small(hidden_t, hidden)
    cross = small(hidden_t, back_cot)
    own_h, own_l = split(own)
    own_twice = jnp.concatenate([own_h, own_h], 1)
    cross_h, cross_l = split(cross)
    cross_twice = jnp.concatenate([cross_h, cross_h], 1)
    lows = jnp.concatenate([own_l, cross_l], 1)
    hidden_cot_pair = stack_pair(hidden_cot.T)
    back_pair = stack_pair(back_t)
    for cols in chunks(keys.shape[-1]):
        left = cot[0, :, cols] + given_left(cols) + fold_rows(nn(hidden_cot_pair, keys[:, cols]))
        right = (
            cot[1, :, cols]
            + given_right(cols)
            + fold_rows(nn(back_pair, err_high[:, cols]))
            + nn(back_pair[0:RANK], err_low[:, cols])
            + nn(own_twice, cot_right[:, cols])
            + nn(cross_twice, right_pair[:, cols])
            + nn(own_l, cot_right[0:RANK, cols])
            + nn(cross_l, right_pair[0:RANK, cols])
        )
        cot[0, :, cols] = left
        cot[1, :, cols] = right
        for value, pair in ((left, cot_left), (right, cot_right)):
            high, low = split(value)
            pair[0:RANK, cols] = high
            pair[RANK:, cols] = low


def first_kernel(
    pos, keys_own, keys_sib, values_own, values_sib, queries_own, queries_sib, cots_own, cots_sib,
    fkeys_own, fkeys_sib, fvalues_own, fvalues_sib, proj_mine, proj_got, fproj_mine, fproj_got, factors,
    sent, err_high_out, err_low_out, right_out, given_out, hidden_out, gram_out, recall_hidden_out, state_out,
    k, v, q, c, p, fk, fv, fp, err_high, err_low, state, left_pair, right_pairs, cot, cot_left, cot_right, given,
    sems, out_sems,
):
    second = pos[0]
    core = pos[1]
    half = proj_mine.shape[-1]
    mine_rows = pl.ds(pl.multiple_of(core * GROUP, GROUP), GROUP)
    sib_rows = pl.ds(pl.multiple_of((1 - core) * GROUP, GROUP), GROUP)
    mine_cols = pl.ds(pl.multiple_of(core * half, half), half)
    sib_cols = pl.ds(pl.multiple_of((1 - core) * half, half), half)

    def token_pair(own, sib, into, at):
        return [
            pltpu.make_async_copy(own, into.at[mine_rows, :], sems.at[at]),
            pltpu.make_async_copy(sib, into.at[sib_rows, :], sems.at[at + 1]),
        ]

    def proj_four(mine, got, into, at):
        first, last = pl.ds(0, GROUP), pl.ds(GROUP, GROUP)
        return [
            pltpu.make_async_copy(mine.at[first, :], into.at[mine_rows, mine_cols], sems.at[at]),
            pltpu.make_async_copy(mine.at[last, :], into.at[sib_rows, mine_cols], sems.at[at + 1]),
            pltpu.make_async_copy(got.at[first, :], into.at[sib_rows, sib_cols], sems.at[at + 2]),
            pltpu.make_async_copy(got.at[last, :], into.at[mine_rows, sib_cols], sems.at[at + 3]),
        ]

    load_state = [pltpu.make_async_copy(factors, state, sems.at[0])]
    load_f = (
        token_pair(fkeys_own, fkeys_sib, fk, 1)
        + proj_four(fproj_mine, fproj_got, fp, 3)
        + token_pair(fvalues_own, fvalues_sib, fv, 7)
    )
    load_own = (
        token_pair(keys_own, keys_sib, k, 9)
        + proj_four(proj_mine, proj_got, p, 11)
        + token_pair(values_own, values_sib, v, 15)
    )
    load_late = token_pair(queries_own, queries_sib, q, 17) + token_pair(cots_own, cots_sib, c, 19)

    for copy in load_state:
        copy.start()

    @pl.when(second == 1)
    def _():
        for copy in load_f:
            copy.start()

    for copy in load_own + load_late:
        copy.start()
    for copy in load_state:
        copy.wait()

    rows = [pl.ds(0, GROUP), pl.ds(GROUP, GROUP)]

    @pl.when(second == 1)
    def _():
        for copy in load_f:
            copy.wait()
        for block in rows:
            split_state(state, left_pair, right_pairs.at[0])
            forward_block(
                fk.at[block, :], fv.at[block, :], fp.at[block, :], state, left_pair, right_pairs.at[0],
                err_high.at[block, :], err_low.at[block, :], True,
            )

    for copy in load_own:
        copy.wait()
    outs = []
    hiddens = []
    grams = []
    recall = []
    for i, block in enumerate(rows):
        pair = right_pairs.at[i]
        split_state(state, left_pair, pair)

        @pl.when(core == i)
        def _():
            state_out[...] = state[1, :, :]

        if i == 0:
            for copy in load_late:
                copy.wait()
        read = fold_lanes(nt(q[block, :], left_pair[...]))
        recall.append(read)
        hidden = forward_block(
            k.at[block, :], v.at[block, :], p.at[block, :], state, left_pair, pair,
            err_high.at[block, :], err_low.at[block, :], i == 0,
        )
        hiddens.append(hidden)
        grams.append(gram(pair[...], pair[...]))
        hidden_out[i] = hidden
        gram_out[i] = grams[i]
        more = [
            pltpu.make_async_copy(err_high.at[block, :], err_high_out.at[block, :], out_sems.at[3 * i]),
            pltpu.make_async_copy(err_low.at[block, :], err_low_out.at[block, :], out_sems.at[3 * i + 1]),
            pltpu.make_async_copy(pair, right_out.at[i], out_sems.at[3 * i + 2]),
        ]
        for copy in more:
            copy.start()
        outs += more

    @pl.when(core == 0)
    def _():
        recall_hidden_out[...] = recall[0]

    @pl.when(core == 1)
    def _():
        recall_hidden_out[...] = recall[1]

    for i in (1, 0):
        block = rows[i]
        pair = right_pairs.at[i]
        spread = stack_pair(fold_lanes(nt(c[block, :], pair[...])).T)
        read = stack_pair(recall[i].T)
        for cols in chunks(k.shape[-1]):
            given[i, 0, :, cols] = fold_rows(nn(spread, q[block, cols]))
            given[i, 1, :, cols] = fold_rows(nn(read, c[block, cols]))
    copy = pltpu.make_async_copy(given.at[1], given_out, out_sems.at[6])
    copy.start()
    outs.append(copy)

    for cols in chunks(k.shape[-1]):
        for part, pair in ((0, cot_left), (1, cot_right)):
            value = given[1, part, :, cols]
            cot[part, :, cols] = value
            high, low = split(value)
            pair[0:RANK, cols] = high
            pair[RANK:, cols] = low
    block = rows[0]
    back_cot, hidden_cot = backward_hidden(
        k.at[block, :], right_pairs.at[0], err_high.at[block, :], err_low.at[block, :], hiddens[0], grams[0], cot_left, cot_right
    )
    backward_state(
        k.at[block, :], right_pairs.at[0], err_high.at[block, :], err_low.at[block, :], hiddens[0], back_cot, hidden_cot,
        cot, cot_left, cot_right, lambda cols: given[0, 0, :, cols], lambda cols: given[0, 1, :, cols],
    )
    sent[0:RANK, :] = cot_left[0:RANK, mine_cols]
    sent[RANK:, :] = cot_right[0:RANK, mine_cols]
    for copy in outs:
        copy.wait()


def first_call(pos, *arrays):
    width = arrays[0].shape[1]
    two = 2 * GROUP
    any_spec = pl.BlockSpec(memory_space=pl.ANY)
    vmem = pl.BlockSpec(memory_space=pltpu.VMEM)
    out_shape = (
        jax.ShapeDtypeStruct((2 * RANK, width // 2), bf16),
        jax.ShapeDtypeStruct((two, width), bf16),
        jax.ShapeDtypeStruct((two, width), bf16),
        jax.ShapeDtypeStruct((2, 2 * RANK, width), bf16),
        jax.ShapeDtypeStruct((2, RANK, width), f32),
        jax.ShapeDtypeStruct((2, GROUP, RANK), f32),
        jax.ShapeDtypeStruct((2, RANK, RANK), f32),
        jax.ShapeDtypeStruct((GROUP, RANK), f32),
        jax.ShapeDtypeStruct((RANK, width), f32),
    )
    tokens = pltpu.VMEM((two, width), bf16)
    wide = pltpu.VMEM((two, width), f32)
    pair = pltpu.VMEM((2 * RANK, width), bf16)
    return pl.pallas_call(
        first_kernel,
        out_shape=out_shape,
        in_specs=[pl.BlockSpec(memory_space=pltpu.SMEM)] + [any_spec] * len(arrays),
        out_specs=(vmem, any_spec, any_spec, any_spec, any_spec, vmem, vmem, vmem, vmem),
        scratch_shapes=[
            tokens, tokens, tokens, tokens, wide, tokens, tokens, wide, tokens, tokens,
            pltpu.VMEM((2, RANK, width), f32), pair, pltpu.VMEM((2, 2 * RANK, width), bf16),
            pltpu.VMEM((2, RANK, width), f32), pair, pair, pltpu.VMEM((2, 2, RANK, width), f32),
            pltpu.SemaphoreType.DMA((21,)), pltpu.SemaphoreType.DMA((7,)),
        ],
        compiler_params=pltpu.CompilerParams(vmem_limit_bytes=56 * 2**20),
        cost_estimate=pl.CostEstimate(flops=20 * 10**9, bytes_accessed=30 * 2**20, transcendentals=0),
    )(pos, *arrays)


def second_kernel(
    pos, got_mine, got_sib, keys_own, keys_sib, err_high_in, err_low_in, right_in, given_in, hidden_in, gram_in,
    grad_out,
    k, err_high, err_low, right_pairs, given, received, cot, cot_left, cot_right, sems,
):
    core = pos[1]
    width = keys_own.shape[-1]
    half = width // 2
    mine_rows = pl.ds(pl.multiple_of(core * GROUP, GROUP), GROUP)
    sib_rows = pl.ds(pl.multiple_of((1 - core) * GROUP, GROUP), GROUP)
    mine_cols = pl.ds(pl.multiple_of(core * half, half), half)
    sib_cols = pl.ds(pl.multiple_of((1 - core) * half, half), half)
    rows = [pl.ds(0, GROUP), pl.ds(GROUP, GROUP)]
    load_cot = [
        pltpu.make_async_copy(got_mine, received.at[:, mine_cols], sems.at[0]),
        pltpu.make_async_copy(got_sib, received.at[:, sib_cols], sems.at[1]),
    ]
    load_keys = [
        pltpu.make_async_copy(keys_own, k.at[mine_rows, :], sems.at[2]),
        pltpu.make_async_copy(keys_sib, k.at[sib_rows, :], sems.at[3]),
    ]

    def load_block(i):
        return [
            pltpu.make_async_copy(right_in.at[i], right_pairs.at[i], sems.at[4 + 3 * i]),
            pltpu.make_async_copy(err_high_in.at[rows[i], :], err_high.at[rows[i], :], sems.at[5 + 3 * i]),
            pltpu.make_async_copy(err_low_in.at[rows[i], :], err_low.at[rows[i], :], sems.at[6 + 3 * i]),
        ]

    load_given = [pltpu.make_async_copy(given_in, given, sems.at[10])]
    loads = [load_cot + load_keys + load_block(1), load_given + load_block(0)]
    for copy in loads[0] + loads[1]:
        copy.start()
    for copy in loads[0]:
        copy.wait()
    for cols in chunks(width):
        for part, pair in ((0, cot_left), (1, cot_right)):
            value = received[part * RANK : (part + 1) * RANK, cols]
            cot[part, :, cols] = value.astype(f32)
            pair[0:RANK, cols] = value
            pair[RANK:, cols] = jnp.zeros((RANK, CHUNK), bf16)

    for i in (1, 0):
        block = rows[i]
        keys, eh, el, pair = k.at[block, :], err_high.at[block, :], err_low.at[block, :], right_pairs.at[i]
        hidden = hidden_in[i]
        back_cot, hidden_cot = backward_hidden(keys, pair, eh, el, hidden, gram_in[i], cot_left, cot_right)
        scaled = -RATE * hidden
        sh, sl = split(scaled)
        bh, bl = split(back_cot)
        s_twice = jnp.concatenate([sh, sh], 1)
        b_twice = jnp.concatenate([bh, bh], 1)
        out_rows = mine_rows if i == 0 else sib_rows
        for j in range(0, half, CHUNK):
            cols = pl.ds(pl.multiple_of(core * half + j, CHUNK), CHUNK)
            grad = (
                nn(s_twice, cot_right[:, cols])
                + nn(b_twice, pair[:, cols])
                + nn(sl, cot_right[0:RANK, cols])
                + nn(bl, pair[0:RANK, cols])
            ).astype(bf16)

            @pl.when(core == i)
            def _():
                grad_out[0:GROUP, j : j + CHUNK] = grad

            @pl.when(core != i)
            def _():
                grad_out[GROUP:, j : j + CHUNK] = grad

        if i == 1:
            for copy in loads[1]:
                copy.wait()
            backward_state(
                keys, pair, eh, el, hidden, back_cot, hidden_cot, cot, cot_left, cot_right,
                lambda cols: given[0, :, cols], lambda cols: given[1, :, cols],
            )


def second_call(pos, got_mine, got_sib, keys_own, keys_sib, *saved):
    width = keys_own.shape[1]
    two = 2 * GROUP
    any_spec = pl.BlockSpec(memory_space=pl.ANY)
    vmem = pl.BlockSpec(memory_space=pltpu.VMEM)
    tokens = pltpu.VMEM((two, width), bf16)
    pair = pltpu.VMEM((2 * RANK, width), bf16)
    return pl.pallas_call(
        second_kernel,
        out_shape=jax.ShapeDtypeStruct((two, width // 2), bf16),
        in_specs=[pl.BlockSpec(memory_space=pltpu.SMEM)] + [any_spec] * 8 + [vmem] * 2,
        out_specs=vmem,
        scratch_shapes=[
            tokens, tokens, tokens, pltpu.VMEM((2, 2 * RANK, width), bf16),
            pltpu.VMEM((2, RANK, width), f32), pair, pltpu.VMEM((2, RANK, width), f32), pair, pair,
            pltpu.SemaphoreType.DMA((11,)),
        ],
        compiler_params=pltpu.CompilerParams(vmem_limit_bytes=40 * 2**20),
        cost_estimate=pl.CostEstimate(flops=10 * 10**9, bytes_accessed=14 * 2**20, transcendentals=0),
    )(pos, got_mine, got_sib, keys_own, keys_sib, *saved)


def block_of(pos, far, near):
    core, along_x, along_z = pos[1], pos[2], pos[3]
    by_x = lax.rem(along_x + 4 - jnp.where(core == 0, far, near), 4)
    by_z = lax.rem(along_z + 4 - jnp.where(core == 0, near, far), 4)
    return by_x * 4 + by_z


def project_kernel(pos, piece0, piece1, piece2, piece3, tokens_own, tokens_sib, out, weight, sems):
    copies = [
        pltpu.make_async_copy(piece, weight.at[far], sems.at[far])
        for far, piece in enumerate((piece0, piece1, piece2, piece3))
    ]
    for copy in copies:
        copy.start()
    for far, copy in enumerate(copies):
        copy.wait()
        for part, tokens in enumerate((tokens_own, tokens_sib)):
            left = jnp.concatenate(
                [
                    tokens[:, pl.ds(pl.multiple_of(block_of(pos, far, near) * 128, 128), 128)]
                    for near in range(4)
                ],
                1,
            )
            rows = slice(part * GROUP, (part + 1) * GROUP)
            for at in range(0, out.shape[1], CHUNK):
                cols = slice(at, at + CHUNK)
                term = nn(left, weight[far, :, cols])
                if far == 0:
                    out[rows, cols] = term
                else:
                    out[rows, cols] += term


def project_call(pos, pieces, tokens_own, tokens_sib):
    depth, half = pieces[0].shape
    any_spec = pl.BlockSpec(memory_space=pl.ANY)
    vmem = pl.BlockSpec(memory_space=pltpu.VMEM)
    return pl.pallas_call(
        project_kernel,
        out_shape=jax.ShapeDtypeStruct((2 * GROUP, half), f32),
        in_specs=[pl.BlockSpec(memory_space=pltpu.SMEM)] + [any_spec] * 4 + [vmem] * 2,
        out_specs=vmem,
        scratch_shapes=[pltpu.VMEM((4, depth, half), bf16), pltpu.SemaphoreType.DMA((4,))],
        compiler_params=pltpu.CompilerParams(vmem_limit_bytes=24 * 2**20),
        cost_estimate=pl.CostEstimate(flops=2 * 512 * 2048 * 1024, bytes_accessed=8 * 2**20, transcendentals=0),
    )(pos, *pieces, tokens_own, tokens_sib)


DP = ("x", "z", "yh")
SEQ = ("yl", "c")
CHIPS = ("x", "z", "yh", "yl")
ALL = ("x", "z", "yh", "yl", "c")
SIZES = (4, 4, 2, 2, 2)


def swap_cores(value):
    return lax.ppermute(value, "c", [(0, 1), (1, 0)])


def ring_pairs(by, x_core):
    pairs = []
    for place in np.ndindex(*SIZES):
        there = list(place)
        axis = 0 if place[4] == x_core else 1
        there[axis] = (place[axis] + by) % 4
        pairs.append((int(np.ravel_multi_index(place, SIZES)), int(np.ravel_multi_index(there, SIZES))))
    return pairs


def after(value, *others):
    return lax.optimization_barrier((value, *others))[0]


def gather_weight(mine):
    across = lax.ppermute(mine, ("yh", "yl"), [(0, 3), (3, 0), (1, 2), (2, 1)])
    pair = jnp.where(
        lax.axis_index("yh") == 0,
        jnp.concatenate([mine, across], 0),
        jnp.concatenate([across, mine], 0),
    )
    near = [pair] + [lax.ppermute(pair, ALL, ring_pairs(by, 1)) for by in (1, 2, 3)]
    near = jnp.concatenate(near, 0)
    far = [near] + [lax.ppermute(near, ALL, ring_pairs(by, 0)) for by in (1, 2, 3)]
    return far, across


def per_device(key_tokens, value_tokens, query_tokens, cotangent, base_weight, factors):
    _, slice_len, width = key_tokens.shape
    half = width // 2
    rows = base_weight.shape[0]
    core = lax.axis_index("c")
    place = jnp.stack([lax.axis_index(a) for a in ("yl", "c", "x", "z")]).astype(jnp.int32)

    def own_half(array):
        return lax.dynamic_slice_in_dim(array, core * half, half, 1)

    def join_halves(own, other):
        return jnp.where(
            core == 0, jnp.concatenate([own, other], 1), jnp.concatenate([other, own], 1)
        )

    keys, values, queries, cots = (a[0] for a in (key_tokens, value_tokens, query_tokens, cotangent))
    pieces, across = gather_weight(own_half(base_weight))
    keys_sib = swap_cores(keys)
    onward = [(0, 1)]
    fkeys = lax.ppermute(after(keys, across), "yl", onward)
    fvalues = lax.ppermute(after(values, fkeys), "yl", onward)
    queries_sib, cots_sib, values_sib = swap_cores(queries), swap_cores(cots), swap_cores(values)
    fkeys_sib, fvalues_sib = swap_cores(fkeys), swap_cores(fvalues)

    fproj = project_call(place, pieces, fkeys, fkeys_sib)
    fproj_got = swap_cores(fproj)
    proj = project_call(place, pieces, keys, keys_sib)
    proj_got = swap_cores(proj)

    (sent, err_high, err_low, right, given, hidden, grams, recall_hidden, recall_right) = first_call(
        place, keys, keys_sib, values, values_sib, queries, queries_sib, cots, cots_sib,
        fkeys, fkeys_sib, fvalues, fvalues_sib, proj, proj_got, fproj, fproj_got, jnp.swapaxes(factors, 1, 2),
    )
    got = lax.ppermute(sent, "yl", [(1, 0)])
    got_sib = swap_cores(got)

    qproj = project_call(after(place, sent), pieces, queries, queries_sib)
    qproj = join_halves(qproj[:slice_len], swap_cores(qproj[slice_len:]))
    low = jnp.dot(recall_hidden, recall_right, precision=lax.Precision.HIGHEST)
    recalled = (qproj + low).astype(bf16)[None]

    grad = second_call(place, got, got_sib, keys, keys_sib, err_high, err_low, right, given, hidden, grams)
    grad_left = jnp.concatenate([keys, keys_sib, queries, queries_sib], 0)
    grad_right = jnp.concatenate([grad, own_half(cots), own_half(cots_sib)], 0)
    partial = lax.dot_general(
        grad_left, grad_right, (((0,), (0,)), ((), ())), preferred_element_type=jnp.float32
    )
    peak = jnp.max(jnp.abs(partial), axis=1, keepdims=True)
    power = jnp.clip(jnp.ceil(jnp.log2(jnp.maximum(peak, 1e-30))), -100.0, 120.0)
    scaled = (partial * jnp.exp2(-power)).astype(jnp.float16)
    beside = jnp.broadcast_to(power, (width, 128)).astype(jnp.float16)
    message = jnp.concatenate([scaled, beside], 1)
    message = lax.all_to_all(message, CHIPS, 0, 0, tiled=True).reshape(64, rows // 2, half + 128)
    factor = jnp.exp2(message[:, :, half : half + 1].astype(jnp.float32))
    share = jnp.sum(message[:, :, :half].astype(jnp.float32) * factor, 0)
    share = join_halves(share, swap_cores(share))
    share_other = lax.ppermute(share, "yl", [(0, 1), (1, 0)])
    base_grad = jnp.where(
        lax.axis_index("yl") == 0,
        jnp.concatenate([share, share_other], 0),
        jnp.concatenate([share_other, share], 0),
    )
    return (recalled, base_grad)


def solution(mesh):
    fine = Mesh(mesh.devices.reshape(SIZES), ALL)
    tokens = P(DP, SEQ, None)
    in_specs = (tokens, tokens, tokens, tokens, P(DP, None), P())
    out_specs = (tokens, P(DP, None))
    return jax.shard_map(
        per_device, mesh=fine, in_specs=in_specs, out_specs=out_specs, check_vma=False
    )
```

```python
import functools

import jax
import jax.numpy as jnp
import numpy as np
from jax import lax
from jax.experimental import pallas as pl
from jax.experimental.pallas import tpu as pltpu
from jax.sharding import Mesh, PartitionSpec as P

GROUP = 256
RANK = 128
CHUNK = 512
VMEM = 60 * 2**20
RATE = 0.01 / GROUP
f32 = jnp.float32
bf16 = jnp.bfloat16


def nt(a, b):
    return lax.dot_general(a, b, (((1,), (1,)), ((), ())), preferred_element_type=f32)


def nn(a, b):
    return lax.dot_general(a, b, (((1,), (0,)), ((), ())), preferred_element_type=f32)


def split(x):
    high = x.astype(bf16)
    return high, (x - high.astype(f32)).astype(bf16)


def fold_lanes(x):
    return x[:, :RANK] + x[:, RANK:]


def fold_rows(x):
    return x[:RANK] + x[RANK:]


def small(x, y):
    xh, xl = split(x)
    yh, yl = split(y)
    return nn(xh, yh) + nn(xl, yh) + nn(xh, yl)


def stack_pair(x):
    return jnp.concatenate(split(x), 0)


def gram(pair_a, pair_b):
    return fold_lanes(fold_rows(nt(pair_a, pair_b)))


def chunks(width):
    return [pl.ds(j, CHUNK) for j in range(0, width, CHUNK)]


def split_state(state, left_pair, right_pair):
    for cols in chunks(state.shape[-1]):
        for part, pair in ((0, left_pair), (1, right_pair)):
            high, low = split(state[part, :, cols])
            pair[0:RANK, cols] = high
            pair[RANK:, cols] = low


def forward_block(keys, values, proj, state, left_pair, right_pair, err_high, err_low, update):
    width = keys.shape[-1]
    hidden = fold_lanes(nt(keys[...], left_pair[...]))
    high, low = split(hidden)
    twice = jnp.concatenate([high, high], 1)
    for cols in chunks(width):
        err = (
            proj[:, cols]
            - values[:, cols].astype(f32)
            + (nn(twice, right_pair[:, cols]) + nn(low, right_pair[0:RANK, cols]))
        )
        eh, el = split(err)
        err_high[:, cols] = eh
        err_low[:, cols] = el
    if not update:
        return hidden
    back = fold_lanes(nt(err_high[...], right_pair[...])) + nt(err_low[...], right_pair[0:RANK, :])
    back_pair = stack_pair((-RATE * back).T)
    hidden_pair = stack_pair((-RATE * hidden).T)
    for cols in chunks(width):
        state[0, :, cols] += fold_rows(nn(back_pair, keys[:, cols]))
        state[1, :, cols] += fold_rows(nn(hidden_pair, err_high[:, cols])) + nn(
            hidden_pair[0:RANK], err_low[:, cols]
        )
    return hidden


def backward_hidden(keys, right_pair, err_high, err_low, hidden, gram_right, cot_left, cot_right):
    back_cot = -RATE * fold_lanes(nt(keys[...], cot_left[...]))
    err_cot = fold_lanes(nt(err_high[...], cot_right[...])) + nt(err_low[...], cot_right[0:RANK, :])
    mixed = gram(cot_right[...], right_pair[...])
    hidden_cot = -RATE * (err_cot + small(hidden, mixed)) + small(back_cot, gram_right)
    return back_cot, hidden_cot


def backward_state(
    keys, right_pair, err_high, err_low, hidden, back_cot, hidden_cot, cot, cot_left, cot_right, given_left, given_right
):
    hidden_t = hidden.T
    back_t = back_cot.T
    own = -RATE * small(hidden_t, hidden)
    cross = small(hidden_t, back_cot)
    own_h, own_l = split(own)
    own_twice = jnp.concatenate([own_h, own_h], 1)
    cross_h, cross_l = split(cross)
    cross_twice = jnp.concatenate([cross_h, cross_h], 1)
    lows = jnp.concatenate([own_l, cross_l], 1)
    hidden_cot_pair = stack_pair(hidden_cot.T)
    back_pair = stack_pair(back_t)
    for cols in chunks(keys.shape[-1]):
        left = cot[0, :, cols] + given_left(cols) + fold_rows(nn(hidden_cot_pair, keys[:, cols]))
        right = (
            cot[1, :, cols]
            + given_right(cols)
            + fold_rows(nn(back_pair, err_high[:, cols]))
            + nn(back_pair[0:RANK], err_low[:, cols])
            + nn(own_twice, cot_right[:, cols])
            + nn(cross_twice, right_pair[:, cols])
            + nn(own_l, cot_right[0:RANK, cols])
            + nn(cross_l, right_pair[0:RANK, cols])
        )
        cot[0, :, cols] = left
        cot[1, :, cols] = right
        for value, pair in ((left, cot_left), (right, cot_right)):
            high, low = split(value)
            pair[0:RANK, cols] = high
            pair[RANK:, cols] = low


def first_kernel(
    pos, keys_own, keys_sib, values_own, values_sib, queries_own, queries_sib, cots_own, cots_sib,
    fkeys_own, fkeys_sib, fvalues_own, fvalues_sib, proj_mine, proj_got, fproj_mine, fproj_got, factors,
    sent, err_high_out, err_low_out, right_out, given_out, hidden_out, gram_out, recall_hidden_out, state_out,
    k, v, q, c, p, fk, fv, fp, err_high, err_low, state, left_pair, right_pairs, cot, cot_left, cot_right, given,
    sems, out_sems,
):
    second = pos[0]
    core = pos[1]
    half = proj_mine.shape[-1]
    mine_rows = pl.ds(pl.multiple_of(core * GROUP, GROUP), GROUP)
    sib_rows = pl.ds(pl.multiple_of((1 - core) * GROUP, GROUP), GROUP)
    mine_cols = pl.ds(pl.multiple_of(core * half, half), half)
    sib_cols = pl.ds(pl.multiple_of((1 - core) * half, half), half)

    def token_pair(own, sib, into, at):
        return [
            pltpu.make_async_copy(own, into.at[mine_rows, :], sems.at[at]),
            pltpu.make_async_copy(sib, into.at[sib_rows, :], sems.at[at + 1]),
        ]

    def proj_four(mine, got, into, at):
        first, last = pl.ds(0, GROUP), pl.ds(GROUP, GROUP)
        return [
            pltpu.make_async_copy(mine.at[first, :], into.at[mine_rows, mine_cols], sems.at[at]),
            pltpu.make_async_copy(mine.at[last, :], into.at[sib_rows, mine_cols], sems.at[at + 1]),
            pltpu.make_async_copy(got.at[first, :], into.at[sib_rows, sib_cols], sems.at[at + 2]),
            pltpu.make_async_copy(got.at[last, :], into.at[mine_rows, sib_cols], sems.at[at + 3]),
        ]

    load_state = [pltpu.make_async_copy(factors, state, sems.at[0])]
    load_f = (
        token_pair(fkeys_own, fkeys_sib, fk, 1)
        + proj_four(fproj_mine, fproj_got, fp, 3)
        + token_pair(fvalues_own, fvalues_sib, fv, 7)
    )
    load_own = (
        token_pair(keys_own, keys_sib, k, 9)
        + proj_four(proj_mine, proj_got, p, 11)
        + token_pair(values_own, values_sib, v, 15)
    )
    load_late = token_pair(queries_own, queries_sib, q, 17) + token_pair(cots_own, cots_sib, c, 19)

    for copy in load_state:
        copy.start()

    @pl.when(second == 1)
    def _():
        for copy in load_f:
            copy.start()

    for copy in load_own + load_late:
        copy.start()
    for copy in load_state:
        copy.wait()

    rows = [pl.ds(0, GROUP), pl.ds(GROUP, GROUP)]

    @pl.when(second == 1)
    def _():
        for copy in load_f:
            copy.wait()
        for block in rows:
            split_state(state, left_pair, right_pairs.at[0])
            forward_block(
                fk.at[block, :], fv.at[block, :], fp.at[block, :], state, left_pair, right_pairs.at[0],
                err_high.at[block, :], err_low.at[block, :], True,
            )

    for copy in load_own:
        copy.wait()
    outs = []
    hiddens = []
    grams = []
    recall = []
    for i, block in enumerate(rows):
        pair = right_pairs.at[i]
        split_state(state, left_pair, pair)

        @pl.when(core == i)
        def _():
            state_out[...] = state[1, :, :]

        if i == 0:
            for copy in load_late:
                copy.wait()
        read = fold_lanes(nt(q[block, :], left_pair[...]))
        recall.append(read)
        hidden = forward_block(
            k.at[block, :], v.at[block, :], p.at[block, :], state, left_pair, pair,
            err_high.at[block, :], err_low.at[block, :], i == 0,
        )
        hiddens.append(hidden)
        grams.append(gram(pair[...], pair[...]))
        hidden_out[i] = hidden
        gram_out[i] = grams[i]
        more = [
            pltpu.make_async_copy(err_high.at[block, :], err_high_out.at[block, :], out_sems.at[3 * i]),
            pltpu.make_async_copy(err_low.at[block, :], err_low_out.at[block, :], out_sems.at[3 * i + 1]),
            pltpu.make_async_copy(pair, right_out.at[i], out_sems.at[3 * i + 2]),
        ]
        for copy in more:
            copy.start()
        outs += more

    @pl.when(core == 0)
    def _():
        recall_hidden_out[...] = recall[0]

    @pl.when(core == 1)
    def _():
        recall_hidden_out[...] = recall[1]

    for i in (1, 0):
        block = rows[i]
        pair = right_pairs.at[i]
        spread = stack_pair(fold_lanes(nt(c[block, :], pair[...])).T)
        read = stack_pair(recall[i].T)
        for cols in chunks(k.shape[-1]):
            given[i, 0, :, cols] = fold_rows(nn(spread, q[block, cols]))
            given[i, 1, :, cols] = fold_rows(nn(read, c[block, cols]))
    copy = pltpu.make_async_copy(given.at[1], given_out, out_sems.at[6])
    copy.start()
    outs.append(copy)

    for cols in chunks(k.shape[-1]):
        for part, pair in ((0, cot_left), (1, cot_right)):
            value = given[1, part, :, cols]
            cot[part, :, cols] = value
            high, low = split(value)
            pair[0:RANK, cols] = high
            pair[RANK:, cols] = low
    block = rows[0]
    back_cot, hidden_cot = backward_hidden(
        k.at[block, :], right_pairs.at[0], err_high.at[block, :], err_low.at[block, :], hiddens[0], grams[0], cot_left, cot_right
    )
    backward_state(
        k.at[block, :], right_pairs.at[0], err_high.at[block, :], err_low.at[block, :], hiddens[0], back_cot, hidden_cot,
        cot, cot_left, cot_right, lambda cols: given[0, 0, :, cols], lambda cols: given[0, 1, :, cols],
    )
    sent[0:RANK, :] = cot_left[0:RANK, mine_cols]
    sent[RANK:, :] = cot_right[0:RANK, mine_cols]
    for copy in outs:
        copy.wait()


def first_call(pos, *arrays):
    width = arrays[0].shape[1]
    two = 2 * GROUP
    any_spec = pl.BlockSpec(memory_space=pl.ANY)
    vmem = pl.BlockSpec(memory_space=pltpu.VMEM)
    out_shape = (
        jax.ShapeDtypeStruct((2 * RANK, width // 2), bf16),
        jax.ShapeDtypeStruct((two, width), bf16),
        jax.ShapeDtypeStruct((two, width), bf16),
        jax.ShapeDtypeStruct((2, 2 * RANK, width), bf16),
        jax.ShapeDtypeStruct((2, RANK, width), f32),
        jax.ShapeDtypeStruct((2, GROUP, RANK), f32),
        jax.ShapeDtypeStruct((2, RANK, RANK), f32),
        jax.ShapeDtypeStruct((GROUP, RANK), f32),
        jax.ShapeDtypeStruct((RANK, width), f32),
    )
    tokens = pltpu.VMEM((two, width), bf16)
    wide = pltpu.VMEM((two, width), f32)
    pair = pltpu.VMEM((2 * RANK, width), bf16)
    return pl.pallas_call(
        first_kernel,
        out_shape=out_shape,
        in_specs=[pl.BlockSpec(memory_space=pltpu.SMEM)] + [any_spec] * len(arrays),
        out_specs=(vmem, any_spec, any_spec, any_spec, any_spec, vmem, vmem, vmem, vmem),
        scratch_shapes=[
            tokens, tokens, tokens, tokens, wide, tokens, tokens, wide, tokens, tokens,
            pltpu.VMEM((2, RANK, width), f32), pair, pltpu.VMEM((2, 2 * RANK, width), bf16),
            pltpu.VMEM((2, RANK, width), f32), pair, pair, pltpu.VMEM((2, 2, RANK, width), f32),
            pltpu.SemaphoreType.DMA((21,)), pltpu.SemaphoreType.DMA((7,)),
        ],
        compiler_params=pltpu.CompilerParams(vmem_limit_bytes=VMEM),
        cost_estimate=pl.CostEstimate(flops=20 * 10**9, bytes_accessed=30 * 2**20, transcendentals=0),
    )(pos, *arrays)


def second_kernel(
    pos, got_mine, got_sib, keys_own, keys_sib, err_high_in, err_low_in, right_in, given_in, hidden_in, gram_in,
    grad_out,
    k, err_high, err_low, right_pairs, given, received, cot, cot_left, cot_right, sems,
):
    core = pos[1]
    width = keys_own.shape[-1]
    half = width // 2
    mine_rows = pl.ds(pl.multiple_of(core * GROUP, GROUP), GROUP)
    sib_rows = pl.ds(pl.multiple_of((1 - core) * GROUP, GROUP), GROUP)
    mine_cols = pl.ds(pl.multiple_of(core * half, half), half)
    sib_cols = pl.ds(pl.multiple_of((1 - core) * half, half), half)
    rows = [pl.ds(0, GROUP), pl.ds(GROUP, GROUP)]
    load_cot = [
        pltpu.make_async_copy(got_mine, received.at[:, mine_cols], sems.at[0]),
        pltpu.make_async_copy(got_sib, received.at[:, sib_cols], sems.at[1]),
    ]
    load_keys = [
        pltpu.make_async_copy(keys_own, k.at[mine_rows, :], sems.at[2]),
        pltpu.make_async_copy(keys_sib, k.at[sib_rows, :], sems.at[3]),
    ]

    def load_block(i):
        return [
            pltpu.make_async_copy(right_in.at[i], right_pairs.at[i], sems.at[4 + 3 * i]),
            pltpu.make_async_copy(err_high_in.at[rows[i], :], err_high.at[rows[i], :], sems.at[5 + 3 * i]),
            pltpu.make_async_copy(err_low_in.at[rows[i], :], err_low.at[rows[i], :], sems.at[6 + 3 * i]),
        ]

    load_given = [pltpu.make_async_copy(given_in, given, sems.at[10])]
    loads = [load_cot + load_keys + load_block(1), load_given + load_block(0)]
    for copy in loads[0] + loads[1]:
        copy.start()
    for copy in loads[0]:
        copy.wait()
    for cols in chunks(width):
        for part, pair in ((0, cot_left), (1, cot_right)):
            value = received[part * RANK : (part + 1) * RANK, cols]
            cot[part, :, cols] = value.astype(f32)
            pair[0:RANK, cols] = value
            pair[RANK:, cols] = jnp.zeros((RANK, CHUNK), bf16)

    for i in (1, 0):
        block = rows[i]
        keys, eh, el, pair = k.at[block, :], err_high.at[block, :], err_low.at[block, :], right_pairs.at[i]
        hidden = hidden_in[i]
        back_cot, hidden_cot = backward_hidden(keys, pair, eh, el, hidden, gram_in[i], cot_left, cot_right)
        scaled = -RATE * hidden
        sh, sl = split(scaled)
        bh, bl = split(back_cot)
        s_twice = jnp.concatenate([sh, sh], 1)
        b_twice = jnp.concatenate([bh, bh], 1)
        out_rows = mine_rows if i == 0 else sib_rows
        for j in range(0, half, CHUNK):
            cols = pl.ds(pl.multiple_of(core * half + j, CHUNK), CHUNK)
            grad = (
                nn(s_twice, cot_right[:, cols])
                + nn(b_twice, pair[:, cols])
                + nn(sl, cot_right[0:RANK, cols])
                + nn(bl, pair[0:RANK, cols])
            ).astype(bf16)

            @pl.when(core == i)
            def _():
                grad_out[0:GROUP, j : j + CHUNK] = grad

            @pl.when(core != i)
            def _():
                grad_out[GROUP:, j : j + CHUNK] = grad

        if i == 1:
            for copy in loads[1]:
                copy.wait()
            backward_state(
                keys, pair, eh, el, hidden, back_cot, hidden_cot, cot, cot_left, cot_right,
                lambda cols: given[0, :, cols], lambda cols: given[1, :, cols],
            )


def second_call(pos, got_mine, got_sib, keys_own, keys_sib, *saved):
    width = keys_own.shape[1]
    two = 2 * GROUP
    any_spec = pl.BlockSpec(memory_space=pl.ANY)
    vmem = pl.BlockSpec(memory_space=pltpu.VMEM)
    tokens = pltpu.VMEM((two, width), bf16)
    pair = pltpu.VMEM((2 * RANK, width), bf16)
    return pl.pallas_call(
        second_kernel,
        out_shape=jax.ShapeDtypeStruct((two, width // 2), bf16),
        in_specs=[pl.BlockSpec(memory_space=pltpu.SMEM)] + [any_spec] * 8 + [vmem] * 2,
        out_specs=vmem,
        scratch_shapes=[
            tokens, tokens, tokens, pltpu.VMEM((2, 2 * RANK, width), bf16),
            pltpu.VMEM((2, RANK, width), f32), pair, pltpu.VMEM((2, RANK, width), f32), pair, pair,
            pltpu.SemaphoreType.DMA((11,)),
        ],
        compiler_params=pltpu.CompilerParams(vmem_limit_bytes=VMEM),
        cost_estimate=pl.CostEstimate(flops=10 * 10**9, bytes_accessed=14 * 2**20, transcendentals=0),
    )(pos, got_mine, got_sib, keys_own, keys_sib, *saved)


def block_of(pos, far, near):
    core, along_x, along_z = pos[1], pos[2], pos[3]
    by_x = lax.rem(along_x + 4 - jnp.where(core == 0, far, near), 4)
    by_z = lax.rem(along_z + 4 - jnp.where(core == 0, near, far), 4)
    return by_x * 4 + by_z


def project_kernel(fars, begun, pos, *refs):
    count = len(fars)
    pieces, (tokens_own, tokens_sib) = refs[:count], refs[count : count + 2]
    refs = refs[count + 2 :]
    if begun:
        total, refs = refs[0], refs[1:]
    out, weight, sems = refs
    copies = [
        pltpu.make_async_copy(piece, weight.at[i], sems.at[i]) for i, piece in enumerate(pieces)
    ]
    for copy in copies:
        copy.start()
    for i, copy in enumerate(copies):
        copy.wait()
        for part, tokens in enumerate((tokens_own, tokens_sib)):
            left = jnp.concatenate(
                [
                    tokens[:, pl.ds(pl.multiple_of(block_of(pos, fars[i], near) * 128, 128), 128)]
                    for near in range(4)
                ],
                1,
            )
            rows = slice(part * GROUP, (part + 1) * GROUP)
            for at in range(0, out.shape[1], CHUNK):
                cols = slice(at, at + CHUNK)
                term = nn(left, weight[i, :, cols])
                if i > 0:
                    out[rows, cols] += term
                elif begun:
                    out[rows, cols] = total[rows, cols] + term
                else:
                    out[rows, cols] = term


def project_call(pos, fars, pieces, tokens_own, tokens_sib, total=None):
    depth, half = pieces[0].shape
    count = len(fars)
    any_spec = pl.BlockSpec(memory_space=pl.ANY)
    vmem = pl.BlockSpec(memory_space=pltpu.VMEM)
    begun = total is not None
    return pl.pallas_call(
        functools.partial(project_kernel, fars, begun),
        out_shape=jax.ShapeDtypeStruct((2 * GROUP, half), f32),
        in_specs=[pl.BlockSpec(memory_space=pltpu.SMEM)] + [any_spec] * count + [vmem] * (3 if begun else 2),
        out_specs=vmem,
        scratch_shapes=[pltpu.VMEM((count, depth, half), bf16), pltpu.SemaphoreType.DMA((count,))],
        compiler_params=pltpu.CompilerParams(vmem_limit_bytes=VMEM),
        cost_estimate=pl.CostEstimate(
            flops=count * 2 * 512 * 512 * 1024, bytes_accessed=(4 + count) * 2**20, transcendentals=0
        ),
    )(pos, *pieces, tokens_own, tokens_sib, *((total,) if begun else ()))


EXTRA = 16
PART = 512 + EXTRA
TOP = 15.0


def gradient_kernel(firsts, pos, keys_own, keys_sib, queries_own, queries_sib, grad, cots_own, cots_sib, out):
    core, along_x, along_z = pos[1], pos[2], pos[3]
    half = grad.shape[1]
    cols = pl.ds(pl.multiple_of(core * half, half), half)
    tops = [jnp.max(jnp.abs(a.astype(f32))) for a in (grad[...], cots_own[:, cols], cots_sib[:, cols])]
    bound = 512.0 * (4.0 * tops[0] + 6.0 * jnp.maximum(tops[1], tops[2]))
    bound = jnp.full((8, 128), jnp.maximum(bound, 1e-26))
    power = jnp.clip(jnp.ceil(jnp.log2(bound)), -80.0, 127.0)
    scale = jnp.exp2(TOP - power)[0:1, 0:1]
    right = jnp.concatenate([grad[...], cots_own[:, cols], cots_sib[:, cols]], 0)

    def block(first, second):
        by_x = lax.rem(along_x + jnp.where(core == 0, first, second), 4)
        by_z = lax.rem(along_z + jnp.where(core == 0, second, first), 4)
        return pl.ds(pl.multiple_of((by_x * 4 + by_z) * 128, 128), 128)

    for i, first in enumerate(firsts):
        for second in range(0, 4, 2):
            left = jnp.concatenate(
                [
                    jnp.concatenate([a[:, block(first, second)], a[:, block(first, second + 1)]], 1)
                    for a in (keys_own, keys_sib, queries_own, queries_sib)
                ],
                0,
            )
            for at in range(0, half, CHUNK):
                term = lax.dot_general(
                    left, right[:, at : at + CHUNK], (((0,), (0,)), ((), ())), preferred_element_type=f32
                )
                out[i, 128 * second : 128 * second + 256, at : at + CHUNK] = term * scale
        out[i, 512:, :] = jnp.broadcast_to(power[0:1, 0:1], (EXTRA, half))


def gradient_call(pos, firsts, *arrays):
    half = arrays[4].shape[1]
    vmem = pl.BlockSpec(memory_space=pltpu.VMEM)
    return pl.pallas_call(
        functools.partial(gradient_kernel, firsts),
        out_shape=jax.ShapeDtypeStruct((len(firsts), PART, half), f32),
        in_specs=[pl.BlockSpec(memory_space=pltpu.SMEM)] + [vmem] * len(arrays),
        out_specs=vmem,
        compiler_params=pltpu.CompilerParams(vmem_limit_bytes=VMEM),
        cost_estimate=pl.CostEstimate(
            flops=len(firsts) * 2 * 512 * 1024 * 1024, bytes_accessed=(7 + 2 * len(firsts)) * 2**20, transcendentals=0
        ),
    )(pos, *arrays)


DP = ("x", "z", "yh")
SEQ = ("yl", "c")
ALL = ("x", "z", "yh", "yl", "c")
SIZES = (4, 4, 2, 2, 2)
f16 = jnp.float16


def swap_cores(value):
    return lax.ppermute(value, "c", [(0, 1), (1, 0)])


def ring_pairs(by, x_core):
    pairs = []
    for place in np.ndindex(*SIZES):
        there = list(place)
        axis = 0 if place[4] == x_core else 1
        there[axis] = (place[axis] + by) % 4
        pairs.append((int(np.ravel_multi_index(place, SIZES)), int(np.ravel_multi_index(there, SIZES))))
    return pairs


def after(value, *others):
    return lax.optimization_barrier((value, *others))[0]


def across(value):
    return lax.ppermute(value, ("yh", "yl"), [(0, 3), (3, 0), (1, 2), (2, 1)])


def gather_near(mine):
    other = across(mine)
    pair = jnp.where(
        lax.axis_index("yh") == 0,
        jnp.concatenate([mine, other], 0),
        jnp.concatenate([other, mine], 0),
    )
    near = [pair] + [lax.ppermute(pair, ALL, ring_pairs(by, 1)) for by in (1, 2, 3)]
    return jnp.concatenate(near, 0)


def add_up(own, messages):
    rows = own.shape[0] - EXTRA
    powers = [a[rows, 0].astype(f32) for a in (own, *messages)]
    power = powers[0]
    for other in powers[1:]:
        power = jnp.maximum(power, other)
    power = power + (2.0 if len(messages) == 3 else 1.0)
    total = own[:rows].astype(f32) * jnp.exp2(powers[0] - power)
    for message, other in zip(messages, powers[1:]):
        total = total + message[:rows].astype(f32) * jnp.exp2(other - power)
    return total, power


def packed(total, power):
    below = jnp.full((EXTRA, total.shape[1]), power)
    return jnp.concatenate([total, below], 0).astype(f16)


def scatter_sum(own, parts):
    got = [
        lax.ppermute(parts[by - 1].astype(f16), ALL, ring_pairs(by, 0)) for by in (1, 2, 3)
    ]
    total, power = add_up(own, got)
    blocks = [total[128 * i : 128 * (i + 1)] for i in range(4)]
    got = [
        lax.ppermute(packed(blocks[by], power), ALL, ring_pairs(by, 1)) for by in (1, 2, 3)
    ]
    below = jnp.full((EXTRA, total.shape[1]), power)
    total, power = add_up(jnp.concatenate([blocks[0], below], 0), got)
    low_half = lax.axis_index("yh") == 0
    keep = jnp.where(low_half, total[:64], total[64:])
    give = jnp.where(low_half, total[64:], total[:64])
    below = jnp.full((EXTRA, total.shape[1]), power)
    total, power = add_up(jnp.concatenate([keep, below], 0), [across(packed(give, power))])
    below = jnp.full((EXTRA, total.shape[1]), power)
    other = lax.ppermute(packed(total, power), "yl", [(0, 1), (1, 0)])
    total, power = add_up(jnp.concatenate([total, below], 0), [other])
    return total * jnp.exp2(power - TOP)


def per_device(key_tokens, value_tokens, query_tokens, cotangent, base_weight, factors):
    _, slice_len, width = key_tokens.shape
    half = width // 2
    core = lax.axis_index("c")
    place = jnp.stack([lax.axis_index(a) for a in ("yl", "c", "x", "z")]).astype(jnp.int32)

    def own_half(array):
        return lax.dynamic_slice_in_dim(array, core * half, half, 1)

    def join_halves(own, other):
        return jnp.where(
            core == 0, jnp.concatenate([own, other], 1), jnp.concatenate([other, own], 1)
        )

    keys, values, queries, cots = (a[0] for a in (key_tokens, value_tokens, query_tokens, cotangent))
    onward = [(0, 1)]
    fkeys = lax.ppermute(keys, "yl", onward)
    near = gather_near(own_half(base_weight))
    fvalues = lax.ppermute(after(values, fkeys), "yl", onward)
    factors_t = jnp.swapaxes(factors, 1, 2)
    keys_sib, queries_sib, cots_sib, values_sib = (swap_cores(a) for a in (keys, queries, cots, values))
    far = {by: lax.ppermute(near, ALL, ring_pairs(by, 0)) for by in (1, 3)}
    far[2] = lax.ppermute(after(near, far[1], far[3]), ALL, ring_pairs(2, 0))
    fkeys_sib, fvalues_sib = swap_cores(fkeys), swap_cores(fvalues)

    early = after(place, factors_t, keys_sib, queries_sib, cots_sib, values_sib)
    most, last = (0, 1, 3), (2,)
    most_pieces, last_pieces = (near, far[1], far[3]), (far[2],)
    fproj = project_call(early, most, most_pieces, fkeys, fkeys_sib)
    proj = project_call(early, most, most_pieces, keys, keys_sib)
    fproj = project_call(place, last, last_pieces, fkeys, fkeys_sib, fproj)
    fproj_got = swap_cores(fproj)
    proj = project_call(after(place, fproj), last, last_pieces, keys, keys_sib, proj)
    proj_got = swap_cores(proj)

    (sent, err_high, err_low, right, given, hidden, grams, recall_hidden, recall_right) = first_call(
        place, keys, keys_sib, values, values_sib, queries, queries_sib, cots, cots_sib,
        fkeys, fkeys_sib, fvalues, fvalues_sib, proj, proj_got, fproj, fproj_got, factors_t,
    )
    got = lax.ppermute(sent, "yl", [(1, 0)])

    later = after(place, sent)
    pieces = (near, far[1], far[2], far[3])
    qproj = project_call(later, (0, 1, 2, 3), pieces, queries, queries_sib)
    low = jnp.dot(recall_hidden, recall_right, precision=lax.Precision.HIGHEST)
    recalled = (join_halves(qproj[:slice_len], swap_cores(qproj[slice_len:])) + low).astype(bf16)[None]

    got = after(got, recalled)
    got_sib = swap_cores(got)
    grad = second_call(place, got, got_sib, keys, keys_sib, err_high, err_low, right, given, hidden, grams)
    gradient_of = (keys, keys_sib, queries, queries_sib, grad, cots, cots_sib)
    parts = gradient_call(place, (1, 2, 3), *gradient_of)
    own = gradient_call(after(place, parts), (0,), *gradient_of)
    share = scatter_sum(own[0], parts)
    base_grad = join_halves(share, swap_cores(share))
    return (recalled, base_grad)


def solution(mesh):
    fine = Mesh(mesh.devices.reshape(SIZES), ALL)
    tokens = P(DP, SEQ, None)
    in_specs = (tokens, tokens, tokens, tokens, P(DP, None), P())
    out_specs = (tokens, P(DP, None))
    return jax.shard_map(
        per_device, mesh=fine, in_specs=in_specs, out_specs=out_specs, check_vma=False
    )
```

```python
import functools

import jax
import jax.numpy as jnp
import numpy as np
from jax import lax
from jax.experimental import pallas as pl
from jax.experimental.pallas import tpu as pltpu
from jax.sharding import Mesh, PartitionSpec as P

GROUP = 256
RANK = 128
CHUNK = 512
VMEM = 60 * 2**20
RATE = 0.01 / GROUP
f32 = jnp.float32
bf16 = jnp.bfloat16
f16 = jnp.float16


def nt(a, b):
    return lax.dot_general(a, b, (((1,), (1,)), ((), ())), preferred_element_type=f32)


def nn(a, b):
    return lax.dot_general(a, b, (((1,), (0,)), ((), ())), preferred_element_type=f32)


def split(x):
    high = x.astype(bf16)
    return high, (x - high.astype(f32)).astype(bf16)


def fold_lanes(x):
    return x[:, :RANK] + x[:, RANK:]


def fold_rows(x):
    return x[:RANK] + x[RANK:]


def small(x, y):
    xh, xl = split(x)
    yh, yl = split(y)
    return nn(xh, yh) + nn(xl, yh) + nn(xh, yl)


def stack_pair(x):
    return jnp.concatenate(split(x), 0)


def gram(pair_a, pair_b):
    return fold_lanes(fold_rows(nt(pair_a, pair_b)))


def chunks(width):
    return [pl.ds(j, CHUNK) for j in range(0, width, CHUNK)]


def put_pair(pair, cols, value):
    high, low = split(value)
    pair[0:RANK, cols] = high
    pair[RANK:, cols] = low


class Square:
    def __init__(self, value):
        high, self.low = split(value)
        self.twice = jnp.concatenate([high, high], 1)

    def times(self, pair, cols):
        return nn(self.twice, pair[:, cols]) + nn(self.low, pair[0:RANK, cols])


def advance(keys, diff_high, diff_low, hidden, back, state, left_pair, right_old, right_new):
    back_pair = stack_pair((-RATE * back).T)
    hidden_t = (-RATE * hidden).T
    hidden_pair = stack_pair(hidden_t)
    own = Square(small(hidden_t, hidden))
    for cols in chunks(keys.shape[-1]):
        left = state[0, :, cols] + fold_rows(nn(back_pair, keys[:, cols]))
        right = (
            state[1, :, cols]
            + fold_rows(nn(hidden_pair, diff_high[:, cols]))
            + nn(hidden_pair[0:RANK], diff_low[:, cols])
            + own.times(right_old, cols)
        )
        state[0, :, cols] = left
        state[1, :, cols] = right
        put_pair(left_pair, cols, left)
        put_pair(right_new, cols, right)


def backward_hidden(keys, diff_high, diff_low, right_pair, hidden, gram_right, cot_left, cot_right):
    back_cot = -RATE * fold_lanes(nt(keys[...], cot_left[...]))
    diff_cot = fold_lanes(nt(diff_high[...], cot_right[...])) + nt(diff_low[...], cot_right[0:RANK, :])
    mixed = gram(cot_right[...], right_pair[...])
    hidden_cot = -RATE * (diff_cot + small(hidden, mixed + mixed.T)) + small(back_cot, gram_right)
    return back_cot, hidden_cot


def backward_state(keys, diff_high, diff_low, right_pair, hidden, back_cot, hidden_cot, cot, cot_left, cot_right, given):
    hidden_t = hidden.T
    back_t = back_cot.T
    own = Square(-RATE * small(hidden_t, hidden))
    cross = small(hidden_t, back_cot)
    cross = Square(cross + cross.T)
    hidden_cot_pair = stack_pair(hidden_cot.T)
    back_pair = stack_pair(back_t)
    for cols in chunks(keys.shape[-1]):
        left = cot[0, :, cols] + given[0, :, cols] + fold_rows(nn(hidden_cot_pair, keys[:, cols]))
        right = (
            cot[1, :, cols]
            + given[1, :, cols]
            + fold_rows(nn(back_pair, diff_high[:, cols]))
            + nn(back_pair[0:RANK], diff_low[:, cols])
            + own.times(cot_right, cols)
            + cross.times(right_pair, cols)
        )
        cot[0, :, cols] = left
        cot[1, :, cols] = right
        put_pair(cot_left, cols, left)
        put_pair(cot_right, cols, right)


def first_kernel(
    pos, keys_own, keys_sib, queries_own, queries_sib, cots_own, cots_sib, fkeys_own, fkeys_sib,
    high_mine, high_got, low_mine, low_got, fhigh_mine, fhigh_got, flow_mine, flow_got, factors,
    sent, right_out, given_out, hidden_out, gram_out, recall_hidden_out, recall_right_out,
    kq, uc, low, fk, fhigh, flow, state, left_pair, right_pairs, cot, cot_left, cot_right, given, kept,
    sems, out_sems,
):
    second = pos[0]
    core = pos[1]
    other = 1 - core
    width = keys_own.shape[-1]
    half = width // 2
    mine_cols = pl.ds(pl.multiple_of(core * half, half), half)
    sib_cols = pl.ds(pl.multiple_of(other * half, half), half)
    top, bottom = pl.ds(0, GROUP), pl.ds(GROUP, GROUP)
    used = [0]

    def copy_of(source, into):
        used[0] += 1
        return pltpu.make_async_copy(source, into, sems.at[used[0] - 1])

    def pair_of(own, sib, into, rows):
        return [copy_of(own, into.at[core, rows, :]), copy_of(sib, into.at[other, rows, :])]

    def halves(mine, got, into, rows):
        return [
            copy_of(mine.at[top, :], into.at[core, rows, mine_cols]),
            copy_of(mine.at[bottom, :], into.at[other, rows, mine_cols]),
            copy_of(got.at[top, :], into.at[other, rows, sib_cols]),
            copy_of(got.at[bottom, :], into.at[core, rows, sib_cols]),
        ]

    load_state = [copy_of(factors, state)]
    load_f = (
        pair_of(fkeys_own, fkeys_sib, fk, top)
        + halves(fhigh_mine, fhigh_got, fhigh, top)
        + halves(flow_mine, flow_got, flow, top)
    )
    load_own = (
        pair_of(keys_own, keys_sib, kq, top)
        + pair_of(queries_own, queries_sib, kq, bottom)
        + halves(high_mine, high_got, uc, top)
        + pair_of(cots_own, cots_sib, uc, bottom)
        + halves(low_mine, low_got, low, top)
    )
    for copy in load_state:
        copy.start()

    @pl.when(second == 1)
    def _():
        for copy in load_f:
            copy.start()

    for copy in load_own:
        copy.start()
    for copy in load_state:
        copy.wait()
    for cols in chunks(width):
        put_pair(left_pair, cols, state[0, :, cols])
        put_pair(right_pairs.at[0], cols, state[1, :, cols])

    @pl.when(second == 1)
    def _():
        for copy in load_f:
            copy.wait()
        pair = right_pairs.at[0]
        for i in range(2):
            hidden = fold_lanes(nt(fk[i], left_pair[...]))
            back = fold_lanes(nt(fhigh[i], pair[...])) + nt(flow[i], pair[0:RANK, :])
            back += small(hidden, gram(pair[...], pair[...]))
            advance(fk.at[i], fhigh.at[i], flow.at[i], hidden, back, state, left_pair, pair, pair)

    for copy in load_own:
        copy.wait()
    outs = []
    hiddens, grams, reads, spreads = [], [], [], []
    for i in range(2):
        pair = right_pairs.at[i]
        copy = pltpu.make_async_copy(pair, right_out.at[i], out_sems.at[i])
        copy.start()
        outs.append(copy)

        @pl.when(core == i)
        def _():
            kept[...] = state[1, :, :]

        both = fold_lanes(nt(kq[i], left_pair[...]))
        hidden, read = both[:GROUP], both[GROUP:]
        both = fold_lanes(nt(uc[i], pair[...]))
        square = gram(pair[...], pair[...])
        hidden_out[i] = hidden
        gram_out[i] = square
        hiddens.append(hidden)
        grams.append(square)
        reads.append(read)
        spreads.append(both[GROUP:])
        if i == 0:
            back = both[:GROUP] + nt(low[i], pair[0:RANK, :]) + small(hidden, square)
            advance(
                kq.at[i, top, :], uc.at[i, top, :], low.at[i], hidden, back, state, left_pair, pair, right_pairs.at[1]
            )

    @pl.when(core == 0)
    def _():
        recall_hidden_out[...] = reads[0]

    @pl.when(core == 1)
    def _():
        recall_hidden_out[...] = reads[1]

    outs.append(pltpu.make_async_copy(kept, recall_right_out, out_sems.at[3]))
    outs[-1].start()

    for i in (1, 0):
        spread, read = stack_pair(spreads[i].T), stack_pair(reads[i].T)
        for cols in chunks(width):
            left = fold_rows(nn(spread, kq[i, bottom, cols]))
            right = fold_rows(nn(read, uc[i, bottom, cols]))
            given[i, 0, :, cols] = left
            given[i, 1, :, cols] = right
            if i == 1:
                cot[0, :, cols] = left
                cot[1, :, cols] = right
                put_pair(cot_left, cols, left)
                put_pair(cot_right, cols, right)
    outs.append(pltpu.make_async_copy(given.at[1], given_out, out_sems.at[2]))
    outs[-1].start()
    keys, diff_high = kq.at[0, top, :], uc.at[0, top, :]
    back_cot, hidden_cot = backward_hidden(
        keys, diff_high, low.at[0], right_pairs.at[0], hiddens[0], grams[0], cot_left, cot_right
    )
    backward_state(
        keys, diff_high, low.at[0], right_pairs.at[0], hiddens[0], back_cot, hidden_cot,
        cot, cot_left, cot_right, given.at[0],
    )
    sent[0:RANK, :] = cot_left[0:RANK, mine_cols]
    sent[RANK:, :] = cot_right[0:RANK, mine_cols]
    for copy in outs:
        copy.wait()


def first_call(pos, *arrays):
    width = arrays[0].shape[1]
    two = 2 * GROUP
    any_spec = pl.BlockSpec(memory_space=pl.ANY)
    vmem = pl.BlockSpec(memory_space=pltpu.VMEM)
    out_shape = (
        jax.ShapeDtypeStruct((2 * RANK, width // 2), bf16),
        jax.ShapeDtypeStruct((2, 2 * RANK, width), bf16),
        jax.ShapeDtypeStruct((2, RANK, width), f32),
        jax.ShapeDtypeStruct((2, GROUP, RANK), f32),
        jax.ShapeDtypeStruct((2, RANK, RANK), f32),
        jax.ShapeDtypeStruct((GROUP, RANK), f32),
        jax.ShapeDtypeStruct((RANK, width), f32),
    )
    one = pltpu.VMEM((2, GROUP, width), bf16)
    both = pltpu.VMEM((2, two, width), bf16)
    pair = pltpu.VMEM((2 * RANK, width), bf16)
    state = pltpu.VMEM((2, RANK, width), f32)
    return pl.pallas_call(
        first_kernel,
        out_shape=out_shape,
        in_specs=[pl.BlockSpec(memory_space=pltpu.SMEM)] + [any_spec] * len(arrays),
        out_specs=(vmem, any_spec, any_spec, vmem, vmem, vmem, any_spec),
        scratch_shapes=[
            both, both, one, one, one, one,
            state, pair, pltpu.VMEM((2, 2 * RANK, width), bf16),
            state, pair, pair, pltpu.VMEM((2, 2, RANK, width), f32), pltpu.VMEM((RANK, width), f32),
            pltpu.SemaphoreType.DMA((25,)), pltpu.SemaphoreType.DMA((4,)),
        ],
        compiler_params=pltpu.CompilerParams(vmem_limit_bytes=VMEM),
        cost_estimate=pl.CostEstimate(flops=16 * 10**9, bytes_accessed=26 * 2**20, transcendentals=0),
    )(pos, *arrays)


def second_kernel(
    pos, got_mine, got_sib, keys_own, keys_sib, high_mine, high_got, low_mine, low_got, right_in, given_in, cots_own, cots_sib,
    hidden_in, gram_in,
    grad_out, power_out,
    k, high, low, right_pairs, given, received, cot, cot_left, cot_right, grad, sems, out_sems,
):
    core = pos[1]
    other = 1 - core
    width = keys_own.shape[-1]
    half = width // 2
    mine_cols = pl.ds(pl.multiple_of(core * half, half), half)
    sib_cols = pl.ds(pl.multiple_of(other * half, half), half)
    top, bottom = pl.ds(0, GROUP), pl.ds(GROUP, GROUP)
    used = [0]

    def copy_of(source, into):
        used[0] += 1
        return pltpu.make_async_copy(source, into, sems.at[used[0] - 1])

    def halves(mine, got, into):
        return [
            copy_of(mine.at[top, :], into.at[core, :, mine_cols]),
            copy_of(mine.at[bottom, :], into.at[other, :, mine_cols]),
            copy_of(got.at[top, :], into.at[other, :, sib_cols]),
            copy_of(got.at[bottom, :], into.at[core, :, sib_cols]),
        ]

    load_first = [
        copy_of(got_mine, received.at[:, mine_cols]),
        copy_of(got_sib, received.at[:, sib_cols]),
        copy_of(keys_own, k.at[core]),
        copy_of(keys_sib, k.at[other]),
        copy_of(right_in, right_pairs),
    ]
    load_diff = halves(high_mine, high_got, high) + halves(low_mine, low_got, low)
    load_later = [
        copy_of(given_in, given),
        copy_of(cots_own.at[:, mine_cols], grad.at[pl.ds(2 * GROUP, GROUP), :]),
        copy_of(cots_sib.at[:, mine_cols], grad.at[pl.ds(3 * GROUP, GROUP), :]),
    ]
    for copy in load_first + load_diff + load_later:
        copy.start()
    for copy in load_first:
        copy.wait()
    for cols in chunks(width):
        for part, pair in ((0, cot_left), (1, cot_right)):
            value = received[part * RANK : (part + 1) * RANK, cols]
            cot[part, :, cols] = value.astype(f32)
            pair[0:RANK, cols] = value
            pair[RANK:, cols] = jnp.zeros((RANK, CHUNK), bf16)
    for copy in load_diff:
        copy.wait()

    peak = jnp.zeros((1, 1), f32)
    for i in (1, 0):
        pair = right_pairs.at[i]
        hidden = hidden_in[i]
        back_cot, hidden_cot = backward_hidden(
            k.at[i], high.at[i], low.at[i], pair, hidden, gram_in[i], cot_left, cot_right
        )
        sh, sl = split(-RATE * hidden)
        bh, bl = split(back_cot)
        s_twice = jnp.concatenate([sh, sh], 1)
        b_twice = jnp.concatenate([bh, bh], 1)
        rows = pl.ds(pl.multiple_of(jnp.where(core == i, 0, GROUP), GROUP), GROUP)
        for j in range(0, half, CHUNK):
            cols = pl.ds(pl.multiple_of(core * half + j, CHUNK), CHUNK)
            value = (
                nn(s_twice, cot_right[:, cols])
                + nn(b_twice, pair[:, cols])
                + nn(sl, cot_right[0:RANK, cols])
                + nn(bl, pair[0:RANK, cols])
            )
            peak = jnp.maximum(peak, jnp.max(jnp.abs(value), axis=(0, 1), keepdims=True))
            grad[rows, j : j + CHUNK] = value.astype(bf16)
        if i == 1:
            for copy in load_later:
                copy.wait()
            backward_state(
                k.at[i], high.at[i], low.at[i], pair, hidden, back_cot, hidden_cot, cot, cot_left, cot_right, given
            )
    out = pltpu.make_async_copy(grad, grad_out, out_sems.at[0])
    out.start()
    cots = jnp.max(jnp.abs(grad[2 * GROUP :, :].astype(f32)), axis=(0, 1), keepdims=True)
    bound = jnp.maximum(512.0 * (4.04 * peak + 6.0 * cots), 1e-26)
    power = jnp.clip(jnp.ceil(jnp.log2(jnp.broadcast_to(bound, (8, 128)))), -80.0, 127.0)
    power_out[...] = power
    out.wait()


def second_call(pos, *arrays):
    width = arrays[2].shape[1]
    half = width // 2
    any_spec = pl.BlockSpec(memory_space=pl.ANY)
    vmem = pl.BlockSpec(memory_space=pltpu.VMEM)
    one = pltpu.VMEM((2, GROUP, width), bf16)
    pair = pltpu.VMEM((2 * RANK, width), bf16)
    state = pltpu.VMEM((2, RANK, width), f32)
    return pl.pallas_call(
        second_kernel,
        out_shape=(jax.ShapeDtypeStruct((4 * GROUP, half), bf16), jax.ShapeDtypeStruct((8, 128), f32)),
        in_specs=[pl.BlockSpec(memory_space=pltpu.SMEM)] + [any_spec] * (len(arrays) - 2) + [vmem] * 2,
        out_specs=(any_spec, vmem),
        scratch_shapes=[
            one, one, one, pltpu.VMEM((2, 2 * RANK, width), bf16), state, pair, state, pair, pair,
            pltpu.VMEM((4 * GROUP, half), bf16),
            pltpu.SemaphoreType.DMA((16,)), pltpu.SemaphoreType.DMA((1,)),
        ],
        compiler_params=pltpu.CompilerParams(vmem_limit_bytes=VMEM),
        cost_estimate=pl.CostEstimate(flops=8 * 10**9, bytes_accessed=14 * 2**20, transcendentals=0),
    )(pos, *arrays)


ORDER = (0, 1, 3, 2)


def permute_kernel(count, pos, *refs):
    core, along_x, along_z = pos[1], pos[2], pos[3]
    out = refs[count]
    for at, first in enumerate(ORDER):
        for second in range(4):
            by_x = lax.rem(along_x + jnp.where(core == 0, first, second), 4)
            by_z = lax.rem(along_z + jnp.where(core == 0, second, first), 4)
            source = pl.ds(pl.multiple_of((by_x * 4 + by_z) * 128, 128), 128)
            for i in range(count):
                out[i * GROUP : (i + 1) * GROUP, 128 * (4 * at + second) : 128 * (4 * at + second + 1)] = refs[i][:, source]


def permute_call(pos, *arrays):
    count = len(arrays)
    vmem = pl.BlockSpec(memory_space=pltpu.VMEM)
    return pl.pallas_call(
        functools.partial(permute_kernel, count),
        out_shape=jax.ShapeDtypeStruct((count * GROUP, arrays[0].shape[1]), bf16),
        in_specs=[pl.BlockSpec(memory_space=pltpu.SMEM)] + [vmem] * count,
        out_specs=vmem,
        compiler_params=pltpu.CompilerParams(vmem_limit_bytes=VMEM),
        cost_estimate=pl.CostEstimate(flops=0, bytes_accessed=2 * count * 2**20, transcendentals=0),
    )(pos, *arrays)


DP = ("x", "z", "yh")
SEQ = ("yl", "c")
ALL = ("x", "z", "yh", "yl", "c")
SIZES = (4, 4, 2, 2, 2)
TOP = 15.0


def swap_cores(value):
    return lax.ppermute(value, "c", [(0, 1), (1, 0)])


def ring_pairs(by, x_core):
    pairs = []
    for place in np.ndindex(*SIZES):
        there = list(place)
        axis = 0 if place[4] == x_core else 1
        there[axis] = (place[axis] + by) % 4
        pairs.append((int(np.ravel_multi_index(place, SIZES)), int(np.ravel_multi_index(there, SIZES))))
    return pairs


def first_axis(value, by):
    return lax.ppermute(value, ALL, ring_pairs(by, 0))


def second_axis(value, by):
    return lax.ppermute(value, ALL, ring_pairs(by, 1))


def across(value):
    return lax.ppermute(value, ("yh", "yl"), [(0, 3), (3, 0), (1, 2), (2, 1)])


def along(value):
    return lax.ppermute(value, "yl", [(0, 1), (1, 0)])


def after(value, *others):
    return lax.optimization_barrier((value, *others))[0]


def dot(left, right):
    return jnp.dot(left, right, preferred_element_type=f32)


def scatter_sum(left, right, power):
    def product(at):
        return lax.dot_general(
            left[:, 512 * at : 512 * (at + 1)], right, (((0,), (0,)), ((), ())), preferred_element_type=f32
        )

    scale = jnp.exp2(TOP - power[0, 0])
    parts = {by: (product(ORDER.index(by)) * scale).astype(f16) for by in (2, 1, 3)}
    powers = [power] + [first_axis(power, by) for by in (1, 2, 3)]
    got = {by: first_axis(parts[by], by) for by in (2, 1, 3)}
    own = product(0)

    common = jnp.maximum(jnp.maximum(powers[0], powers[1]), jnp.maximum(powers[2], powers[3]))
    others = [second_axis(common, by) for by in (1, 2, 3)]
    common = jnp.maximum(jnp.maximum(common, others[0]), jnp.maximum(others[1], others[2]))
    common = jnp.maximum(common, across(common))
    common = jnp.maximum(common, along(common))

    level = common[0, 0] + 2.0
    total = own * jnp.exp2(TOP - level)
    for by in (1, 2, 3):
        total = total + got[by].astype(f32) * jnp.exp2(powers[by][0, 0] - level)
    send = {by: (total[128 * by : 128 * (by + 1)] * 0.25).astype(f16) for by in (2, 1, 3)}
    got = {by: second_axis(send[by], by) for by in (2, 1, 3)}
    total = total[:128] * 0.25 + got[1].astype(f32) + got[2].astype(f32) + got[3].astype(f32)
    low_half = lax.axis_index("yh") == 0
    keep = jnp.where(low_half, total[:64], total[64:])
    give = jnp.where(low_half, total[64:], total[:64])
    total = keep * 0.5 + across((give * 0.5).astype(f16)).astype(f32)
    total = total * 0.5 + along((total * 0.5).astype(f16)).astype(f32)
    return total * jnp.exp2(level + 4.0 - TOP)


def per_device(key_tokens, value_tokens, query_tokens, cotangent, base_weight, factors):
    _, slice_len, width = key_tokens.shape
    half = width // 2
    core = lax.axis_index("c")
    place = jnp.stack([lax.axis_index(a) for a in ("yl", "c", "x", "z")]).astype(jnp.int32)

    def own_half(array):
        return lax.dynamic_slice_in_dim(array, core * half, half, 1)

    def other_half(array):
        return lax.dynamic_slice_in_dim(array, (1 - core) * half, half, 1)

    def join_halves(own, other):
        return jnp.where(
            core == 0, jnp.concatenate([own, other], 1), jnp.concatenate([other, own], 1)
        )

    keys, values, queries, cots = (a[0] for a in (key_tokens, value_tokens, query_tokens, cotangent))
    onward = [(0, 1)]
    mine = own_half(base_weight)
    facing = across(mine)
    fkeys = lax.ppermute(keys, "yl", onward)
    values_half = jnp.concatenate([own_half(values), swap_cores(other_half(values))], 0)
    fvalues_half = lax.ppermute(values_half, "yl", onward)
    near = jnp.where(
        lax.axis_index("yh") == 0,
        jnp.concatenate([mine, facing], 0),
        jnp.concatenate([facing, mine], 0),
    )
    near = jnp.concatenate([near] + [second_axis(near, by) for by in (3, 2, 1)], 0)
    factors_t = jnp.swapaxes(factors, 1, 2)
    keys_sib, queries_sib, cots_sib = (swap_cores(a) for a in (keys, queries, cots))
    keys_p = permute_call(place, keys, keys_sib)
    queries_p = permute_call(place, queries, queries_sib)
    near = after(near, factors_t, keys_p)
    far1, far3 = first_axis(near, 3), first_axis(near, 1)
    far2 = first_axis(after(near, far1, far3), 2)
    fkeys_sib = swap_cores(fkeys)
    fkeys_p = permute_call(place, fkeys, fkeys_sib)

    most = jnp.concatenate([near, far1, far3], 0)
    depth = most.shape[0]
    begun = dot(keys_p[:, :depth], most)
    fbegun = dot(fkeys_p[:, :depth], most)

    def diff(begun, tokens, subtract):
        whole = begun + dot(tokens[:, depth:], far2) - subtract.astype(f32)
        high = lax.reduce_precision(whole, 8, 7)
        return high.astype(bf16), (whole - high).astype(bf16)

    fhigh, flow = diff(fbegun, fkeys_p, fvalues_half)
    high, low = diff(begun, keys_p, values_half)
    high_got, low_got, fhigh_got, flow_got = (swap_cores(a) for a in (high, low, fhigh, flow))

    sent, right, given, hidden, grams, recall_hidden, recall_right = first_call(
        place, keys, keys_sib, queries, queries_sib, cots, cots_sib, fkeys, fkeys_sib,
        high, high_got, low, low_got, fhigh, fhigh_got, flow, flow_got, factors_t,
    )
    got = lax.ppermute(sent, "yl", [(1, 0)])
    got_sib = swap_cores(got)
    grad, power = second_call(
        place, got, got_sib, keys, keys_sib, high, high_got, low, low_got, right, given, cots, cots_sib, hidden, grams
    )
    share = scatter_sum(jnp.concatenate([keys_p, queries_p], 0), grad, power)
    base_grad = join_halves(share, swap_cores(share))

    qproj = dot(queries_p[:, :depth], most) + dot(queries_p[:, depth:], far2)
    small_low = jnp.dot(recall_hidden, recall_right, precision=lax.Precision.HIGHEST)
    recalled = join_halves(qproj[:slice_len], swap_cores(qproj[slice_len:])) + small_low
    return (recalled.astype(bf16)[None], base_grad)


def solution(mesh):
    fine = Mesh(mesh.devices.reshape(SIZES), ALL)
    tokens = P(DP, SEQ, None)
    in_specs = (tokens, tokens, tokens, tokens, P(DP, None), P())
    out_specs = (tokens, P(DP, None))
    return jax.shard_map(
        per_device, mesh=fine, in_specs=in_specs, out_specs=out_specs, check_vma=False
    )
```

```python
import functools

import jax
import jax.numpy as jnp
import numpy as np
from jax import lax
from jax.experimental import pallas as pl
from jax.experimental.pallas import tpu as pltpu
from jax.sharding import Mesh, PartitionSpec as P

GROUP = 256
RANK = 128
CHUNK = 512
VMEM = 60 * 2**20
RATE = 0.01 / GROUP
TOP = 15.0
f32 = jnp.float32
bf16 = jnp.bfloat16
f16 = jnp.float16


def nt(a, b):
    return lax.dot_general(a, b, (((1,), (1,)), ((), ())), preferred_element_type=f32)


def nn(a, b):
    return lax.dot_general(a, b, (((1,), (0,)), ((), ())), preferred_element_type=f32)


def split(x):
    high = x.astype(bf16)
    return high, (x - high.astype(f32)).astype(bf16)


def fold_lanes(x):
    return x[:, :RANK] + x[:, RANK:]


def fold_rows(x):
    return x[:RANK] + x[RANK:]


def small(x, y):
    xh, xl = split(x)
    yh, yl = split(y)
    return nn(xh, yh) + nn(xl, yh) + nn(xh, yl)


def stack_pair(x):
    return jnp.concatenate(split(x), 0)


def gram(pair_a, pair_b):
    return fold_lanes(fold_rows(nt(pair_a, pair_b)))


def chunks(width):
    return [pl.ds(j, CHUNK) for j in range(0, width, CHUNK)]


def put_pair(pair, cols, value):
    high, low = split(value)
    pair[0:RANK, cols] = high
    pair[RANK:, cols] = low


class Square:
    def __init__(self, value):
        high, self.low = split(value)
        self.twice = jnp.concatenate([high, high], 1)

    def times(self, pair, cols):
        return nn(self.twice, pair[:, cols]) + nn(self.low, pair[0:RANK, cols])


def advance(keys, diff_high, diff_low, hidden, back, state, left_pair, right_old, right_new):
    back_pair = stack_pair((-RATE * back).T)
    hidden_t = (-RATE * hidden).T
    hidden_pair = stack_pair(hidden_t)
    own = Square(small(hidden_t, hidden))
    for cols in chunks(keys.shape[-1]):
        left = state[0, :, cols] + fold_rows(nn(back_pair, keys[:, cols]))
        right = (
            state[1, :, cols]
            + fold_rows(nn(hidden_pair, diff_high[:, cols]))
            + nn(hidden_pair[0:RANK], diff_low[:, cols])
            + own.times(right_old, cols)
        )
        state[0, :, cols] = left
        state[1, :, cols] = right
        put_pair(left_pair, cols, left)
        put_pair(right_new, cols, right)


def backward_hidden(keys, diff_high, diff_low, right_pair, hidden, gram_right, cot_left, cot_right):
    back_cot = -RATE * fold_lanes(nt(keys[...], cot_left[...]))
    diff_cot = fold_lanes(nt(diff_high[...], cot_right[...])) + nt(diff_low[...], cot_right[0:RANK, :])
    mixed = gram(cot_right[...], right_pair[...])
    hidden_cot = -RATE * (diff_cot + small(hidden, mixed + mixed.T)) + small(back_cot, gram_right)
    return back_cot, hidden_cot


def backward_state(keys, diff_high, diff_low, right_pair, hidden, back_cot, hidden_cot, cot, cot_left, cot_right, given):
    hidden_t = hidden.T
    back_t = back_cot.T
    own = Square(-RATE * small(hidden_t, hidden))
    cross = small(hidden_t, back_cot)
    cross = Square(cross + cross.T)
    hidden_cot_pair = stack_pair(hidden_cot.T)
    back_pair = stack_pair(back_t)
    for cols in chunks(keys.shape[-1]):
        left = cot[0, :, cols] + given[0, :, cols] + fold_rows(nn(hidden_cot_pair, keys[:, cols]))
        right = (
            cot[1, :, cols]
            + given[1, :, cols]
            + fold_rows(nn(back_pair, diff_high[:, cols]))
            + nn(back_pair[0:RANK], diff_low[:, cols])
            + own.times(cot_right, cols)
            + cross.times(right_pair, cols)
        )
        cot[0, :, cols] = left
        cot[1, :, cols] = right
        put_pair(cot_left, cols, left)
        put_pair(cot_right, cols, right)


def first_kernel(
    pos, keys_own, keys_sib, queries_own, queries_sib, cots_own, cots_sib, fkeys_own, fkeys_sib,
    high_mine, high_got, low_mine, low_got, fhigh_mine, fhigh_got, flow_mine, flow_got, factors,
    sent, right_out, given_out, hidden_out, gram_out, recall_hidden_out, recall_right_out,
    kq, uc, low, fk, fhigh, flow, state, left_pair, right_pairs, cot, cot_left, cot_right, given, kept,
    sems, out_sems,
):
    second = pos[0]
    core = pos[1]
    other = 1 - core
    width = keys_own.shape[-1]
    half = width // 2
    mine_cols = pl.ds(pl.multiple_of(core * half, half), half)
    sib_cols = pl.ds(pl.multiple_of(other * half, half), half)
    top, bottom = pl.ds(0, GROUP), pl.ds(GROUP, GROUP)
    def own_and_sib(own, sib, into, rows, at):
        return [
            pltpu.make_async_copy(own, into.at[core, rows, :], sems.at[at + core]),
            pltpu.make_async_copy(sib, into.at[other, rows, :], sems.at[at + other]),
        ]

    def halves(mine, got, into, rows, at):
        return [
            pltpu.make_async_copy(mine.at[top, :], into.at[core, rows, mine_cols], sems.at[at + core]),
            pltpu.make_async_copy(mine.at[bottom, :], into.at[other, rows, mine_cols], sems.at[at + other]),
            pltpu.make_async_copy(got.at[top, :], into.at[other, rows, sib_cols], sems.at[at + 2 + other]),
            pltpu.make_async_copy(got.at[bottom, :], into.at[core, rows, sib_cols], sems.at[at + 2 + core]),
        ]

    def wait_block(i, tokens, split_ones):
        for own, into, rows, at in tokens:
            pltpu.make_async_copy(own, into.at[i, rows, :], sems.at[at + i]).wait()
        for mine, into, rows, at in split_ones:
            for step, cols in ((0, mine_cols), (2, sib_cols)):
                pltpu.make_async_copy(mine.at[top, :], into.at[i, rows, cols], sems.at[at + step + i]).wait()

    load_state = pltpu.make_async_copy(factors, state, sems.at[0])
    load_f = (
        own_and_sib(fkeys_own, fkeys_sib, fk, top, 1)
        + halves(fhigh_mine, fhigh_got, fhigh, top, 3)
        + halves(flow_mine, flow_got, flow, top, 7)
    )
    load_own = (
        own_and_sib(keys_own, keys_sib, kq, top, 11)
        + own_and_sib(queries_own, queries_sib, kq, bottom, 13)
        + halves(high_mine, high_got, uc, top, 15)
        + own_and_sib(cots_own, cots_sib, uc, bottom, 19)
        + halves(low_mine, low_got, low, top, 21)
    )
    load_state.start()

    @pl.when(second == 1)
    def _():
        for copy in load_f:
            copy.start()

    for copy in load_own:
        copy.start()
    load_state.wait()
    for cols in chunks(width):
        put_pair(left_pair, cols, state[0, :, cols])
        put_pair(right_pairs.at[0], cols, state[1, :, cols])

    @pl.when(second == 1)
    def _():
        pair = right_pairs.at[0]
        for i in range(2):
            wait_block(i, [(fkeys_own, fk, top, 1)], [(fhigh_mine, fhigh, top, 3), (flow_mine, flow, top, 7)])
            hidden = fold_lanes(nt(fk[i], left_pair[...]))
            back = fold_lanes(nt(fhigh[i], pair[...])) + nt(flow[i], pair[0:RANK, :])
            back += small(hidden, gram(pair[...], pair[...]))
            advance(fk.at[i], fhigh.at[i], flow.at[i], hidden, back, state, left_pair, pair, pair)

    outs = []
    hiddens, grams, reads, spreads = [], [], [], []
    for i in range(2):
        wait_block(
            i,
            [(keys_own, kq, top, 11), (queries_own, kq, bottom, 13), (cots_own, uc, bottom, 19)],
            [(high_mine, uc, top, 15), (low_mine, low, top, 21)],
        )
        pair = right_pairs.at[i]
        copy = pltpu.make_async_copy(pair, right_out.at[i], out_sems.at[i])
        copy.start()
        outs.append(copy)

        @pl.when(core == i)
        def _():
            kept[...] = state[1, :, :]

        both = fold_lanes(nt(kq[i], left_pair[...]))
        hidden, read = both[:GROUP], both[GROUP:]
        both = fold_lanes(nt(uc[i], pair[...]))
        square = gram(pair[...], pair[...])
        hidden_out[i] = hidden
        gram_out[i] = square
        hiddens.append(hidden)
        grams.append(square)
        reads.append(read)
        spreads.append(both[GROUP:])
        if i == 0:
            back = both[:GROUP] + nt(low[i], pair[0:RANK, :]) + small(hidden, square)
            advance(
                kq.at[i, top, :], uc.at[i, top, :], low.at[i], hidden, back, state, left_pair, pair, right_pairs.at[1]
            )

    @pl.when(core == 0)
    def _():
        recall_hidden_out[...] = reads[0]

    @pl.when(core == 1)
    def _():
        recall_hidden_out[...] = reads[1]

    outs.append(pltpu.make_async_copy(kept, recall_right_out, out_sems.at[3]))
    outs[-1].start()

    for i in (1, 0):
        spread, read = stack_pair(spreads[i].T), stack_pair(reads[i].T)
        for cols in chunks(width):
            left = fold_rows(nn(spread, kq[i, bottom, cols]))
            right = fold_rows(nn(read, uc[i, bottom, cols]))
            given[i, 0, :, cols] = left
            given[i, 1, :, cols] = right
            if i == 1:
                cot[0, :, cols] = left
                cot[1, :, cols] = right
                put_pair(cot_left, cols, left)
                put_pair(cot_right, cols, right)
    outs.append(pltpu.make_async_copy(given.at[1], given_out, out_sems.at[2]))
    outs[-1].start()
    keys, diff_high = kq.at[0, top, :], uc.at[0, top, :]
    back_cot, hidden_cot = backward_hidden(
        keys, diff_high, low.at[0], right_pairs.at[0], hiddens[0], grams[0], cot_left, cot_right
    )
    backward_state(
        keys, diff_high, low.at[0], right_pairs.at[0], hiddens[0], back_cot, hidden_cot,
        cot, cot_left, cot_right, given.at[0],
    )
    sent[0:RANK, :] = cot_left[0:RANK, mine_cols]
    sent[RANK:, :] = cot_right[0:RANK, mine_cols]
    for copy in outs:
        copy.wait()


def first_call(pos, *arrays):
    width = arrays[0].shape[1]
    two = 2 * GROUP
    any_spec = pl.BlockSpec(memory_space=pl.ANY)
    vmem = pl.BlockSpec(memory_space=pltpu.VMEM)
    out_shape = (
        jax.ShapeDtypeStruct((2 * RANK, width // 2), bf16),
        jax.ShapeDtypeStruct((2, 2 * RANK, width), bf16),
        jax.ShapeDtypeStruct((2, RANK, width), f32),
        jax.ShapeDtypeStruct((2, GROUP, RANK), f32),
        jax.ShapeDtypeStruct((2, RANK, RANK), f32),
        jax.ShapeDtypeStruct((GROUP, RANK), f32),
        jax.ShapeDtypeStruct((RANK, width), f32),
    )
    one = pltpu.VMEM((2, GROUP, width), bf16)
    both = pltpu.VMEM((2, two, width), bf16)
    pair = pltpu.VMEM((2 * RANK, width), bf16)
    state = pltpu.VMEM((2, RANK, width), f32)
    return pl.pallas_call(
        first_kernel,
        out_shape=out_shape,
        in_specs=[pl.BlockSpec(memory_space=pltpu.SMEM)] + [any_spec] * len(arrays),
        out_specs=(vmem, any_spec, any_spec, vmem, vmem, vmem, any_spec),
        scratch_shapes=[
            both, both, one, one, one, one,
            state, pair, pltpu.VMEM((2, 2 * RANK, width), bf16),
            state, pair, pair, pltpu.VMEM((2, 2, RANK, width), f32), pltpu.VMEM((RANK, width), f32),
            pltpu.SemaphoreType.DMA((25,)), pltpu.SemaphoreType.DMA((4,)),
        ],
        compiler_params=pltpu.CompilerParams(vmem_limit_bytes=VMEM),
        cost_estimate=pl.CostEstimate(flops=16 * 10**9, bytes_accessed=26 * 2**20, transcendentals=0),
    )(pos, *arrays)


def second_kernel(
    pos, got_mine, got_sib, keys_own, keys_sib, high_mine, high_got, low_mine, low_got, right_in, given_in, cots_own, cots_sib,
    hidden_in, gram_in,
    grad_out, power_out,
    k, high, low, right_pairs, given, received, cot, cot_left, cot_right, grad, sems, out_sems,
):
    core = pos[1]
    other = 1 - core
    width = keys_own.shape[-1]
    half = width // 2
    mine_cols = pl.ds(pl.multiple_of(core * half, half), half)
    sib_cols = pl.ds(pl.multiple_of(other * half, half), half)
    top, bottom = pl.ds(0, GROUP), pl.ds(GROUP, GROUP)
    def halves(mine, got, into, at):
        return [
            pltpu.make_async_copy(mine.at[top, :], into.at[core, :, mine_cols], sems.at[at + core]),
            pltpu.make_async_copy(mine.at[bottom, :], into.at[other, :, mine_cols], sems.at[at + other]),
            pltpu.make_async_copy(got.at[top, :], into.at[other, :, sib_cols], sems.at[at + 2 + other]),
            pltpu.make_async_copy(got.at[bottom, :], into.at[core, :, sib_cols], sems.at[at + 2 + core]),
        ]

    def wait_block(i):
        pltpu.make_async_copy(keys_own, k.at[i], sems.at[2 + i]).wait()
        pltpu.make_async_copy(right_in.at[i], right_pairs.at[i], sems.at[4 + i]).wait()
        for mine, into, at in ((high_mine, high, 6), (low_mine, low, 10)):
            for step, cols in ((0, mine_cols), (2, sib_cols)):
                pltpu.make_async_copy(mine.at[top, :], into.at[i, :, cols], sems.at[at + step + i]).wait()

    load_got = [
        pltpu.make_async_copy(got_mine, received.at[:, mine_cols], sems.at[0]),
        pltpu.make_async_copy(got_sib, received.at[:, sib_cols], sems.at[1]),
    ]
    load_blocks = (
        [
            pltpu.make_async_copy(keys_own, k.at[core], sems.at[2 + core]),
            pltpu.make_async_copy(keys_sib, k.at[other], sems.at[2 + other]),
            pltpu.make_async_copy(right_in.at[1], right_pairs.at[1], sems.at[5]),
        ]
        + halves(high_mine, high_got, high, 6)
        + halves(low_mine, low_got, low, 10)
        + [pltpu.make_async_copy(right_in.at[0], right_pairs.at[0], sems.at[4])]
    )
    load_later = [
        pltpu.make_async_copy(given_in, given, sems.at[14]),
        pltpu.make_async_copy(cots_own.at[:, mine_cols], grad.at[pl.ds(2 * GROUP, GROUP), :], sems.at[15]),
        pltpu.make_async_copy(cots_sib.at[:, mine_cols], grad.at[pl.ds(3 * GROUP, GROUP), :], sems.at[16]),
    ]
    for copy in load_got + load_blocks + load_later:
        copy.start()
    for copy in load_got:
        copy.wait()
    for cols in chunks(width):
        for part, pair in ((0, cot_left), (1, cot_right)):
            value = received[part * RANK : (part + 1) * RANK, cols]
            cot[part, :, cols] = value.astype(f32)
            pair[0:RANK, cols] = value
            pair[RANK:, cols] = jnp.zeros((RANK, CHUNK), bf16)
    peak = jnp.zeros((1, 1), f32)
    for i in (1, 0):
        wait_block(i)
        pair = right_pairs.at[i]
        hidden = hidden_in[i]
        back_cot, hidden_cot = backward_hidden(
            k.at[i], high.at[i], low.at[i], pair, hidden, gram_in[i], cot_left, cot_right
        )
        sh, sl = split(-RATE * hidden)
        bh, bl = split(back_cot)
        s_twice = jnp.concatenate([sh, sh], 1)
        b_twice = jnp.concatenate([bh, bh], 1)
        rows = pl.ds(pl.multiple_of(jnp.where(core == i, 0, GROUP), GROUP), GROUP)
        for j in range(0, half, CHUNK):
            cols = pl.ds(pl.multiple_of(core * half + j, CHUNK), CHUNK)
            value = (
                nn(s_twice, cot_right[:, cols])
                + nn(b_twice, pair[:, cols])
                + nn(sl, cot_right[0:RANK, cols])
                + nn(bl, pair[0:RANK, cols])
            )
            peak = jnp.maximum(peak, jnp.max(jnp.abs(value), axis=(0, 1), keepdims=True))
            grad[rows, j : j + CHUNK] = value.astype(bf16)
        if i == 1:
            for copy in load_later:
                copy.wait()
            backward_state(
                k.at[i], high.at[i], low.at[i], pair, hidden, back_cot, hidden_cot, cot, cot_left, cot_right, given
            )
    cots = jnp.max(jnp.abs(grad[2 * GROUP :, :].astype(f32)), axis=(0, 1), keepdims=True)
    bound = jnp.maximum(512.0 * (4.04 * peak + 6.0 * cots), 1e-26)
    power = jnp.clip(jnp.ceil(jnp.log2(jnp.broadcast_to(bound, (8, 128)))), -80.0, 127.0)
    power_out[...] = power
    scale = jnp.exp2(TOP - power[0:1, 0:1])
    for part in range(4):
        rows = pl.ds(part * GROUP, GROUP)
        grad[rows, :] = (grad[rows, :].astype(f32) * scale).astype(bf16)
        out = pltpu.make_async_copy(grad.at[rows, :], grad_out.at[rows, :], out_sems.at[part])
        out.start()
    for part in range(4):
        rows = pl.ds(part * GROUP, GROUP)
        pltpu.make_async_copy(grad.at[rows, :], grad_out.at[rows, :], out_sems.at[part]).wait()


def second_call(pos, *arrays):
    width = arrays[2].shape[1]
    half = width // 2
    any_spec = pl.BlockSpec(memory_space=pl.ANY)
    vmem = pl.BlockSpec(memory_space=pltpu.VMEM)
    one = pltpu.VMEM((2, GROUP, width), bf16)
    pair = pltpu.VMEM((2 * RANK, width), bf16)
    state = pltpu.VMEM((2, RANK, width), f32)
    return pl.pallas_call(
        second_kernel,
        out_shape=(jax.ShapeDtypeStruct((4 * GROUP, half), bf16), jax.ShapeDtypeStruct((8, 128), f32)),
        in_specs=[pl.BlockSpec(memory_space=pltpu.SMEM)] + [any_spec] * (len(arrays) - 2) + [vmem] * 2,
        out_specs=(any_spec, vmem),
        scratch_shapes=[
            one, one, one, pltpu.VMEM((2, 2 * RANK, width), bf16), state, pair, state, pair, pair,
            pltpu.VMEM((4 * GROUP, half), bf16),
            pltpu.SemaphoreType.DMA((17,)), pltpu.SemaphoreType.DMA((4,)),
        ],
        compiler_params=pltpu.CompilerParams(vmem_limit_bytes=VMEM),
        cost_estimate=pl.CostEstimate(flops=8 * 10**9, bytes_accessed=14 * 2**20, transcendentals=0),
    )(pos, *arrays)


ORDER = (0, 1, 3, 2)


def permute_kernel(count, pos, *refs):
    core, along_x, along_z = pos[1], pos[2], pos[3]
    out = refs[count]
    for at, first in enumerate(ORDER):
        for second in range(4):
            by_x = lax.rem(along_x + jnp.where(core == 0, first, second), 4)
            by_z = lax.rem(along_z + jnp.where(core == 0, second, first), 4)
            source = pl.ds(pl.multiple_of((by_x * 4 + by_z) * 128, 128), 128)
            for i in range(count):
                out[i * GROUP : (i + 1) * GROUP, 128 * (4 * at + second) : 128 * (4 * at + second + 1)] = refs[i][:, source]


def permute_call(pos, *arrays):
    count = len(arrays)
    vmem = pl.BlockSpec(memory_space=pltpu.VMEM)
    return pl.pallas_call(
        functools.partial(permute_kernel, count),
        out_shape=jax.ShapeDtypeStruct((count * GROUP, arrays[0].shape[1]), bf16),
        in_specs=[pl.BlockSpec(memory_space=pltpu.SMEM)] + [vmem] * count,
        out_specs=vmem,
        compiler_params=pltpu.CompilerParams(vmem_limit_bytes=VMEM),
        cost_estimate=pl.CostEstimate(flops=0, bytes_accessed=2 * count * 2**20, transcendentals=0),
    )(pos, *arrays)


def assemble_kernel(pos, near, far1, far3, far2, out, sems):
    core, along_x, along_z = pos[1], pos[2], pos[3]
    copies = []
    for first, piece in ((0, near), (1, far1), (3, far3), (2, far2)):
        for second in range(4):
            by_x = lax.rem(along_x + jnp.where(core == 0, first, second), 4)
            by_z = lax.rem(along_z + jnp.where(core == 0, second, first), 4)
            rows = pl.ds(pl.multiple_of((by_x * 4 + by_z) * 128, 128), 128)
            copies.append(
                pltpu.make_async_copy(
                    piece.at[pl.ds(128 * second, 128), :], out.at[rows, :], sems.at[4 * first + second]
                )
            )
    for copy in copies:
        copy.start()
    for copy in copies:
        copy.wait()


def assemble_call(pos, *pieces):
    any_spec = pl.BlockSpec(memory_space=pl.ANY)
    rows, half = pieces[0].shape
    return pl.pallas_call(
        assemble_kernel,
        out_shape=jax.ShapeDtypeStruct((4 * rows, half), bf16),
        in_specs=[pl.BlockSpec(memory_space=pltpu.SMEM)] + [any_spec] * 4,
        out_specs=any_spec,
        scratch_shapes=[pltpu.SemaphoreType.DMA((16,))],
        compiler_params=pltpu.CompilerParams(vmem_limit_bytes=VMEM),
        cost_estimate=pl.CostEstimate(flops=0, bytes_accessed=8 * 2**20, transcendentals=0),
    )(pos, *pieces)


DP = ("x", "z", "yh")
SEQ = ("yl", "c")
ALL = ("x", "z", "yh", "yl", "c")
SIZES = (4, 4, 2, 2, 2)


def swap_cores(value):
    return lax.ppermute(value, "c", [(0, 1), (1, 0)])


def ring_pairs(by, x_core):
    pairs = []
    for place in np.ndindex(*SIZES):
        there = list(place)
        axis = 0 if place[4] == x_core else 1
        there[axis] = (place[axis] + by) % 4
        pairs.append((int(np.ravel_multi_index(place, SIZES)), int(np.ravel_multi_index(there, SIZES))))
    return pairs


def first_axis(value, by):
    return lax.ppermute(value, ALL, ring_pairs(by, 0))


def second_axis(value, by):
    return lax.ppermute(value, ALL, ring_pairs(by, 1))


def across(value):
    return lax.ppermute(value, ("yh", "yl"), [(0, 3), (3, 0), (1, 2), (2, 1)])


def along(value):
    return lax.ppermute(value, "yl", [(0, 1), (1, 0)])


def after(value, *others):
    return lax.optimization_barrier((value, *others))[0]


def dot(left, right):
    return jnp.dot(left, right, preferred_element_type=f32)


def scatter_sum(left, right, power, beside):
    def product(at):
        return lax.dot_general(
            left[:, 512 * at : 512 * (at + 1)], right, (((0,), (0,)), ((), ())), preferred_element_type=f32
        )

    parts = {by: product(ORDER.index(by)).astype(f16) for by in (2, 1, 3)}
    got = {by: first_axis(parts[by], by) for by in (2, 1, 3)}
    own = product(0)
    power = after(power, own)
    powers = [power] + [first_axis(power, by) for by in (1, 2, 3)]

    common = jnp.maximum(jnp.maximum(powers[0], powers[1]), jnp.maximum(powers[2], powers[3]))
    others = [second_axis(common, by) for by in (1, 2, 3)]
    common = jnp.maximum(jnp.maximum(common, others[0]), jnp.maximum(others[1], others[2]))
    common = jnp.maximum(common, across(common))
    common = jnp.maximum(common, along(common))

    level = common[0, 0] + 2.0
    total = own * jnp.exp2(powers[0][0, 0] - level)
    for by in (1, 2, 3):
        total = total + got[by].astype(f32) * jnp.exp2(powers[by][0, 0] - level)
    total = after(total, beside)
    send = {by: (total[128 * by : 128 * (by + 1)] * 0.25).astype(f16) for by in (2, 1, 3)}
    got = {by: second_axis(send[by], by) for by in (2, 1, 3)}
    total = total[:128] * 0.25 + got[1].astype(f32) + got[2].astype(f32) + got[3].astype(f32)
    low_half = lax.axis_index("yh") == 0
    keep = jnp.where(low_half, total[:64], total[64:])
    give = jnp.where(low_half, total[64:], total[:64])
    total = keep * 0.5 + across((give * 0.5).astype(f16)).astype(f32)
    total = total * 0.5 + along((total * 0.5).astype(f16)).astype(f32)
    return total * jnp.exp2(level + 4.0 - TOP)


def per_device(key_tokens, value_tokens, query_tokens, cotangent, base_weight, factors):
    _, slice_len, width = key_tokens.shape
    half = width // 2
    core = lax.axis_index("c")
    place = jnp.stack([lax.axis_index(a) for a in ("yl", "c", "x", "z")]).astype(jnp.int32)

    def own_half(array):
        return lax.dynamic_slice_in_dim(array, core * half, half, 1)

    def other_half(array):
        return lax.dynamic_slice_in_dim(array, (1 - core) * half, half, 1)

    def join_halves(own, other):
        return jnp.where(
            core == 0, jnp.concatenate([own, other], 1), jnp.concatenate([other, own], 1)
        )

    keys, values, queries, cots = (a[0] for a in (key_tokens, value_tokens, query_tokens, cotangent))
    mine = own_half(base_weight)
    facing = across(mine)
    fboth = lax.ppermute(jnp.concatenate([keys, values], 0), "yl", [(0, 1)])
    near = jnp.where(
        lax.axis_index("yh") == 0,
        jnp.concatenate([mine, facing], 0),
        jnp.concatenate([facing, mine], 0),
    )
    near = jnp.concatenate([near] + [second_axis(near, by) for by in (3, 2, 1)], 0)
    factors_t = jnp.swapaxes(factors, 1, 2)
    near = after(near, factors_t)
    far1, far2, far3 = (first_axis(near, by) for by in (3, 2, 1))
    keys_sib, queries_sib, cots_sib = (swap_cores(a) for a in (keys, queries, cots))
    values_half = jnp.concatenate([own_half(values), swap_cores(other_half(values))], 0)
    weight = assemble_call(place, near, far1, far3, far2)

    def diff(tokens, tokens_sib, subtract):
        whole = dot(jnp.concatenate([tokens, tokens_sib], 0), weight) - subtract.astype(f32)
        high = lax.reduce_precision(whole, 8, 7)
        return high.astype(bf16), (whole - high).astype(bf16)

    high, low = diff(keys, keys_sib, values_half)
    high_got, low_got = swap_cores(high), swap_cores(low)
    fkeys, fvalues = fboth[:slice_len], fboth[slice_len:]
    fkeys_sib = swap_cores(fkeys)
    fvalues_half = jnp.concatenate([own_half(fvalues), swap_cores(other_half(fvalues))], 0)
    fhigh, flow = diff(fkeys, fkeys_sib, fvalues_half)
    fhigh_got, flow_got = swap_cores(fhigh), swap_cores(flow)

    sent, right, given, hidden, grams, recall_hidden, recall_right = first_call(
        place, keys, keys_sib, queries, queries_sib, cots, cots_sib, fkeys, fkeys_sib,
        high, high_got, low, low_got, fhigh, fhigh_got, flow, flow_got, factors_t,
    )
    got = lax.ppermute(sent, "yl", [(1, 0)])
    got_sib = swap_cores(got)
    grad, power = second_call(
        place, got, got_sib, keys, keys_sib, high, high_got, low, low_got, right, given, cots, cots_sib, hidden, grams
    )

    later = after(weight, sent)
    qproj = dot(jnp.concatenate([queries, queries_sib], 0), later)
    small_low = jnp.dot(recall_hidden, recall_right, precision=lax.Precision.HIGHEST)
    recalled = join_halves(qproj[:slice_len], swap_cores(qproj[slice_len:])) + small_low
    recalled = recalled.astype(bf16)[None]

    left = jnp.concatenate([permute_call(place, keys, keys_sib), permute_call(place, queries, queries_sib)], 0)
    share = scatter_sum(left, grad, power, recalled)
    base_grad = join_halves(share, swap_cores(share))
    return (recalled, base_grad)


def solution(mesh):
    fine = Mesh(mesh.devices.reshape(SIZES), ALL)
    tokens = P(DP, SEQ, None)
    in_specs = (tokens, tokens, tokens, tokens, P(DP, None), P())
    out_specs = (tokens, P(DP, None))
    return jax.shard_map(
        per_device, mesh=fine, in_specs=in_specs, out_specs=out_specs, check_vma=False
    )
```

```python
import functools

import jax
import jax.numpy as jnp
import numpy as np
from jax import lax
from jax.experimental import pallas as pl
from jax.experimental.pallas import tpu as pltpu
from jax.sharding import Mesh, PartitionSpec as P

GROUP = 256
RANK = 128
CHUNK = 512
VMEM = 60 * 2**20
RATE = 0.01 / GROUP
TOP = 15.0
f32 = jnp.float32
bf16 = jnp.bfloat16
f16 = jnp.float16


def nt(a, b):
    return lax.dot_general(a, b, (((1,), (1,)), ((), ())), preferred_element_type=f32)


def nn(a, b):
    return lax.dot_general(a, b, (((1,), (0,)), ((), ())), preferred_element_type=f32)


def split(x):
    high = x.astype(bf16)
    return high, (x - high.astype(f32)).astype(bf16)


def fold_lanes(x):
    return x[:, :RANK] + x[:, RANK:]


def fold_rows(x):
    return x[:RANK] + x[RANK:]


def small(x, y):
    xh, xl = split(x)
    yh, yl = split(y)
    return nn(xh, yh) + nn(xl, yh) + nn(xh, yl)


def stack_pair(x):
    return jnp.concatenate(split(x), 0)


def gram(pair_a, pair_b):
    return fold_lanes(fold_rows(nt(pair_a, pair_b)))


def chunks(width):
    return [pl.ds(j, CHUNK) for j in range(0, width, CHUNK)]


def put_pair(pair, cols, value):
    high, low = split(value)
    pair[0:RANK, cols] = high
    pair[RANK:, cols] = low


class Square:
    def __init__(self, value):
        high, self.low = split(value)
        self.twice = jnp.concatenate([high, high], 1)

    def times(self, pair, cols):
        return nn(self.twice, pair[:, cols]) + nn(self.low, pair[0:RANK, cols])


def advance(keys, diff_high, diff_low, hidden, back, state, left_pair, right_old, right_new):
    back_pair = stack_pair((-RATE * back).T)
    hidden_t = (-RATE * hidden).T
    hidden_pair = stack_pair(hidden_t)
    own = Square(small(hidden_t, hidden))
    for cols in chunks(keys.shape[-1]):
        left = state[0, :, cols] + fold_rows(nn(back_pair, keys[:, cols]))
        right = (
            state[1, :, cols]
            + fold_rows(nn(hidden_pair, diff_high[:, cols]))
            + nn(hidden_pair[0:RANK], diff_low[:, cols])
            + own.times(right_old, cols)
        )
        state[0, :, cols] = left
        state[1, :, cols] = right
        put_pair(left_pair, cols, left)
        put_pair(right_new, cols, right)


def backward_hidden(keys, diff_high, diff_low, right_pair, hidden, gram_right, cot_left, cot_right):
    back_cot = -RATE * fold_lanes(nt(keys[...], cot_left[...]))
    diff_cot = fold_lanes(nt(diff_high[...], cot_right[...])) + nt(diff_low[...], cot_right[0:RANK, :])
    mixed = gram(cot_right[...], right_pair[...])
    hidden_cot = -RATE * (diff_cot + small(hidden, mixed + mixed.T)) + small(back_cot, gram_right)
    return back_cot, hidden_cot


def backward_state(keys, diff_high, diff_low, right_pair, hidden, back_cot, hidden_cot, cot, cot_left, cot_right, given):
    hidden_t = hidden.T
    back_t = back_cot.T
    own = Square(-RATE * small(hidden_t, hidden))
    cross = small(hidden_t, back_cot)
    cross = Square(cross + cross.T)
    hidden_cot_pair = stack_pair(hidden_cot.T)
    back_pair = stack_pair(back_t)
    for cols in chunks(keys.shape[-1]):
        left = cot[0, :, cols] + given[0, :, cols] + fold_rows(nn(hidden_cot_pair, keys[:, cols]))
        right = (
            cot[1, :, cols]
            + given[1, :, cols]
            + fold_rows(nn(back_pair, diff_high[:, cols]))
            + nn(back_pair[0:RANK], diff_low[:, cols])
            + own.times(cot_right, cols)
            + cross.times(right_pair, cols)
        )
        cot[0, :, cols] = left
        cot[1, :, cols] = right
        put_pair(cot_left, cols, left)
        put_pair(cot_right, cols, right)


def first_kernel(
    pos, keys_own, keys_sib, queries_own, queries_sib, cots_own, cots_sib, fkeys_own, fkeys_sib,
    high_mine, high_got, low_mine, low_got, fhigh_mine, fhigh_got, flow_mine, flow_got, factors,
    sent, right_out, given_out, hidden_out, gram_out, recall_hidden_out, recall_right_out,
    kq, uc, low, fk, fhigh, flow, state, left_pair, right_pairs, cot, cot_left, cot_right, given, kept,
    sems, out_sems,
):
    second = pos[0]
    core = pos[1]
    other = 1 - core
    width = keys_own.shape[-1]
    half = width // 2
    mine_cols = pl.ds(pl.multiple_of(core * half, half), half)
    sib_cols = pl.ds(pl.multiple_of(other * half, half), half)
    top, bottom = pl.ds(0, GROUP), pl.ds(GROUP, GROUP)
    def own_and_sib(own, sib, into, rows, at):
        return [
            pltpu.make_async_copy(own, into.at[core, rows, :], sems.at[at + core]),
            pltpu.make_async_copy(sib, into.at[other, rows, :], sems.at[at + other]),
        ]

    def halves(mine, got, into, rows, at):
        return [
            pltpu.make_async_copy(mine.at[top, :], into.at[core, rows, mine_cols], sems.at[at + core]),
            pltpu.make_async_copy(mine.at[bottom, :], into.at[other, rows, mine_cols], sems.at[at + other]),
            pltpu.make_async_copy(got.at[top, :], into.at[other, rows, sib_cols], sems.at[at + 2 + other]),
            pltpu.make_async_copy(got.at[bottom, :], into.at[core, rows, sib_cols], sems.at[at + 2 + core]),
        ]

    def wait_block(i, tokens, split_ones):
        for own, into, rows, at in tokens:
            pltpu.make_async_copy(own, into.at[i, rows, :], sems.at[at + i]).wait()
        for mine, into, rows, at in split_ones:
            for step, cols in ((0, mine_cols), (2, sib_cols)):
                pltpu.make_async_copy(mine.at[top, :], into.at[i, rows, cols], sems.at[at + step + i]).wait()

    load_state = pltpu.make_async_copy(factors, state, sems.at[0])
    load_f = (
        own_and_sib(fkeys_own, fkeys_sib, fk, top, 1)
        + halves(fhigh_mine, fhigh_got, fhigh, top, 3)
        + halves(flow_mine, flow_got, flow, top, 7)
    )
    load_own = (
        own_and_sib(keys_own, keys_sib, kq, top, 11)
        + own_and_sib(queries_own, queries_sib, kq, bottom, 13)
        + halves(high_mine, high_got, uc, top, 15)
        + own_and_sib(cots_own, cots_sib, uc, bottom, 19)
        + halves(low_mine, low_got, low, top, 21)
    )
    load_state.start()

    @pl.when(second == 1)
    def _():
        for copy in load_f:
            copy.start()

    for copy in load_own:
        copy.start()
    load_state.wait()
    for cols in chunks(width):
        put_pair(left_pair, cols, state[0, :, cols])
        put_pair(right_pairs.at[0], cols, state[1, :, cols])

    @pl.when(second == 1)
    def _():
        pair = right_pairs.at[0]
        for i in range(2):
            wait_block(i, [(fkeys_own, fk, top, 1)], [(fhigh_mine, fhigh, top, 3), (flow_mine, flow, top, 7)])
            hidden = fold_lanes(nt(fk[i], left_pair[...]))
            back = fold_lanes(nt(fhigh[i], pair[...])) + nt(flow[i], pair[0:RANK, :])
            back += small(hidden, gram(pair[...], pair[...]))
            advance(fk.at[i], fhigh.at[i], flow.at[i], hidden, back, state, left_pair, pair, pair)

    outs = []
    hiddens, grams, reads, spreads = [], [], [], []
    for i in range(2):
        wait_block(
            i,
            [(keys_own, kq, top, 11), (queries_own, kq, bottom, 13), (cots_own, uc, bottom, 19)],
            [(high_mine, uc, top, 15), (low_mine, low, top, 21)],
        )
        pair = right_pairs.at[i]
        copy = pltpu.make_async_copy(pair, right_out.at[i], out_sems.at[i])
        copy.start()
        outs.append(copy)

        @pl.when(core == i)
        def _():
            kept[...] = state[1, :, :]

        both = fold_lanes(nt(kq[i], left_pair[...]))
        hidden, read = both[:GROUP], both[GROUP:]
        both = fold_lanes(nt(uc[i], pair[...]))
        square = gram(pair[...], pair[...])
        hidden_out[i] = hidden
        gram_out[i] = square
        hiddens.append(hidden)
        grams.append(square)
        reads.append(read)
        spreads.append(both[GROUP:])
        if i == 0:
            back = both[:GROUP] + nt(low[i], pair[0:RANK, :]) + small(hidden, square)
            advance(
                kq.at[i, top, :], uc.at[i, top, :], low.at[i], hidden, back, state, left_pair, pair, right_pairs.at[1]
            )

    @pl.when(core == 0)
    def _():
        recall_hidden_out[...] = reads[0]

    @pl.when(core == 1)
    def _():
        recall_hidden_out[...] = reads[1]

    outs.append(pltpu.make_async_copy(kept, recall_right_out, out_sems.at[3]))
    outs[-1].start()

    for i in (1, 0):
        spread, read = stack_pair(spreads[i].T), stack_pair(reads[i].T)
        for cols in chunks(width):
            left = fold_rows(nn(spread, kq[i, bottom, cols]))
            right = fold_rows(nn(read, uc[i, bottom, cols]))
            given[i, 0, :, cols] = left
            given[i, 1, :, cols] = right
            if i == 1:
                cot[0, :, cols] = left
                cot[1, :, cols] = right
                put_pair(cot_left, cols, left)
                put_pair(cot_right, cols, right)
    outs.append(pltpu.make_async_copy(given.at[1], given_out, out_sems.at[2]))
    outs[-1].start()
    keys, diff_high = kq.at[0, top, :], uc.at[0, top, :]
    back_cot, hidden_cot = backward_hidden(
        keys, diff_high, low.at[0], right_pairs.at[0], hiddens[0], grams[0], cot_left, cot_right
    )
    backward_state(
        keys, diff_high, low.at[0], right_pairs.at[0], hiddens[0], back_cot, hidden_cot,
        cot, cot_left, cot_right, given.at[0],
    )
    sent[0:RANK, :] = cot_left[0:RANK, mine_cols]
    sent[RANK:, :] = cot_right[0:RANK, mine_cols]
    for copy in outs:
        copy.wait()


def first_call(pos, *arrays):
    width = arrays[0].shape[1]
    two = 2 * GROUP
    any_spec = pl.BlockSpec(memory_space=pl.ANY)
    vmem = pl.BlockSpec(memory_space=pltpu.VMEM)
    out_shape = (
        jax.ShapeDtypeStruct((2 * RANK, width // 2), bf16),
        jax.ShapeDtypeStruct((2, 2 * RANK, width), bf16),
        jax.ShapeDtypeStruct((2, RANK, width), f32),
        jax.ShapeDtypeStruct((2, GROUP, RANK), f32),
        jax.ShapeDtypeStruct((2, RANK, RANK), f32),
        jax.ShapeDtypeStruct((GROUP, RANK), f32),
        jax.ShapeDtypeStruct((RANK, width), f32),
    )
    one = pltpu.VMEM((2, GROUP, width), bf16)
    both = pltpu.VMEM((2, two, width), bf16)
    pair = pltpu.VMEM((2 * RANK, width), bf16)
    state = pltpu.VMEM((2, RANK, width), f32)
    return pl.pallas_call(
        first_kernel,
        out_shape=out_shape,
        in_specs=[pl.BlockSpec(memory_space=pltpu.SMEM)] + [any_spec] * len(arrays),
        out_specs=(vmem, any_spec, any_spec, vmem, vmem, vmem, any_spec),
        scratch_shapes=[
            both, both, one, one, one, one,
            state, pair, pltpu.VMEM((2, 2 * RANK, width), bf16),
            state, pair, pair, pltpu.VMEM((2, 2, RANK, width), f32), pltpu.VMEM((RANK, width), f32),
            pltpu.SemaphoreType.DMA((25,)), pltpu.SemaphoreType.DMA((4,)),
        ],
        compiler_params=pltpu.CompilerParams(vmem_limit_bytes=VMEM),
        cost_estimate=pl.CostEstimate(flops=16 * 10**9, bytes_accessed=26 * 2**20, transcendentals=0),
    )(pos, *arrays)


def second_kernel(
    pos, got_mine, got_sib, keys_own, keys_sib, high_mine, high_got, low_mine, low_got, right_in, given_in, cots_own, cots_sib,
    hidden_in, gram_in,
    grad_out,
    k, high, low, right_pairs, given, received, cot, cot_left, cot_right, grad, sems, out_sems,
):
    core = pos[1]
    other = 1 - core
    width = keys_own.shape[-1]
    half = width // 2
    mine_cols = pl.ds(pl.multiple_of(core * half, half), half)
    sib_cols = pl.ds(pl.multiple_of(other * half, half), half)
    top, bottom = pl.ds(0, GROUP), pl.ds(GROUP, GROUP)
    def halves(mine, got, into, at):
        return [
            pltpu.make_async_copy(mine.at[top, :], into.at[core, :, mine_cols], sems.at[at + core]),
            pltpu.make_async_copy(mine.at[bottom, :], into.at[other, :, mine_cols], sems.at[at + other]),
            pltpu.make_async_copy(got.at[top, :], into.at[other, :, sib_cols], sems.at[at + 2 + other]),
            pltpu.make_async_copy(got.at[bottom, :], into.at[core, :, sib_cols], sems.at[at + 2 + core]),
        ]

    def wait_block(i):
        pltpu.make_async_copy(keys_own, k.at[i], sems.at[2 + i]).wait()
        pltpu.make_async_copy(right_in.at[i], right_pairs.at[i], sems.at[4 + i]).wait()
        for mine, into, at in ((high_mine, high, 6), (low_mine, low, 10)):
            for step, cols in ((0, mine_cols), (2, sib_cols)):
                pltpu.make_async_copy(mine.at[top, :], into.at[i, :, cols], sems.at[at + step + i]).wait()

    load_got = [
        pltpu.make_async_copy(got_mine, received.at[:, mine_cols], sems.at[0]),
        pltpu.make_async_copy(got_sib, received.at[:, sib_cols], sems.at[1]),
    ]
    load_blocks = (
        [
            pltpu.make_async_copy(keys_own, k.at[core], sems.at[2 + core]),
            pltpu.make_async_copy(keys_sib, k.at[other], sems.at[2 + other]),
            pltpu.make_async_copy(right_in.at[1], right_pairs.at[1], sems.at[5]),
        ]
        + halves(high_mine, high_got, high, 6)
        + halves(low_mine, low_got, low, 10)
        + [pltpu.make_async_copy(right_in.at[0], right_pairs.at[0], sems.at[4])]
    )
    load_later = [
        pltpu.make_async_copy(given_in, given, sems.at[14]),
        pltpu.make_async_copy(cots_own.at[:, mine_cols], grad.at[pl.ds(2 * GROUP, GROUP), :], sems.at[15]),
        pltpu.make_async_copy(cots_sib.at[:, mine_cols], grad.at[pl.ds(3 * GROUP, GROUP), :], sems.at[16]),
    ]
    for copy in load_got + load_blocks + load_later:
        copy.start()
    for copy in load_got:
        copy.wait()
    for cols in chunks(width):
        for part, pair in ((0, cot_left), (1, cot_right)):
            value = received[part * RANK : (part + 1) * RANK, cols]
            cot[part, :, cols] = value.astype(f32)
            pair[0:RANK, cols] = value
            pair[RANK:, cols] = jnp.zeros((RANK, CHUNK), bf16)
    peak = jnp.zeros((1, 1), f32)
    for i in (1, 0):
        wait_block(i)
        pair = right_pairs.at[i]
        hidden = hidden_in[i]
        back_cot, hidden_cot = backward_hidden(
            k.at[i], high.at[i], low.at[i], pair, hidden, gram_in[i], cot_left, cot_right
        )
        sh, sl = split(-RATE * hidden)
        bh, bl = split(back_cot)
        s_twice = jnp.concatenate([sh, sh], 1)
        b_twice = jnp.concatenate([bh, bh], 1)
        rows = pl.ds(pl.multiple_of(jnp.where(core == i, 0, GROUP), GROUP), GROUP)
        for j in range(0, half, CHUNK):
            cols = pl.ds(pl.multiple_of(core * half + j, CHUNK), CHUNK)
            value = (
                nn(s_twice, cot_right[:, cols])
                + nn(b_twice, pair[:, cols])
                + nn(sl, cot_right[0:RANK, cols])
                + nn(bl, pair[0:RANK, cols])
            )
            peak = jnp.maximum(peak, jnp.max(jnp.abs(value), axis=(0, 1), keepdims=True))
            grad[rows, j : j + CHUNK] = value.astype(bf16)
        if i == 1:
            for copy in load_later:
                copy.wait()
            backward_state(
                k.at[i], high.at[i], low.at[i], pair, hidden, back_cot, hidden_cot, cot, cot_left, cot_right, given
            )
    cots = jnp.max(jnp.abs(grad[2 * GROUP : 4 * GROUP, :].astype(f32)), axis=(0, 1), keepdims=True)
    bound = jnp.maximum(512.0 * (4.04 * peak + 6.0 * cots), 1e-26)
    power = jnp.clip(jnp.ceil(jnp.log2(jnp.broadcast_to(bound, (8, 128)))), -80.0, 127.0)
    first_row = lax.broadcasted_iota(jnp.int32, (EXTRA, half), 0) == 0
    grad[4 * GROUP :, :] = jnp.where(first_row, power[0:1, 0:1], 0.0).astype(bf16)
    scale = jnp.exp2(TOP - power[0:1, 0:1])
    outs = []
    for part in range(5):
        rows = pl.ds(part * GROUP, GROUP if part < 4 else EXTRA)
        if part < 4:
            grad[rows, :] = (grad[rows, :].astype(f32) * scale).astype(bf16)
        outs.append(pltpu.make_async_copy(grad.at[rows, :], grad_out.at[rows, :], out_sems.at[part]))
        outs[-1].start()
    for out in outs:
        out.wait()


def second_call(pos, *arrays):
    width = arrays[2].shape[1]
    half = width // 2
    any_spec = pl.BlockSpec(memory_space=pl.ANY)
    vmem = pl.BlockSpec(memory_space=pltpu.VMEM)
    one = pltpu.VMEM((2, GROUP, width), bf16)
    pair = pltpu.VMEM((2 * RANK, width), bf16)
    state = pltpu.VMEM((2, RANK, width), f32)
    return pl.pallas_call(
        second_kernel,
        out_shape=jax.ShapeDtypeStruct((4 * GROUP + EXTRA, half), bf16),
        in_specs=[pl.BlockSpec(memory_space=pltpu.SMEM)] + [any_spec] * (len(arrays) - 2) + [vmem] * 2,
        out_specs=any_spec,
        scratch_shapes=[
            one, one, one, pltpu.VMEM((2, 2 * RANK, width), bf16), state, pair, state, pair, pair,
            pltpu.VMEM((4 * GROUP + EXTRA, half), bf16),
            pltpu.SemaphoreType.DMA((17,)), pltpu.SemaphoreType.DMA((5,)),
        ],
        compiler_params=pltpu.CompilerParams(vmem_limit_bytes=VMEM),
        cost_estimate=pl.CostEstimate(flops=8 * 10**9, bytes_accessed=14 * 2**20, transcendentals=0),
    )(pos, *arrays)


ORDER = (0, 1, 3, 2)
EXTRA = 16
PART = 512 + 128


def permute_kernel(pos, keys_own, keys_sib, queries_own, queries_sib, out):
    core, along_x, along_z = pos[1], pos[2], pos[3]
    extra = lax.broadcasted_iota(jnp.int32, (EXTRA, EXTRA), 0) == 0
    out[4 * GROUP :, :] = jnp.zeros((EXTRA, 4 * PART), bf16)
    for at, first in enumerate(ORDER):
        for second in range(4):
            by_x = lax.rem(along_x + jnp.where(core == 0, first, second), 4)
            by_z = lax.rem(along_z + jnp.where(core == 0, second, first), 4)
            source = pl.ds(pl.multiple_of((by_x * 4 + by_z) * 128, 128), 128)
            for i, tokens in enumerate((keys_own, keys_sib, queries_own, queries_sib)):
                out[i * GROUP : (i + 1) * GROUP, PART * at + 128 * second : PART * at + 128 * (second + 1)] = tokens[:, source]
        out[0 : 4 * GROUP, PART * at + 512 : PART * (at + 1)] = jnp.zeros((4 * GROUP, PART - 512), bf16)
        out[4 * GROUP :, PART * at + 512 : PART * at + 512 + EXTRA] = extra.astype(bf16)


def permute_call(pos, *arrays):
    vmem = pl.BlockSpec(memory_space=pltpu.VMEM)
    return pl.pallas_call(
        permute_kernel,
        out_shape=jax.ShapeDtypeStruct((4 * GROUP + EXTRA, 4 * PART), bf16),
        in_specs=[pl.BlockSpec(memory_space=pltpu.SMEM)] + [vmem] * 4,
        out_specs=vmem,
        compiler_params=pltpu.CompilerParams(vmem_limit_bytes=VMEM),
        cost_estimate=pl.CostEstimate(flops=0, bytes_accessed=9 * 2**20, transcendentals=0),
    )(pos, *arrays)


def assemble_kernel(pos, near, far1, far3, far2, out, sems):
    core, along_x, along_z = pos[1], pos[2], pos[3]
    copies = []
    for first, piece in ((0, near), (1, far1), (3, far3), (2, far2)):
        for second in range(4):
            by_x = lax.rem(along_x + jnp.where(core == 0, first, second), 4)
            by_z = lax.rem(along_z + jnp.where(core == 0, second, first), 4)
            rows = pl.ds(pl.multiple_of((by_x * 4 + by_z) * 128, 128), 128)
            copies.append(
                pltpu.make_async_copy(
                    piece.at[pl.ds(128 * second, 128), :], out.at[rows, :], sems.at[4 * first + second]
                )
            )
    for copy in copies:
        copy.start()
    for copy in copies:
        copy.wait()


def assemble_call(pos, *pieces):
    any_spec = pl.BlockSpec(memory_space=pl.ANY)
    rows, half = pieces[0].shape
    return pl.pallas_call(
        assemble_kernel,
        out_shape=jax.ShapeDtypeStruct((4 * rows, half), bf16),
        in_specs=[pl.BlockSpec(memory_space=pltpu.SMEM)] + [any_spec] * 4,
        out_specs=pl.BlockSpec(memory_space=pltpu.VMEM),
        scratch_shapes=[pltpu.SemaphoreType.DMA((16,))],
        compiler_params=pltpu.CompilerParams(vmem_limit_bytes=VMEM),
        cost_estimate=pl.CostEstimate(flops=0, bytes_accessed=8 * 2**20, transcendentals=0),
    )(pos, *pieces)


DP = ("x", "z", "yh")
SEQ = ("yl", "c")
ALL = ("x", "z", "yh", "yl", "c")
SIZES = (4, 4, 2, 2, 2)


def swap_cores(value):
    return lax.ppermute(value, "c", [(0, 1), (1, 0)])


def ring_pairs(by, x_core):
    pairs = []
    for place in np.ndindex(*SIZES):
        there = list(place)
        axis = 0 if place[4] == x_core else 1
        there[axis] = (place[axis] + by) % 4
        pairs.append((int(np.ravel_multi_index(place, SIZES)), int(np.ravel_multi_index(there, SIZES))))
    return pairs


def first_axis(value, by):
    return lax.ppermute(value, ALL, ring_pairs(by, 0))


def second_axis(value, by):
    return lax.ppermute(value, ALL, ring_pairs(by, 1))


def across(value):
    return lax.ppermute(value, ("yh", "yl"), [(0, 3), (3, 0), (1, 2), (2, 1)])


def along(value):
    return lax.ppermute(value, "yl", [(0, 1), (1, 0)])


def after(value, *others):
    return lax.optimization_barrier((value, *others))[0]


def dot(left, right):
    return jnp.dot(left, right, preferred_element_type=f32)


def add_up(arrays, rows):
    powers = [a[rows : rows + 1].astype(f32) for a in arrays]
    power = powers[0]
    for other in powers[1:]:
        power = jnp.maximum(power, other)
    power = power + (2.0 if len(arrays) == 4 else 1.0)
    total = 0.0
    for array, other in zip(arrays, powers):
        total = total + array.astype(f32) * jnp.exp2(other - power)
    return total, power


def packed(total, power):
    return jnp.concatenate([total, jnp.broadcast_to(power, (EXTRA, total.shape[1]))], 0).astype(f16)


def scatter_sum(left, right, beside):
    def product(at):
        return lax.dot_general(
            left[:, PART * at : PART * at + 512 + EXTRA],
            right,
            (((0,), (0,)), ((), ())),
            preferred_element_type=f32,
        )

    parts = {by: product(ORDER.index(by)).astype(f16) for by in (2, 1, 3)}
    got = [first_axis(parts[by], by) for by in (2, 1, 3)]
    own = product(0)
    other = beside(own)
    total, power = add_up([own] + got, 512)
    total = after(total, other)
    send = {by: packed(total[128 * by : 128 * (by + 1)], power) for by in (2, 1, 3)}
    got = [second_axis(send[by], by) for by in (2, 1, 3)]
    total, power = add_up([packed(total[:128], power).astype(f32)] + got, 128)
    low_half = lax.axis_index("yh") == 0
    keep = jnp.where(low_half, total[:64], total[64:128])
    give = jnp.where(low_half, total[64:128], total[:64])
    got = across(packed(give, power))
    total, power = add_up([packed(keep, power).astype(f32), got], 64)
    mine = packed(total[:64], power)
    total, power = add_up([mine.astype(f32), along(mine)], 64)
    return total[:64] * jnp.exp2(power - TOP), other


def per_device(key_tokens, value_tokens, query_tokens, cotangent, base_weight, factors):
    _, slice_len, width = key_tokens.shape
    half = width // 2
    core = lax.axis_index("c")
    place = jnp.stack([lax.axis_index(a) for a in ("yl", "c", "x", "z")]).astype(jnp.int32)

    def own_half(array):
        return lax.dynamic_slice_in_dim(array, core * half, half, 1)

    def other_half(array):
        return lax.dynamic_slice_in_dim(array, (1 - core) * half, half, 1)

    def join_halves(own, other):
        return jnp.where(
            core == 0, jnp.concatenate([own, other], 1), jnp.concatenate([other, own], 1)
        )

    keys, values, queries, cots = (a[0] for a in (key_tokens, value_tokens, query_tokens, cotangent))
    mine = own_half(base_weight)
    facing = across(mine)
    fkeys, fvalues = (lax.ppermute(a, "yl", [(0, 1)]) for a in (keys, values))
    near = jnp.where(
        lax.axis_index("yh") == 0,
        jnp.concatenate([mine, facing], 0),
        jnp.concatenate([facing, mine], 0),
    )
    near = jnp.concatenate([near] + [second_axis(near, by) for by in (3, 2, 1)], 0)
    factors_t = jnp.swapaxes(factors, 1, 2)
    near = after(near, factors_t)
    far1, far2, far3 = (first_axis(near, by) for by in (3, 2, 1))
    keys_sib, queries_sib, cots_sib = (swap_cores(a) for a in (keys, queries, cots))
    values_half = jnp.concatenate([own_half(values), swap_cores(other_half(values))], 0)
    weight = assemble_call(place, near, far1, far3, far2)

    def diff(tokens, tokens_sib, subtract):
        whole = dot(jnp.concatenate([tokens, tokens_sib], 0), weight) - subtract.astype(f32)
        high = lax.reduce_precision(whole, 8, 7)
        return high.astype(bf16), (whole - high).astype(bf16)

    high, low = diff(keys, keys_sib, values_half)
    high_got, low_got = swap_cores(high), swap_cores(low)
    fkeys_sib = swap_cores(fkeys)
    fvalues_half = jnp.concatenate([own_half(fvalues), swap_cores(other_half(fvalues))], 0)
    fhigh, flow = diff(fkeys, fkeys_sib, fvalues_half)
    fhigh_got, flow_got = swap_cores(fhigh), swap_cores(flow)

    sent, right, given, hidden, grams, recall_hidden, recall_right = first_call(
        place, keys, keys_sib, queries, queries_sib, cots, cots_sib, fkeys, fkeys_sib,
        high, high_got, low, low_got, fhigh, fhigh_got, flow, flow_got, factors_t,
    )
    got = lax.ppermute(sent, "yl", [(1, 0)])
    got_sib = swap_cores(got)
    grad = second_call(
        place, got, got_sib, keys, keys_sib, high, high_got, low, low_got, right, given, cots, cots_sib, hidden, grams
    )
    left = permute_call(place, keys, keys_sib, queries, queries_sib)

    def recall(own):
        qproj = dot(jnp.concatenate([queries, queries_sib], 0), after(weight, own))
        result = jnp.dot(recall_hidden, recall_right, precision=lax.Precision.HIGHEST)
        result += join_halves(qproj[:slice_len], swap_cores(qproj[slice_len:]))
        return result.astype(bf16)[None]

    share, recalled = scatter_sum(left, grad, recall)
    base_grad = join_halves(share, swap_cores(share))
    return (recalled, base_grad)


def solution(mesh):
    fine = Mesh(mesh.devices.reshape(SIZES), ALL)
    tokens = P(DP, SEQ, None)
    in_specs = (tokens, tokens, tokens, tokens, P(DP, None), P())
    out_specs = (tokens, P(DP, None))
    return jax.shard_map(
        per_device, mesh=fine, in_specs=in_specs, out_specs=out_specs, check_vma=False
    )
```

```python
import functools

import jax
import jax.numpy as jnp
import numpy as np
from jax import lax
from jax.experimental import pallas as pl
from jax.experimental.pallas import tpu as pltpu
from jax.sharding import Mesh, PartitionSpec as P

GROUP = 256
RANK = 128
CHUNK = 512
RATE = 0.01 / GROUP
TOP = 15.0
f32 = jnp.float32
bf16 = jnp.bfloat16
f16 = jnp.float16


def nt(a, b):
    return lax.dot_general(a, b, (((1,), (1,)), ((), ())), preferred_element_type=f32)


def nn(a, b):
    return lax.dot_general(a, b, (((1,), (0,)), ((), ())), preferred_element_type=f32)


def split(x):
    high = x.astype(bf16)
    return high, (x - high.astype(f32)).astype(bf16)


def fold_lanes(x):
    return x[:, :RANK] + x[:, RANK:]


def fold_rows(x):
    return x[:RANK] + x[RANK:]


def small(x, y):
    xh, xl = split(x)
    yh, yl = split(y)
    return nn(xh, yh) + nn(xl, yh) + nn(xh, yl)


def stack_pair(x):
    return jnp.concatenate(split(x), 0)


def gram(pair_a, pair_b):
    return fold_lanes(fold_rows(nt(pair_a, pair_b)))


def chunks(width):
    return [pl.ds(j, CHUNK) for j in range(0, width, CHUNK)]


def put_pair(pair, cols, value):
    high, low = split(value)
    pair[0:RANK, cols] = high
    pair[RANK:, cols] = low


class Square:
    def __init__(self, value):
        high, self.low = split(value)
        self.twice = jnp.concatenate([high, high], 1)

    def times(self, pair, cols):
        return nn(self.twice, pair[:, cols]) + nn(self.low, pair[0:RANK, cols])


def advance(keys, diff_high, diff_low, hidden, back, state, left_pair, right_old, right_new):
    back_pair = stack_pair((-RATE * back).T)
    hidden_t = (-RATE * hidden).T
    hidden_pair = stack_pair(hidden_t)
    own = Square(small(hidden_t, hidden))
    for cols in chunks(keys.shape[-1]):
        left = state[0, :, cols] + fold_rows(nn(back_pair, keys[:, cols]))
        right = (
            state[1, :, cols]
            + fold_rows(nn(hidden_pair, diff_high[:, cols]))
            + nn(hidden_pair[0:RANK], diff_low[:, cols])
            + own.times(right_old, cols)
        )
        state[0, :, cols] = left
        state[1, :, cols] = right
        put_pair(left_pair, cols, left)
        put_pair(right_new, cols, right)


def backward_hidden(keys, diff_high, diff_low, right_pair, hidden, gram_right, cot_left, cot_right):
    back_cot = -RATE * fold_lanes(nt(keys[...], cot_left[...]))
    diff_cot = fold_lanes(nt(diff_high[...], cot_right[...])) + nt(diff_low[...], cot_right[0:RANK, :])
    mixed = gram(cot_right[...], right_pair[...])
    hidden_cot = -RATE * (diff_cot + small(hidden, mixed + mixed.T)) + small(back_cot, gram_right)
    return back_cot, hidden_cot


def backward_state(keys, diff_high, diff_low, right_pair, hidden, back_cot, hidden_cot, cot, cot_left, cot_right, given):
    hidden_t = hidden.T
    back_t = back_cot.T
    own = Square(-RATE * small(hidden_t, hidden))
    cross = small(hidden_t, back_cot)
    cross = Square(cross + cross.T)
    hidden_cot_pair = stack_pair(hidden_cot.T)
    back_pair = stack_pair(back_t)
    for cols in chunks(keys.shape[-1]):
        left = cot[0, :, cols] + given[0, :, cols] + fold_rows(nn(hidden_cot_pair, keys[:, cols]))
        right = (
            cot[1, :, cols]
            + given[1, :, cols]
            + fold_rows(nn(back_pair, diff_high[:, cols]))
            + nn(back_pair[0:RANK], diff_low[:, cols])
            + own.times(cot_right, cols)
            + cross.times(right_pair, cols)
        )
        cot[0, :, cols] = left
        cot[1, :, cols] = right
        put_pair(cot_left, cols, left)
        put_pair(cot_right, cols, right)


def first_kernel(
    pos, keys_own, keys_sib, queries_own, queries_sib, cots_own, cots_sib, fkeys_own, fkeys_sib,
    high_mine, high_got, low_mine, low_got, fhigh_mine, fhigh_got, flow_mine, flow_got, factors,
    sent, right_out, given_out, hidden_out, gram_out, recall_hidden_out, recall_right_out,
    kq, uc, low, fk, fhigh, flow, state, left_pair, right_pairs, cot, cot_left, cot_right, given, kept,
    sems, out_sems,
):
    second = pos[0]
    core = pos[1]
    other = 1 - core
    width = keys_own.shape[-1]
    half = width // 2
    mine_cols = pl.ds(pl.multiple_of(core * half, half), half)
    sib_cols = pl.ds(pl.multiple_of(other * half, half), half)
    top, bottom = pl.ds(0, GROUP), pl.ds(GROUP, GROUP)
    def own_and_sib(own, sib, into, rows, at):
        return [
            pltpu.make_async_copy(own, into.at[core, rows, :], sems.at[at + core]),
            pltpu.make_async_copy(sib, into.at[other, rows, :], sems.at[at + other]),
        ]

    def halves(mine, got, into, rows, at):
        return [
            pltpu.make_async_copy(mine.at[top, :], into.at[core, rows, mine_cols], sems.at[at + core]),
            pltpu.make_async_copy(mine.at[bottom, :], into.at[other, rows, mine_cols], sems.at[at + other]),
            pltpu.make_async_copy(got.at[top, :], into.at[other, rows, sib_cols], sems.at[at + 2 + other]),
            pltpu.make_async_copy(got.at[bottom, :], into.at[core, rows, sib_cols], sems.at[at + 2 + core]),
        ]

    def wait_block(i, tokens, split_ones):
        for own, into, rows, at in tokens:
            pltpu.make_async_copy(own, into.at[i, rows, :], sems.at[at + i]).wait()
        for mine, into, rows, at in split_ones:
            for step, cols in ((0, mine_cols), (2, sib_cols)):
                pltpu.make_async_copy(mine.at[top, :], into.at[i, rows, cols], sems.at[at + step + i]).wait()

    load_state = pltpu.make_async_copy(factors, state, sems.at[0])
    load_f = (
        own_and_sib(fkeys_own, fkeys_sib, fk, top, 1)
        + halves(fhigh_mine, fhigh_got, fhigh, top, 3)
        + halves(flow_mine, flow_got, flow, top, 7)
    )
    load_own = (
        own_and_sib(keys_own, keys_sib, kq, top, 11)
        + own_and_sib(queries_own, queries_sib, kq, bottom, 13)
        + halves(high_mine, high_got, uc, top, 15)
        + own_and_sib(cots_own, cots_sib, uc, bottom, 19)
        + halves(low_mine, low_got, low, top, 21)
    )
    load_state.start()

    @pl.when(second == 1)
    def _():
        for copy in load_f:
            copy.start()

    for copy in load_own:
        copy.start()
    load_state.wait()
    for cols in chunks(width):
        put_pair(left_pair, cols, state[0, :, cols])
        put_pair(right_pairs.at[0], cols, state[1, :, cols])

    @pl.when(second == 1)
    def _():
        pair = right_pairs.at[0]
        for i in range(2):
            wait_block(i, [(fkeys_own, fk, top, 1)], [(fhigh_mine, fhigh, top, 3), (flow_mine, flow, top, 7)])
            hidden = fold_lanes(nt(fk[i], left_pair[...]))
            back = fold_lanes(nt(fhigh[i], pair[...])) + nt(flow[i], pair[0:RANK, :])
            back += small(hidden, gram(pair[...], pair[...]))
            advance(fk.at[i], fhigh.at[i], flow.at[i], hidden, back, state, left_pair, pair, pair)

    outs = []
    hiddens, grams, reads, spreads = [], [], [], []
    for i in range(2):
        wait_block(
            i,
            [(keys_own, kq, top, 11), (queries_own, kq, bottom, 13), (cots_own, uc, bottom, 19)],
            [(high_mine, uc, top, 15), (low_mine, low, top, 21)],
        )
        pair = right_pairs.at[i]
        copy = pltpu.make_async_copy(pair, right_out.at[i], out_sems.at[i])
        copy.start()
        outs.append(copy)

        @pl.when(core == i)
        def _():
            kept[...] = state[1, :, :]

        both = fold_lanes(nt(kq[i], left_pair[...]))
        hidden, read = both[:GROUP], both[GROUP:]
        both = fold_lanes(nt(uc[i], pair[...]))
        square = gram(pair[...], pair[...])
        hidden_out[i] = hidden
        gram_out[i] = square
        hiddens.append(hidden)
        grams.append(square)
        reads.append(read)
        spreads.append(both[GROUP:])
        if i == 0:
            back = both[:GROUP] + nt(low[i], pair[0:RANK, :]) + small(hidden, square)
            advance(
                kq.at[i, top, :], uc.at[i, top, :], low.at[i], hidden, back, state, left_pair, pair, right_pairs.at[1]
            )

    @pl.when(core == 0)
    def _():
        recall_hidden_out[...] = reads[0]

    @pl.when(core == 1)
    def _():
        recall_hidden_out[...] = reads[1]

    outs.append(pltpu.make_async_copy(kept, recall_right_out, out_sems.at[3]))
    outs[-1].start()

    for i in (1, 0):
        spread, read = stack_pair(spreads[i].T), stack_pair(reads[i].T)
        for cols in chunks(width):
            left = fold_rows(nn(spread, kq[i, bottom, cols]))
            right = fold_rows(nn(read, uc[i, bottom, cols]))
            given[i, 0, :, cols] = left
            given[i, 1, :, cols] = right
            if i == 1:
                cot[0, :, cols] = left
                cot[1, :, cols] = right
                put_pair(cot_left, cols, left)
                put_pair(cot_right, cols, right)
    outs.append(pltpu.make_async_copy(given.at[1], given_out, out_sems.at[2]))
    outs[-1].start()
    keys, diff_high = kq.at[0, top, :], uc.at[0, top, :]
    back_cot, hidden_cot = backward_hidden(
        keys, diff_high, low.at[0], right_pairs.at[0], hiddens[0], grams[0], cot_left, cot_right
    )
    backward_state(
        keys, diff_high, low.at[0], right_pairs.at[0], hiddens[0], back_cot, hidden_cot,
        cot, cot_left, cot_right, given.at[0],
    )
    sent[0:RANK, :] = cot_left[0:RANK, mine_cols]
    sent[RANK:, :] = cot_right[0:RANK, mine_cols]
    for copy in outs:
        copy.wait()


def first_call(pos, *arrays):
    width = arrays[0].shape[1]
    two = 2 * GROUP
    any_spec = pl.BlockSpec(memory_space=pl.ANY)
    vmem = pl.BlockSpec(memory_space=pltpu.VMEM)
    out_shape = (
        jax.ShapeDtypeStruct((2 * RANK, width // 2), bf16),
        jax.ShapeDtypeStruct((2, 2 * RANK, width), bf16),
        jax.ShapeDtypeStruct((2, RANK, width), f32),
        jax.ShapeDtypeStruct((2, GROUP, RANK), f32),
        jax.ShapeDtypeStruct((2, RANK, RANK), f32),
        jax.ShapeDtypeStruct((GROUP, RANK), f32),
        jax.ShapeDtypeStruct((RANK, width), f32),
    )
    one = pltpu.VMEM((2, GROUP, width), bf16)
    both = pltpu.VMEM((2, two, width), bf16)
    pair = pltpu.VMEM((2 * RANK, width), bf16)
    state = pltpu.VMEM((2, RANK, width), f32)
    return pl.pallas_call(
        first_kernel,
        out_shape=out_shape,
        in_specs=[pl.BlockSpec(memory_space=pltpu.SMEM)] + [any_spec] * len(arrays),
        out_specs=(vmem, any_spec, any_spec, vmem, vmem, vmem, any_spec),
        scratch_shapes=[
            both, both, one, one, one, one,
            state, pair, pltpu.VMEM((2, 2 * RANK, width), bf16),
            state, pair, pair, pltpu.VMEM((2, 2, RANK, width), f32), pltpu.VMEM((RANK, width), f32),
            pltpu.SemaphoreType.DMA((25,)), pltpu.SemaphoreType.DMA((4,)),
        ],
        compiler_params=pltpu.CompilerParams(vmem_limit_bytes=36 * 2**20),
        cost_estimate=pl.CostEstimate(flops=16 * 10**9, bytes_accessed=26 * 2**20, transcendentals=0),
    )(pos, *arrays)


def second_kernel(
    pos, got_mine, got_sib, keys_own, keys_sib, high_mine, high_got, low_mine, low_got, right_in, given_in, cots_own, cots_sib,
    hidden_in, gram_in,
    grad_out, power_out,
    k, high, low, right_pairs, given, received, cot, cot_left, cot_right, grad, sems, out_sems,
):
    core = pos[1]
    other = 1 - core
    width = keys_own.shape[-1]
    half = width // 2
    mine_cols = pl.ds(pl.multiple_of(core * half, half), half)
    sib_cols = pl.ds(pl.multiple_of(other * half, half), half)
    top, bottom = pl.ds(0, GROUP), pl.ds(GROUP, GROUP)
    def halves(mine, got, into, at):
        return [
            pltpu.make_async_copy(mine.at[top, :], into.at[core, :, mine_cols], sems.at[at + core]),
            pltpu.make_async_copy(mine.at[bottom, :], into.at[other, :, mine_cols], sems.at[at + other]),
            pltpu.make_async_copy(got.at[top, :], into.at[other, :, sib_cols], sems.at[at + 2 + other]),
            pltpu.make_async_copy(got.at[bottom, :], into.at[core, :, sib_cols], sems.at[at + 2 + core]),
        ]

    def wait_block(i):
        pltpu.make_async_copy(keys_own, k.at[i], sems.at[2 + i]).wait()
        pltpu.make_async_copy(right_in.at[i], right_pairs.at[i], sems.at[4 + i]).wait()
        for mine, into, at in ((high_mine, high, 6), (low_mine, low, 10)):
            for step, cols in ((0, mine_cols), (2, sib_cols)):
                pltpu.make_async_copy(mine.at[top, :], into.at[i, :, cols], sems.at[at + step + i]).wait()

    load_got = [
        pltpu.make_async_copy(got_mine, received.at[:, mine_cols], sems.at[0]),
        pltpu.make_async_copy(got_sib, received.at[:, sib_cols], sems.at[1]),
    ]
    load_blocks = (
        [
            pltpu.make_async_copy(keys_own, k.at[core], sems.at[2 + core]),
            pltpu.make_async_copy(keys_sib, k.at[other], sems.at[2 + other]),
            pltpu.make_async_copy(right_in.at[1], right_pairs.at[1], sems.at[5]),
        ]
        + halves(high_mine, high_got, high, 6)
        + halves(low_mine, low_got, low, 10)
        + [pltpu.make_async_copy(right_in.at[0], right_pairs.at[0], sems.at[4])]
    )
    load_later = [
        pltpu.make_async_copy(given_in, given, sems.at[14]),
        pltpu.make_async_copy(cots_own.at[:, mine_cols], grad.at[pl.ds(2 * GROUP, GROUP), :], sems.at[15]),
        pltpu.make_async_copy(cots_sib.at[:, mine_cols], grad.at[pl.ds(3 * GROUP, GROUP), :], sems.at[16]),
    ]
    for copy in load_got + load_blocks + load_later:
        copy.start()
    for copy in load_got:
        copy.wait()
    for cols in chunks(width):
        for part, pair in ((0, cot_left), (1, cot_right)):
            value = received[part * RANK : (part + 1) * RANK, cols]
            cot[part, :, cols] = value.astype(f32)
            pair[0:RANK, cols] = value
            pair[RANK:, cols] = jnp.zeros((RANK, CHUNK), bf16)
    peak = jnp.zeros((1, 1), f32)
    for i in (1, 0):
        wait_block(i)
        pair = right_pairs.at[i]
        hidden = hidden_in[i]
        back_cot, hidden_cot = backward_hidden(
            k.at[i], high.at[i], low.at[i], pair, hidden, gram_in[i], cot_left, cot_right
        )
        sh, sl = split(-RATE * hidden)
        bh, bl = split(back_cot)
        s_twice = jnp.concatenate([sh, sh], 1)
        b_twice = jnp.concatenate([bh, bh], 1)
        rows = pl.ds(pl.multiple_of(jnp.where(core == i, 0, GROUP), GROUP), GROUP)
        for j in range(0, half, CHUNK):
            cols = pl.ds(pl.multiple_of(core * half + j, CHUNK), CHUNK)
            value = (
                nn(s_twice, cot_right[:, cols])
                + nn(b_twice, pair[:, cols])
                + nn(sl, cot_right[0:RANK, cols])
                + nn(bl, pair[0:RANK, cols])
            )
            peak = jnp.maximum(peak, jnp.max(jnp.abs(value), axis=(0, 1), keepdims=True))
            grad[rows, j : j + CHUNK] = value.astype(bf16)
        if i == 1:
            for copy in load_later:
                copy.wait()
            backward_state(
                k.at[i], high.at[i], low.at[i], pair, hidden, back_cot, hidden_cot, cot, cot_left, cot_right, given
            )
    cots = jnp.max(jnp.abs(grad[2 * GROUP : 4 * GROUP, :].astype(f32)), axis=(0, 1), keepdims=True)
    bound = jnp.maximum(512.0 * (4.04 * peak + 6.0 * cots), 1e-26)
    power = jnp.clip(jnp.ceil(jnp.log2(jnp.broadcast_to(bound, (8, 128)))), -80.0, 127.0)
    power_out[...] = jnp.broadcast_to(power[0:1, 0:1], (EXTRA, half))
    scale = jnp.exp2(TOP - power[0:1, 0:1])
    outs = []
    for part in range(4):
        rows = pl.ds(part * GROUP, GROUP)
        grad[rows, :] = (grad[rows, :].astype(f32) * scale).astype(bf16)
        outs.append(pltpu.make_async_copy(grad.at[rows, :], grad_out.at[rows, :], out_sems.at[part]))
        outs[-1].start()
    for out in outs:
        out.wait()


def second_call(pos, *arrays):
    width = arrays[2].shape[1]
    half = width // 2
    any_spec = pl.BlockSpec(memory_space=pl.ANY)
    vmem = pl.BlockSpec(memory_space=pltpu.VMEM)
    one = pltpu.VMEM((2, GROUP, width), bf16)
    pair = pltpu.VMEM((2 * RANK, width), bf16)
    state = pltpu.VMEM((2, RANK, width), f32)
    return pl.pallas_call(
        second_kernel,
        out_shape=(jax.ShapeDtypeStruct((4 * GROUP, half), bf16), jax.ShapeDtypeStruct((EXTRA, half), f32)),
        in_specs=[pl.BlockSpec(memory_space=pltpu.SMEM)] + [any_spec] * (len(arrays) - 2) + [vmem] * 2,
        out_specs=(any_spec, vmem),
        scratch_shapes=[
            one, one, one, pltpu.VMEM((2, 2 * RANK, width), bf16), state, pair, state, pair, pair,
            pltpu.VMEM((4 * GROUP, half), bf16),
            pltpu.SemaphoreType.DMA((17,)), pltpu.SemaphoreType.DMA((4,)),
        ],
        compiler_params=pltpu.CompilerParams(vmem_limit_bytes=24 * 2**20),
        cost_estimate=pl.CostEstimate(flops=8 * 10**9, bytes_accessed=14 * 2**20, transcendentals=0),
    )(pos, *arrays)


EXTRA = 16


def permute_kernel(pos, keys_own, keys_sib, queries_own, queries_sib, *outs):
    core, along_x, along_z = pos[1], pos[2], pos[3]
    for first, out in enumerate(outs):
        for second in range(4):
            by_x = lax.rem(along_x + jnp.where(core == 0, first, second), 4)
            by_z = lax.rem(along_z + jnp.where(core == 0, second, first), 4)
            source = pl.ds(pl.multiple_of((by_x * 4 + by_z) * 128, 128), 128)
            for i, tokens in enumerate((keys_own, keys_sib, queries_own, queries_sib)):
                out[i * GROUP : (i + 1) * GROUP, 128 * second : 128 * (second + 1)] = tokens[:, source]


def permute_call(pos, *arrays):
    vmem = pl.BlockSpec(memory_space=pltpu.VMEM)
    return pl.pallas_call(
        permute_kernel,
        out_shape=(jax.ShapeDtypeStruct((4 * GROUP, 512), bf16),) * 4,
        in_specs=[pl.BlockSpec(memory_space=pltpu.SMEM)] + [vmem] * 4,
        out_specs=(vmem,) * 4,
        compiler_params=pltpu.CompilerParams(vmem_limit_bytes=14 * 2**20),
        cost_estimate=pl.CostEstimate(flops=0, bytes_accessed=8 * 2**20, transcendentals=0),
    )(pos, *arrays)


def assemble_kernel(pos, near, far1, far3, far2, out, sems):
    core, along_x, along_z = pos[1], pos[2], pos[3]
    copies = []
    for first, piece in ((0, near), (1, far1), (3, far3), (2, far2)):
        for second in range(4):
            by_x = lax.rem(along_x + jnp.where(core == 0, first, second), 4)
            by_z = lax.rem(along_z + jnp.where(core == 0, second, first), 4)
            rows = pl.ds(pl.multiple_of((by_x * 4 + by_z) * 128, 128), 128)
            copies.append(
                pltpu.make_async_copy(
                    piece.at[pl.ds(128 * second, 128), :], out.at[rows, :], sems.at[4 * first + second]
                )
            )
    for copy in copies:
        copy.start()
    for copy in copies:
        copy.wait()


def assemble_call(pos, *pieces):
    any_spec = pl.BlockSpec(memory_space=pl.ANY)
    rows, half = pieces[0].shape
    return pl.pallas_call(
        assemble_kernel,
        out_shape=jax.ShapeDtypeStruct((4 * rows, half), bf16),
        in_specs=[pl.BlockSpec(memory_space=pltpu.SMEM)] + [any_spec] * 4,
        out_specs=any_spec,
        scratch_shapes=[pltpu.SemaphoreType.DMA((16,))],
        compiler_params=pltpu.CompilerParams(vmem_limit_bytes=2 * 2**20),
        cost_estimate=pl.CostEstimate(flops=0, bytes_accessed=8 * 2**20, transcendentals=0),
    )(pos, *pieces)


DP = ("x", "z", "yh")
SEQ = ("yl", "c")
ALL = ("x", "z", "yh", "yl", "c")
SIZES = (4, 4, 2, 2, 2)


def swap_cores(value):
    return lax.ppermute(value, "c", [(0, 1), (1, 0)])


def ring_pairs(by, x_core):
    pairs = []
    for place in np.ndindex(*SIZES):
        there = list(place)
        axis = 0 if place[4] == x_core else 1
        there[axis] = (place[axis] + by) % 4
        pairs.append((int(np.ravel_multi_index(place, SIZES)), int(np.ravel_multi_index(there, SIZES))))
    return pairs


def first_axis(value, by):
    return lax.ppermute(value, ALL, ring_pairs(by, 0))


def second_axis(value, by):
    return lax.ppermute(value, ALL, ring_pairs(by, 1))


def across(value):
    return lax.ppermute(value, ("yh", "yl"), [(0, 3), (3, 0), (1, 2), (2, 1)])


def along(value):
    return lax.ppermute(value, "yl", [(0, 1), (1, 0)])


def after(value, *others):
    return lax.optimization_barrier((value, *others))[0]


def dot(left, right):
    return jnp.dot(left, right, preferred_element_type=f32)


def add_up(arrays, rows):
    powers = [a[rows : rows + 1].astype(f32) for a in arrays]
    power = powers[0]
    for other in powers[1:]:
        power = jnp.maximum(power, other)
    power = power + (2.0 if len(arrays) == 4 else 1.0)
    total = 0.0
    for array, other in zip(arrays, powers):
        total = total + array.astype(f32) * jnp.exp2(other - power)
    return total, power


def packed(total, power):
    return jnp.concatenate([total, jnp.broadcast_to(power, (EXTRA, total.shape[1]))], 0).astype(f16)


def scatter_sum(lefts, right, power, beside):
    def product(left):
        return lax.dot_general(left, right, (((0,), (0,)), ((), ())), preferred_element_type=f32)

    got = [
        first_axis(jnp.concatenate([product(lefts[by]).astype(f16), power.astype(f16)], 0), by)
        for by in (2, 1, 3)
    ]
    own = jnp.concatenate([product(lefts[0]), power], 0)
    total, power = add_up([after(own, beside)] + got, 512)
    send = {by: packed(total[128 * by : 128 * (by + 1)], power) for by in (2, 1, 3)}
    got = [second_axis(send[by], by) for by in (2, 1, 3)]
    total, power = add_up([packed(total[:128], power).astype(f32)] + got, 128)
    low_half = lax.axis_index("yh") == 0
    keep = jnp.where(low_half, total[:64], total[64:128])
    give = jnp.where(low_half, total[64:128], total[:64])
    got = across(packed(give, power))
    total, power = add_up([packed(keep, power).astype(f32), got], 64)
    mine = packed(total[:64], power)
    pairs = [mine, along(mine)], [swap_cores(mine), lax.ppermute(mine, ("yl", "c"), [(0, 3), (3, 0), (1, 2), (2, 1)])]
    own, other = (add_up(pair, 64) for pair in pairs)
    own, other = (total[:64] * jnp.exp2(power - TOP) for total, power in (own, other))
    return jnp.where(
        lax.axis_index("c") == 0, jnp.concatenate([own, other], 1), jnp.concatenate([other, own], 1)
    )


def per_device(key_tokens, value_tokens, query_tokens, cotangent, base_weight, factors):
    _, slice_len, width = key_tokens.shape
    half = width // 2
    core = lax.axis_index("c")
    place = jnp.stack([lax.axis_index(a) for a in ("yl", "c", "x", "z")]).astype(jnp.int32)

    def own_half(array):
        return lax.dynamic_slice_in_dim(array, core * half, half, 1)

    def other_half(array):
        return lax.dynamic_slice_in_dim(array, (1 - core) * half, half, 1)

    def join_halves(own, other):
        return jnp.where(
            core == 0, jnp.concatenate([own, other], 1), jnp.concatenate([other, own], 1)
        )

    keys, values, queries, cots = (a[0] for a in (key_tokens, value_tokens, query_tokens, cotangent))
    mine = own_half(base_weight)
    facing = across(mine)
    fkeys, fvalues = (lax.ppermute(a, "yl", [(0, 1)]) for a in (keys, values))
    near = jnp.where(
        lax.axis_index("yh") == 0,
        jnp.concatenate([mine, facing], 0),
        jnp.concatenate([facing, mine], 0),
    )
    near = jnp.concatenate([near] + [second_axis(near, by) for by in (3, 2, 1)], 0)
    factors_t = jnp.swapaxes(factors, 1, 2)
    near = after(near, factors_t)
    far1, far2, far3 = (first_axis(near, by) for by in (3, 2, 1))
    keys_sib, queries_sib, cots_sib = (swap_cores(a) for a in (keys, queries, cots))
    weight = assemble_call(place, near, far1, far3, far2)

    def diff(proj, subtract):
        whole = after(proj, weight) - subtract.astype(f32)
        high = lax.reduce_precision(whole, 8, 7)
        return high.astype(bf16), (whole - high).astype(bf16)

    fkeys_sib = swap_cores(fkeys)
    values_half = jnp.concatenate([own_half(values), swap_cores(other_half(values))], 0)
    fvalues_half = jnp.concatenate([own_half(fvalues), swap_cores(other_half(fvalues))], 0)
    proj = dot(jnp.concatenate([keys, keys_sib], 0), weight)
    high, low = diff(proj, values_half)
    high_got, low_got = swap_cores(high), swap_cores(low)
    fproj = dot(jnp.concatenate([fkeys, fkeys_sib], 0), after(weight, high))
    fhigh, flow = diff(fproj, fvalues_half)
    fhigh_got, flow_got = swap_cores(fhigh), swap_cores(flow)
    qproj = dot(jnp.concatenate([queries, queries_sib], 0), after(weight, fhigh))

    sent, right, given, hidden, grams, recall_hidden, recall_right = first_call(
        after(place, qproj), keys, keys_sib, queries, queries_sib, cots, cots_sib, fkeys, fkeys_sib,
        high, high_got, low, low_got, fhigh, fhigh_got, flow, flow_got, factors_t,
    )
    got = lax.ppermute(sent, "yl", [(1, 0)])
    got_sib = swap_cores(got)
    grad, power = second_call(
        place, got, got_sib, keys, keys_sib, high, high_got, low, low_got, right, given, cots, cots_sib, hidden, grams
    )
    lefts = permute_call(after(place, sent), keys, keys_sib, queries, queries_sib)
    recalled = jnp.dot(recall_hidden, after(recall_right, grad), precision=lax.Precision.HIGHEST)
    recalled += join_halves(qproj[:slice_len], swap_cores(qproj[slice_len:]))
    recalled = recalled.astype(bf16)[None]
    return (recalled, scatter_sum(lefts, grad, power, recalled))


def solution(mesh):
    fine = Mesh(mesh.devices.reshape(SIZES), ALL)
    tokens = P(DP, SEQ, None)
    in_specs = (tokens, tokens, tokens, tokens, P(DP, None), P())
    out_specs = (tokens, P(DP, None))
    return jax.shard_map(
        per_device, mesh=fine, in_specs=in_specs, out_specs=out_specs, check_vma=False
    )
```

```python
import functools

import jax
import jax.numpy as jnp
import numpy as np
from jax import lax
from jax.experimental import pallas as pl
from jax.experimental.pallas import tpu as pltpu
from jax.sharding import Mesh, PartitionSpec as P

GROUP = 256
RANK = 128
CHUNK = 512
RATE = 0.01 / GROUP
TOP = 15.0
f32 = jnp.float32
bf16 = jnp.bfloat16
f16 = jnp.float16


def nt(a, b):
    return lax.dot_general(a, b, (((1,), (1,)), ((), ())), preferred_element_type=f32)


def nn(a, b):
    return lax.dot_general(a, b, (((1,), (0,)), ((), ())), preferred_element_type=f32)


def split(x):
    high = x.astype(bf16)
    return high, (x - high.astype(f32)).astype(bf16)


def fold_lanes(x):
    return x[:, :RANK] + x[:, RANK:]


def fold_rows(x):
    return x[:RANK] + x[RANK:]


def small(x, y):
    xh, xl = split(x)
    yh, yl = split(y)
    return nn(xh, yh) + nn(xl, yh) + nn(xh, yl)


def stack_pair(x):
    return jnp.concatenate(split(x), 0)


def gram(pair_a, pair_b):
    return fold_lanes(fold_rows(nt(pair_a, pair_b)))


def chunks(width):
    return [pl.ds(j, CHUNK) for j in range(0, width, CHUNK)]


def put_pair(pair, cols, value):
    high, low = split(value)
    pair[0:RANK, cols] = high
    pair[RANK:, cols] = low


class Square:
    def __init__(self, value):
        high, self.low = split(value)
        self.twice = jnp.concatenate([high, high], 1)

    def times(self, pair, cols):
        return nn(self.twice, pair[:, cols]) + nn(self.low, pair[0:RANK, cols])


def advance(keys, diff_high, diff_low, hidden, back, state, left_pair, right_old, right_new):
    back_pair = stack_pair((-RATE * back).T)
    hidden_t = (-RATE * hidden).T
    hidden_pair = stack_pair(hidden_t)
    own = Square(small(hidden_t, hidden))
    for cols in chunks(keys.shape[-1]):
        left = state[0, :, cols] + fold_rows(nn(back_pair, keys[:, cols]))
        right = (
            state[1, :, cols]
            + fold_rows(nn(hidden_pair, diff_high[:, cols]))
            + nn(hidden_pair[0:RANK], diff_low[:, cols])
            + own.times(right_old, cols)
        )
        state[0, :, cols] = left
        state[1, :, cols] = right
        put_pair(left_pair, cols, left)
        put_pair(right_new, cols, right)


def backward_hidden(keys, diff_high, diff_low, right_pair, hidden, gram_right, cot_left, cot_right):
    back_cot = -RATE * fold_lanes(nt(keys[...], cot_left[...]))
    diff_cot = fold_lanes(nt(diff_high[...], cot_right[...])) + nt(diff_low[...], cot_right[0:RANK, :])
    mixed = gram(cot_right[...], right_pair[...])
    hidden_cot = -RATE * (diff_cot + small(hidden, mixed + mixed.T)) + small(back_cot, gram_right)
    return back_cot, hidden_cot


def backward_state(keys, diff_high, diff_low, right_pair, hidden, back_cot, hidden_cot, cot, cot_left, cot_right, given):
    hidden_t = hidden.T
    back_t = back_cot.T
    own = Square(-RATE * small(hidden_t, hidden))
    cross = small(hidden_t, back_cot)
    cross = Square(cross + cross.T)
    hidden_cot_pair = stack_pair(hidden_cot.T)
    back_pair = stack_pair(back_t)
    for cols in chunks(keys.shape[-1]):
        left = cot[0, :, cols] + given[0, :, cols] + fold_rows(nn(hidden_cot_pair, keys[:, cols]))
        right = (
            cot[1, :, cols]
            + given[1, :, cols]
            + fold_rows(nn(back_pair, diff_high[:, cols]))
            + nn(back_pair[0:RANK], diff_low[:, cols])
            + own.times(cot_right, cols)
            + cross.times(right_pair, cols)
        )
        cot[0, :, cols] = left
        cot[1, :, cols] = right
        put_pair(cot_left, cols, left)
        put_pair(cot_right, cols, right)


def first_kernel(
    pos, keys_own, keys_sib, queries_own, queries_sib, cots_own, cots_sib, fkeys_own, fkeys_sib,
    high_mine, high_got, low_mine, low_got, fhigh_mine, fhigh_got, flow_mine, flow_got, factors,
    sent, right_out, given_out, hidden_out, gram_out, recall_hidden_out, recall_right_out,
    kq, uc, low, fk, fhigh, flow, state, left_pair, right_pairs, cot, cot_left, cot_right, given, kept,
    sems, out_sems,
):
    second = pos[0]
    core = pos[1]
    other = 1 - core
    width = keys_own.shape[-1]
    half = width // 2
    mine_cols = pl.ds(pl.multiple_of(core * half, half), half)
    sib_cols = pl.ds(pl.multiple_of(other * half, half), half)
    top, bottom = pl.ds(0, GROUP), pl.ds(GROUP, GROUP)
    def own_and_sib(own, sib, into, rows, at):
        return [
            pltpu.make_async_copy(own, into.at[core, rows, :], sems.at[at + core]),
            pltpu.make_async_copy(sib, into.at[other, rows, :], sems.at[at + other]),
        ]

    def halves(mine, got, into, rows, at):
        return [
            pltpu.make_async_copy(mine.at[top, :], into.at[core, rows, mine_cols], sems.at[at + core]),
            pltpu.make_async_copy(mine.at[bottom, :], into.at[other, rows, mine_cols], sems.at[at + other]),
            pltpu.make_async_copy(got.at[top, :], into.at[other, rows, sib_cols], sems.at[at + 2 + other]),
            pltpu.make_async_copy(got.at[bottom, :], into.at[core, rows, sib_cols], sems.at[at + 2 + core]),
        ]

    def wait_block(i, tokens, split_ones):
        for own, into, rows, at in tokens:
            pltpu.make_async_copy(own, into.at[i, rows, :], sems.at[at + i]).wait()
        for mine, into, rows, at in split_ones:
            for step, cols in ((0, mine_cols), (2, sib_cols)):
                pltpu.make_async_copy(mine.at[top, :], into.at[i, rows, cols], sems.at[at + step + i]).wait()

    load_state = pltpu.make_async_copy(factors, state, sems.at[0])
    load_f = (
        own_and_sib(fkeys_own, fkeys_sib, fk, top, 1)
        + halves(fhigh_mine, fhigh_got, fhigh, top, 3)
        + halves(flow_mine, flow_got, flow, top, 7)
    )
    load_own = (
        own_and_sib(keys_own, keys_sib, kq, top, 11)
        + own_and_sib(queries_own, queries_sib, kq, bottom, 13)
        + halves(high_mine, high_got, uc, top, 15)
        + own_and_sib(cots_own, cots_sib, uc, bottom, 19)
        + halves(low_mine, low_got, low, top, 21)
    )
    load_state.start()

    @pl.when(second == 1)
    def _():
        for copy in load_f:
            copy.start()

    for copy in load_own:
        copy.start()
    load_state.wait()
    for cols in chunks(width):
        put_pair(left_pair, cols, state[0, :, cols])
        put_pair(right_pairs.at[0], cols, state[1, :, cols])

    @pl.when(second == 1)
    def _():
        pair = right_pairs.at[0]
        for i in range(2):
            wait_block(i, [(fkeys_own, fk, top, 1)], [(fhigh_mine, fhigh, top, 3), (flow_mine, flow, top, 7)])
            hidden = fold_lanes(nt(fk[i], left_pair[...]))
            back = fold_lanes(nt(fhigh[i], pair[...])) + nt(flow[i], pair[0:RANK, :])
            back += small(hidden, gram(pair[...], pair[...]))
            advance(fk.at[i], fhigh.at[i], flow.at[i], hidden, back, state, left_pair, pair, pair)

    outs = []
    hiddens, grams, reads, spreads = [], [], [], []
    for i in range(2):
        wait_block(
            i,
            [(keys_own, kq, top, 11), (queries_own, kq, bottom, 13), (cots_own, uc, bottom, 19)],
            [(high_mine, uc, top, 15), (low_mine, low, top, 21)],
        )
        pair = right_pairs.at[i]
        copy = pltpu.make_async_copy(pair, right_out.at[i], out_sems.at[i])
        copy.start()
        outs.append(copy)

        @pl.when(core == i)
        def _():
            kept[...] = state[1, :, :]

        both = fold_lanes(nt(kq[i], left_pair[...]))
        hidden, read = both[:GROUP], both[GROUP:]
        both = fold_lanes(nt(uc[i], pair[...]))
        square = gram(pair[...], pair[...])
        hidden_out[i] = hidden
        gram_out[i] = square
        hiddens.append(hidden)
        grams.append(square)
        reads.append(read)
        spreads.append(both[GROUP:])
        if i == 0:
            back = both[:GROUP] + nt(low[i], pair[0:RANK, :]) + small(hidden, square)
            advance(
                kq.at[i, top, :], uc.at[i, top, :], low.at[i], hidden, back, state, left_pair, pair, right_pairs.at[1]
            )

    @pl.when(core == 0)
    def _():
        recall_hidden_out[...] = reads[0]

    @pl.when(core == 1)
    def _():
        recall_hidden_out[...] = reads[1]

    outs.append(pltpu.make_async_copy(kept, recall_right_out, out_sems.at[3]))
    outs[-1].start()

    for i in (1, 0):
        spread, read = stack_pair(spreads[i].T), stack_pair(reads[i].T)
        for cols in chunks(width):
            left = fold_rows(nn(spread, kq[i, bottom, cols]))
            right = fold_rows(nn(read, uc[i, bottom, cols]))
            given[i, 0, :, cols] = left
            given[i, 1, :, cols] = right
            if i == 1:
                cot[0, :, cols] = left
                cot[1, :, cols] = right
                put_pair(cot_left, cols, left)
                put_pair(cot_right, cols, right)
    outs.append(pltpu.make_async_copy(given.at[1], given_out, out_sems.at[2]))
    outs[-1].start()
    keys, diff_high = kq.at[0, top, :], uc.at[0, top, :]
    back_cot, hidden_cot = backward_hidden(
        keys, diff_high, low.at[0], right_pairs.at[0], hiddens[0], grams[0], cot_left, cot_right
    )
    backward_state(
        keys, diff_high, low.at[0], right_pairs.at[0], hiddens[0], back_cot, hidden_cot,
        cot, cot_left, cot_right, given.at[0],
    )
    sent[0:RANK, :] = cot_left[0:RANK, mine_cols]
    sent[RANK:, :] = cot_right[0:RANK, mine_cols]
    for copy in outs:
        copy.wait()


def first_call(pos, *arrays):
    width = arrays[0].shape[1]
    two = 2 * GROUP
    any_spec = pl.BlockSpec(memory_space=pl.ANY)
    vmem = pl.BlockSpec(memory_space=pltpu.VMEM)
    out_shape = (
        jax.ShapeDtypeStruct((2 * RANK, width // 2), bf16),
        jax.ShapeDtypeStruct((2, 2 * RANK, width), bf16),
        jax.ShapeDtypeStruct((2, RANK, width), f32),
        jax.ShapeDtypeStruct((2, GROUP, RANK), f32),
        jax.ShapeDtypeStruct((2, RANK, RANK), f32),
        jax.ShapeDtypeStruct((GROUP, RANK), f32),
        jax.ShapeDtypeStruct((RANK, width), f32),
    )
    one = pltpu.VMEM((2, GROUP, width), bf16)
    both = pltpu.VMEM((2, two, width), bf16)
    pair = pltpu.VMEM((2 * RANK, width), bf16)
    state = pltpu.VMEM((2, RANK, width), f32)
    return pl.pallas_call(
        first_kernel,
        out_shape=out_shape,
        in_specs=[pl.BlockSpec(memory_space=pltpu.SMEM)] + [any_spec] * len(arrays),
        out_specs=(vmem, any_spec, any_spec, vmem, vmem, vmem, any_spec),
        scratch_shapes=[
            both, both, one, one, one, one,
            state, pair, pltpu.VMEM((2, 2 * RANK, width), bf16),
            state, pair, pair, pltpu.VMEM((2, 2, RANK, width), f32), pltpu.VMEM((RANK, width), f32),
            pltpu.SemaphoreType.DMA((25,)), pltpu.SemaphoreType.DMA((4,)),
        ],
        compiler_params=pltpu.CompilerParams(vmem_limit_bytes=36 * 2**20),
        cost_estimate=pl.CostEstimate(flops=16 * 10**9, bytes_accessed=26 * 2**20, transcendentals=0),
    )(pos, *arrays)


def second_kernel(
    pos, got_mine, got_sib, keys_own, keys_sib, high_mine, high_got, low_mine, low_got, right_in, given_in, cots_own, cots_sib,
    hidden_in, gram_in,
    grad_out, power_out,
    k, high, low, right_pairs, given, received, cot, cot_left, cot_right, grad, sems, out_sems,
):
    core = pos[1]
    other = 1 - core
    width = keys_own.shape[-1]
    half = width // 2
    mine_cols = pl.ds(pl.multiple_of(core * half, half), half)
    sib_cols = pl.ds(pl.multiple_of(other * half, half), half)
    top, bottom = pl.ds(0, GROUP), pl.ds(GROUP, GROUP)
    def halves(mine, got, into, at):
        return [
            pltpu.make_async_copy(mine.at[top, :], into.at[core, :, mine_cols], sems.at[at + core]),
            pltpu.make_async_copy(mine.at[bottom, :], into.at[other, :, mine_cols], sems.at[at + other]),
            pltpu.make_async_copy(got.at[top, :], into.at[other, :, sib_cols], sems.at[at + 2 + other]),
            pltpu.make_async_copy(got.at[bottom, :], into.at[core, :, sib_cols], sems.at[at + 2 + core]),
        ]

    def wait_block(i):
        pltpu.make_async_copy(keys_own, k.at[i], sems.at[2 + i]).wait()
        pltpu.make_async_copy(right_in.at[i], right_pairs.at[i], sems.at[4 + i]).wait()
        for mine, into, at in ((high_mine, high, 6), (low_mine, low, 10)):
            for step, cols in ((0, mine_cols), (2, sib_cols)):
                pltpu.make_async_copy(mine.at[top, :], into.at[i, :, cols], sems.at[at + step + i]).wait()

    load_got = [
        pltpu.make_async_copy(got_mine, received.at[:, mine_cols], sems.at[0]),
        pltpu.make_async_copy(got_sib, received.at[:, sib_cols], sems.at[1]),
    ]
    load_blocks = (
        [
            pltpu.make_async_copy(keys_own, k.at[core], sems.at[2 + core]),
            pltpu.make_async_copy(keys_sib, k.at[other], sems.at[2 + other]),
            pltpu.make_async_copy(right_in.at[1], right_pairs.at[1], sems.at[5]),
        ]
        + halves(high_mine, high_got, high, 6)
        + halves(low_mine, low_got, low, 10)
        + [pltpu.make_async_copy(right_in.at[0], right_pairs.at[0], sems.at[4])]
    )
    load_later = [
        pltpu.make_async_copy(given_in, given, sems.at[14]),
        pltpu.make_async_copy(cots_own.at[:, mine_cols], grad.at[pl.ds(2 * GROUP, GROUP), :], sems.at[15]),
        pltpu.make_async_copy(cots_sib.at[:, mine_cols], grad.at[pl.ds(3 * GROUP, GROUP), :], sems.at[16]),
    ]
    for copy in load_got + load_blocks + load_later:
        copy.start()
    for copy in load_got:
        copy.wait()
    for cols in chunks(width):
        for part, pair in ((0, cot_left), (1, cot_right)):
            value = received[part * RANK : (part + 1) * RANK, cols]
            cot[part, :, cols] = value.astype(f32)
            pair[0:RANK, cols] = value
            pair[RANK:, cols] = jnp.zeros((RANK, CHUNK), bf16)
    peak = jnp.zeros((1, 1), f32)
    for i in (1, 0):
        wait_block(i)
        pair = right_pairs.at[i]
        hidden = hidden_in[i]
        back_cot, hidden_cot = backward_hidden(
            k.at[i], high.at[i], low.at[i], pair, hidden, gram_in[i], cot_left, cot_right
        )
        sh, sl = split(-RATE * hidden)
        bh, bl = split(back_cot)
        s_twice = jnp.concatenate([sh, sh], 1)
        b_twice = jnp.concatenate([bh, bh], 1)
        rows = pl.ds(pl.multiple_of(jnp.where(core == i, 0, GROUP), GROUP), GROUP)
        for j in range(0, half, CHUNK):
            cols = pl.ds(pl.multiple_of(core * half + j, CHUNK), CHUNK)
            value = (
                nn(s_twice, cot_right[:, cols])
                + nn(b_twice, pair[:, cols])
                + nn(sl, cot_right[0:RANK, cols])
                + nn(bl, pair[0:RANK, cols])
            )
            peak = jnp.maximum(peak, jnp.max(jnp.abs(value), axis=(0, 1), keepdims=True))
            grad[rows, j : j + CHUNK] = value.astype(bf16)
        if i == 1:
            for copy in load_later:
                copy.wait()
            backward_state(
                k.at[i], high.at[i], low.at[i], pair, hidden, back_cot, hidden_cot, cot, cot_left, cot_right, given
            )
    cots = jnp.max(jnp.abs(grad[2 * GROUP : 4 * GROUP, :].astype(f32)), axis=(0, 1), keepdims=True)
    bound = jnp.maximum(512.0 * (4.04 * peak + 6.0 * cots), 1e-26)
    power = jnp.clip(jnp.ceil(jnp.log2(jnp.broadcast_to(bound, (8, 128)))), -80.0, 127.0)
    power_out[...] = jnp.broadcast_to(power[0:1, 0:1], (EXTRA, half))
    scale = jnp.exp2(TOP - power[0:1, 0:1])
    outs = []
    for part in range(4):
        rows = pl.ds(part * GROUP, GROUP)
        grad[rows, :] = (grad[rows, :].astype(f32) * scale).astype(bf16)
        outs.append(pltpu.make_async_copy(grad.at[rows, :], grad_out.at[rows, :], out_sems.at[part]))
        outs[-1].start()
    for out in outs:
        out.wait()


def second_call(pos, *arrays):
    width = arrays[2].shape[1]
    half = width // 2
    any_spec = pl.BlockSpec(memory_space=pl.ANY)
    vmem = pl.BlockSpec(memory_space=pltpu.VMEM)
    one = pltpu.VMEM((2, GROUP, width), bf16)
    pair = pltpu.VMEM((2 * RANK, width), bf16)
    state = pltpu.VMEM((2, RANK, width), f32)
    return pl.pallas_call(
        second_kernel,
        out_shape=(jax.ShapeDtypeStruct((4 * GROUP, half), bf16), jax.ShapeDtypeStruct((EXTRA, half), f32)),
        in_specs=[pl.BlockSpec(memory_space=pltpu.SMEM)] + [any_spec] * (len(arrays) - 2) + [vmem] * 2,
        out_specs=(any_spec, vmem),
        scratch_shapes=[
            one, one, one, pltpu.VMEM((2, 2 * RANK, width), bf16), state, pair, state, pair, pair,
            pltpu.VMEM((4 * GROUP, half), bf16),
            pltpu.SemaphoreType.DMA((17,)), pltpu.SemaphoreType.DMA((4,)),
        ],
        compiler_params=pltpu.CompilerParams(vmem_limit_bytes=24 * 2**20),
        cost_estimate=pl.CostEstimate(flops=8 * 10**9, bytes_accessed=14 * 2**20, transcendentals=0),
    )(pos, *arrays)


EXTRA = 16


def permute_kernel(pos, keys_own, keys_sib, queries_own, queries_sib, *outs):
    core, along_x, along_z = pos[1], pos[2], pos[3]
    for first, out in enumerate(outs):
        for second in range(4):
            by_x = lax.rem(along_x + jnp.where(core == 0, first, second), 4)
            by_z = lax.rem(along_z + jnp.where(core == 0, second, first), 4)
            source = pl.ds(pl.multiple_of((by_x * 4 + by_z) * 128, 128), 128)
            for i, tokens in enumerate((keys_own, keys_sib, queries_own, queries_sib)):
                out[i * GROUP : (i + 1) * GROUP, 128 * second : 128 * (second + 1)] = tokens[:, source]


def permute_call(pos, *arrays):
    vmem = pl.BlockSpec(memory_space=pltpu.VMEM)
    return pl.pallas_call(
        permute_kernel,
        out_shape=(jax.ShapeDtypeStruct((4 * GROUP, 512), bf16),) * 4,
        in_specs=[pl.BlockSpec(memory_space=pltpu.SMEM)] + [vmem] * 4,
        out_specs=(vmem,) * 4,
        compiler_params=pltpu.CompilerParams(vmem_limit_bytes=14 * 2**20),
        cost_estimate=pl.CostEstimate(flops=0, bytes_accessed=8 * 2**20, transcendentals=0),
    )(pos, *arrays)


def assemble_kernel(pos, near, far1, far3, far2, out, sems):
    core, along_x, along_z = pos[1], pos[2], pos[3]
    copies = []
    for first, piece in ((0, near), (1, far1), (3, far3), (2, far2)):
        for second in range(4):
            by_x = lax.rem(along_x + jnp.where(core == 0, first, second), 4)
            by_z = lax.rem(along_z + jnp.where(core == 0, second, first), 4)
            rows = pl.ds(pl.multiple_of((by_x * 4 + by_z) * 128, 128), 128)
            copies.append(
                pltpu.make_async_copy(
                    piece.at[pl.ds(128 * second, 128), :], out.at[rows, :], sems.at[4 * first + second]
                )
            )
    for copy in copies:
        copy.start()
    for copy in copies:
        copy.wait()


def assemble_call(pos, *pieces):
    any_spec = pl.BlockSpec(memory_space=pl.ANY)
    rows, half = pieces[0].shape
    return pl.pallas_call(
        assemble_kernel,
        out_shape=jax.ShapeDtypeStruct((4 * rows, half), bf16),
        in_specs=[pl.BlockSpec(memory_space=pltpu.SMEM)] + [any_spec] * 4,
        out_specs=any_spec,
        scratch_shapes=[pltpu.SemaphoreType.DMA((16,))],
        compiler_params=pltpu.CompilerParams(vmem_limit_bytes=2 * 2**20),
        cost_estimate=pl.CostEstimate(flops=0, bytes_accessed=8 * 2**20, transcendentals=0),
    )(pos, *pieces)


DP = ("x", "z", "yh")
SEQ = ("yl", "c")
ALL = ("x", "z", "yh", "yl", "c")
SIZES = (4, 4, 2, 2, 2)


def swap_cores(value):
    return lax.ppermute(value, "c", [(0, 1), (1, 0)])


def ring_pairs(by, x_core):
    pairs = []
    for place in np.ndindex(*SIZES):
        there = list(place)
        axis = 0 if place[4] == x_core else 1
        there[axis] = (place[axis] + by) % 4
        pairs.append((int(np.ravel_multi_index(place, SIZES)), int(np.ravel_multi_index(there, SIZES))))
    return pairs


def first_axis(value, by):
    return lax.ppermute(value, ALL, ring_pairs(by, 0))


def second_axis(value, by):
    return lax.ppermute(value, ALL, ring_pairs(by, 1))


def across(value):
    return lax.ppermute(value, ("yh", "yl"), [(0, 3), (3, 0), (1, 2), (2, 1)])


def along(value):
    return lax.ppermute(value, "yl", [(0, 1), (1, 0)])


def after(value, *others):
    return lax.optimization_barrier((value, *others))[0]


def dot(left, right):
    return jnp.dot(left, right, preferred_element_type=f32)


def add_up(arrays, rows):
    powers = [a[rows : rows + 1].astype(f32) for a in arrays]
    power = powers[0]
    for other in powers[1:]:
        power = jnp.maximum(power, other)
    power = power + (2.0 if len(arrays) == 4 else 1.0)
    factors = lax.optimization_barrier([jnp.exp2(other - power) for other in powers])
    total = 0.0
    for array, factor in zip(arrays, factors):
        total = total + array.astype(f32) * factor
    return total, power


def in_one_order(keep, near, facing, opposite):
    first = lax.axis_index("yl") == 0
    mine, other = (keep, opposite), (near, facing)
    low_half = lax.axis_index("yh") == 0
    mine = [jnp.where(low_half, a, b) for a, b in (mine, mine[::-1])]
    other = [jnp.where(low_half, a, b) for a, b in (other, other[::-1])]
    ordered = [jnp.where(first, a, b) for a, b in zip(mine + other, other + mine)]
    return add_up(ordered, 64)


def packed(total, power):
    return jnp.concatenate([total, jnp.broadcast_to(power, (EXTRA, total.shape[1]))], 0).astype(f16)


def scatter_sum(lefts, right, power, beside):
    def product(left):
        return lax.dot_general(left, right, (((0,), (0,)), ((), ())), preferred_element_type=f32)

    got = [
        first_axis(jnp.concatenate([product(lefts[by]).astype(f16), power.astype(f16)], 0), by)
        for by in (2, 1, 3)
    ]
    own = jnp.concatenate([product(lefts[0]), power], 0)
    total, power = add_up([after(own, beside)] + got, 512)
    send = {by: packed(total[128 * by : 128 * (by + 1)], power) for by in (2, 1, 3)}
    got = [second_axis(send[by], by) for by in (2, 1, 3)]
    total, power = add_up([packed(total[:128], power).astype(f32)] + got, 128)
    low_half = lax.axis_index("yh") == 0
    keep = packed(jnp.where(low_half, total[:64], total[64:128]), power)
    give = packed(jnp.where(low_half, total[64:128], total[:64]), power)
    opposite = lax.ppermute(give, "yh", [(0, 1), (1, 0)])
    total, power = in_one_order(keep, along(keep), across(give), opposite)
    own = total[:64] * jnp.exp2(power - TOP)
    other = swap_cores(own)
    return jnp.where(
        lax.axis_index("c") == 0, jnp.concatenate([own, other], 1), jnp.concatenate([other, own], 1)
    )


def per_device(key_tokens, value_tokens, query_tokens, cotangent, base_weight, factors):
    _, slice_len, width = key_tokens.shape
    half = width // 2
    core = lax.axis_index("c")
    place = jnp.stack([lax.axis_index(a) for a in ("yl", "c", "x", "z")]).astype(jnp.int32)

    def own_half(array):
        return lax.dynamic_slice_in_dim(array, core * half, half, 1)

    def other_half(array):
        return lax.dynamic_slice_in_dim(array, (1 - core) * half, half, 1)

    def join_halves(own, other):
        return jnp.where(
            core == 0, jnp.concatenate([own, other], 1), jnp.concatenate([other, own], 1)
        )

    keys, values, queries, cots = (a[0] for a in (key_tokens, value_tokens, query_tokens, cotangent))
    mine = own_half(base_weight)
    facing = across(mine)
    fkeys, fvalues = (lax.ppermute(a, "yl", [(0, 1)]) for a in (keys, values))
    near = jnp.where(
        lax.axis_index("yh") == 0,
        jnp.concatenate([mine, facing], 0),
        jnp.concatenate([facing, mine], 0),
    )
    near = jnp.concatenate([near] + [second_axis(near, by) for by in (3, 2, 1)], 0)
    factors_t = jnp.swapaxes(factors, 1, 2)
    near = after(near, factors_t)
    far1, far2, far3 = (first_axis(near, by) for by in (3, 2, 1))
    keys_sib, queries_sib, cots_sib = (swap_cores(a) for a in (keys, queries, cots))
    lefts = permute_call(place, keys, keys_sib, queries, queries_sib)
    weight = assemble_call(after(place, lefts), near, far1, far3, far2)

    def diff(proj, subtract):
        whole = after(proj, weight) - subtract.astype(f32)
        high = lax.reduce_precision(whole, 8, 7)
        return high.astype(bf16), (whole - high).astype(bf16)

    fkeys_sib = swap_cores(fkeys)
    fvalues_half = jnp.concatenate([own_half(fvalues), swap_cores(other_half(fvalues))], 0)
    values_half = jnp.concatenate([own_half(values), swap_cores(other_half(values))], 0)
    fproj = dot(jnp.concatenate([fkeys, fkeys_sib], 0), weight)
    fhigh, flow = diff(fproj, fvalues_half)
    fhigh_got, flow_got = swap_cores(fhigh), swap_cores(flow)
    proj = dot(jnp.concatenate([keys, keys_sib], 0), after(weight, fhigh))
    high, low = diff(proj, values_half)
    high_got, low_got = swap_cores(high), swap_cores(low)
    qproj = dot(jnp.concatenate([queries, queries_sib], 0), after(weight, high))

    sent, right, given, hidden, grams, recall_hidden, recall_right = first_call(
        after(place, qproj), keys, keys_sib, queries, queries_sib, cots, cots_sib, fkeys, fkeys_sib,
        high, high_got, low, low_got, fhigh, fhigh_got, flow, flow_got, factors_t,
    )
    got = lax.ppermute(sent, "yl", [(1, 0)])
    got_sib = swap_cores(got)
    grad, power = second_call(
        place, got, got_sib, keys, keys_sib, high, high_got, low, low_got, right, given, cots, cots_sib, hidden, grams
    )
    recalled = jnp.dot(recall_hidden, after(recall_right, grad), precision=lax.Precision.HIGHEST)
    recalled += join_halves(qproj[:slice_len], swap_cores(qproj[slice_len:]))
    recalled = recalled.astype(bf16)[None]
    return (recalled, scatter_sum(lefts, grad, power, recalled))


def solution(mesh):
    fine = Mesh(mesh.devices.reshape(SIZES), ALL)
    tokens = P(DP, SEQ, None)
    in_specs = (tokens, tokens, tokens, tokens, P(DP, None), P())
    out_specs = (tokens, P(DP, None))
    return jax.shard_map(
        per_device, mesh=fine, in_specs=in_specs, out_specs=out_specs, check_vma=False
    )
```

```python
import functools

import jax
import jax.numpy as jnp
import numpy as np
from jax import lax
from jax.experimental import pallas as pl
from jax.experimental.pallas import tpu as pltpu
from jax.sharding import Mesh, PartitionSpec as P

GROUP = 256
RANK = 128
CHUNK = 512
RATE = 0.01 / GROUP
TOP = 15.0
f32 = jnp.float32
bf16 = jnp.bfloat16
f16 = jnp.float16


def nt(a, b):
    return lax.dot_general(a, b, (((1,), (1,)), ((), ())), preferred_element_type=f32)


def nn(a, b):
    return lax.dot_general(a, b, (((1,), (0,)), ((), ())), preferred_element_type=f32)


def split(x):
    high = x.astype(bf16)
    return high, (x - high.astype(f32)).astype(bf16)


def fold_lanes(x):
    return x[:, :RANK] + x[:, RANK:]


def fold_rows(x):
    return x[:RANK] + x[RANK:]


def small(x, y):
    xh, xl = split(x)
    yh, yl = split(y)
    return nn(xh, yh) + nn(xl, yh) + nn(xh, yl)


def stack_pair(x):
    return jnp.concatenate(split(x), 0)


def gram(pair_a, pair_b):
    return fold_lanes(fold_rows(nt(pair_a, pair_b)))


def chunks(width):
    return [pl.ds(j, CHUNK) for j in range(0, width, CHUNK)]


def put_pair(pair, cols, value):
    high, low = split(value)
    pair[0:RANK, cols] = high
    pair[RANK:, cols] = low


class Square:
    def __init__(self, value):
        high, self.low = split(value)
        self.twice = jnp.concatenate([high, high], 1)

    def times(self, pair, cols):
        return nn(self.twice, pair[:, cols]) + nn(self.low, pair[0:RANK, cols])


def advance(keys, diff_high, diff_low, hidden, back, state, left_pair, right_old, right_new):
    back_pair = stack_pair((-RATE * back).T)
    hidden_t = (-RATE * hidden).T
    hidden_pair = stack_pair(hidden_t)
    own = Square(small(hidden_t, hidden))
    for cols in chunks(keys.shape[-1]):
        left = state[0, :, cols] + fold_rows(nn(back_pair, keys[:, cols]))
        right = (
            state[1, :, cols]
            + fold_rows(nn(hidden_pair, diff_high[:, cols]))
            + nn(hidden_pair[0:RANK], diff_low[:, cols])
            + own.times(right_old, cols)
        )
        state[0, :, cols] = left
        state[1, :, cols] = right
        put_pair(left_pair, cols, left)
        put_pair(right_new, cols, right)


def backward_hidden(keys, diff_high, diff_low, right_pair, hidden, gram_right, cot_left, cot_right):
    back_cot = -RATE * fold_lanes(nt(keys[...], cot_left[...]))
    diff_cot = fold_lanes(nt(diff_high[...], cot_right[...])) + nt(diff_low[...], cot_right[0:RANK, :])
    mixed = gram(cot_right[...], right_pair[...])
    hidden_cot = -RATE * (diff_cot + small(hidden, mixed + mixed.T)) + small(back_cot, gram_right)
    return back_cot, hidden_cot


def backward_state(keys, diff_high, diff_low, right_pair, hidden, back_cot, hidden_cot, cot, cot_left, cot_right, given):
    hidden_t = hidden.T
    back_t = back_cot.T
    own = Square(-RATE * small(hidden_t, hidden))
    cross = small(hidden_t, back_cot)
    cross = Square(cross + cross.T)
    hidden_cot_pair = stack_pair(hidden_cot.T)
    back_pair = stack_pair(back_t)
    for cols in chunks(keys.shape[-1]):
        left = cot[0, :, cols] + given[0, :, cols] + fold_rows(nn(hidden_cot_pair, keys[:, cols]))
        right = (
            cot[1, :, cols]
            + given[1, :, cols]
            + fold_rows(nn(back_pair, diff_high[:, cols]))
            + nn(back_pair[0:RANK], diff_low[:, cols])
            + own.times(cot_right, cols)
            + cross.times(right_pair, cols)
        )
        cot[0, :, cols] = left
        cot[1, :, cols] = right
        put_pair(cot_left, cols, left)
        put_pair(cot_right, cols, right)


def first_kernel(
    pos, keys_own, keys_sib, queries_own, queries_sib, cots_own, cots_sib, fkeys_own, fkeys_sib,
    high_mine, high_got, low_mine, low_got, fhigh_mine, fhigh_got, flow_mine, flow_got, factors,
    sent, right_out, given_out, hidden_out, gram_out, recall_hidden_out, recall_right_out,
    kq, uc, low, fk, fhigh, flow, state, left_pair, right_pairs, cot, cot_left, cot_right, given, kept,
    sems, out_sems,
):
    second = pos[0]
    core = pos[1]
    other = 1 - core
    width = keys_own.shape[-1]
    half = width // 2
    mine_cols = pl.ds(pl.multiple_of(core * half, half), half)
    sib_cols = pl.ds(pl.multiple_of(other * half, half), half)
    top, bottom = pl.ds(0, GROUP), pl.ds(GROUP, GROUP)
    def own_and_sib(own, sib, into, rows, at):
        return [
            pltpu.make_async_copy(own, into.at[core, rows, :], sems.at[at + core]),
            pltpu.make_async_copy(sib, into.at[other, rows, :], sems.at[at + other]),
        ]

    def halves(mine, got, into, rows, at):
        return [
            pltpu.make_async_copy(mine.at[top, :], into.at[core, rows, mine_cols], sems.at[at + core]),
            pltpu.make_async_copy(mine.at[bottom, :], into.at[other, rows, mine_cols], sems.at[at + other]),
            pltpu.make_async_copy(got.at[top, :], into.at[other, rows, sib_cols], sems.at[at + 2 + other]),
            pltpu.make_async_copy(got.at[bottom, :], into.at[core, rows, sib_cols], sems.at[at + 2 + core]),
        ]

    def wait_block(i, tokens, split_ones):
        for own, into, rows, at in tokens:
            pltpu.make_async_copy(own, into.at[i, rows, :], sems.at[at + i]).wait()
        for mine, into, rows, at in split_ones:
            for step, cols in ((0, mine_cols), (2, sib_cols)):
                pltpu.make_async_copy(mine.at[top, :], into.at[i, rows, cols], sems.at[at + step + i]).wait()

    load_state = pltpu.make_async_copy(factors, state, sems.at[0])
    load_f = (
        own_and_sib(fkeys_own, fkeys_sib, fk, top, 1)
        + halves(fhigh_mine, fhigh_got, fhigh, top, 3)
        + halves(flow_mine, flow_got, flow, top, 7)
    )
    load_own = (
        own_and_sib(keys_own, keys_sib, kq, top, 11)
        + own_and_sib(queries_own, queries_sib, kq, bottom, 13)
        + halves(high_mine, high_got, uc, top, 15)
        + own_and_sib(cots_own, cots_sib, uc, bottom, 19)
        + halves(low_mine, low_got, low, top, 21)
    )
    load_state.start()

    @pl.when(second == 1)
    def _():
        for copy in load_f:
            copy.start()

    for copy in load_own:
        copy.start()
    load_state.wait()
    for cols in chunks(width):
        put_pair(left_pair, cols, state[0, :, cols])
        put_pair(right_pairs.at[0], cols, state[1, :, cols])

    @pl.when(second == 1)
    def _():
        pair = right_pairs.at[0]
        for i in range(2):
            wait_block(i, [(fkeys_own, fk, top, 1)], [(fhigh_mine, fhigh, top, 3), (flow_mine, flow, top, 7)])
            hidden = fold_lanes(nt(fk[i], left_pair[...]))
            back = fold_lanes(nt(fhigh[i], pair[...])) + nt(flow[i], pair[0:RANK, :])
            back += small(hidden, gram(pair[...], pair[...]))
            advance(fk.at[i], fhigh.at[i], flow.at[i], hidden, back, state, left_pair, pair, pair)

    outs = []
    hiddens, grams, reads, spreads = [], [], [], []
    for i in range(2):
        wait_block(
            i,
            [(keys_own, kq, top, 11), (queries_own, kq, bottom, 13), (cots_own, uc, bottom, 19)],
            [(high_mine, uc, top, 15), (low_mine, low, top, 21)],
        )
        pair = right_pairs.at[i]
        copy = pltpu.make_async_copy(pair, right_out.at[i], out_sems.at[i])
        copy.start()
        outs.append(copy)

        @pl.when(core == i)
        def _():
            kept[...] = state[1, :, :]

        both = fold_lanes(nt(kq[i], left_pair[...]))
        hidden, read = both[:GROUP], both[GROUP:]
        both = fold_lanes(nt(uc[i], pair[...]))
        square = gram(pair[...], pair[...])
        hidden_out[i] = hidden
        gram_out[i] = square
        hiddens.append(hidden)
        grams.append(square)
        reads.append(read)
        spreads.append(both[GROUP:])
        if i == 0:
            back = both[:GROUP] + nt(low[i], pair[0:RANK, :]) + small(hidden, square)
            advance(
                kq.at[i, top, :], uc.at[i, top, :], low.at[i], hidden, back, state, left_pair, pair, right_pairs.at[1]
            )

    @pl.when(core == 0)
    def _():
        recall_hidden_out[...] = reads[0]

    @pl.when(core == 1)
    def _():
        recall_hidden_out[...] = reads[1]

    outs.append(pltpu.make_async_copy(kept, recall_right_out, out_sems.at[3]))
    outs[-1].start()

    for i in (1, 0):
        spread, read = stack_pair(spreads[i].T), stack_pair(reads[i].T)
        for cols in chunks(width):
            left = fold_rows(nn(spread, kq[i, bottom, cols]))
            right = fold_rows(nn(read, uc[i, bottom, cols]))
            given[i, 0, :, cols] = left
            given[i, 1, :, cols] = right
            if i == 1:
                cot[0, :, cols] = left
                cot[1, :, cols] = right
                put_pair(cot_left, cols, left)
                put_pair(cot_right, cols, right)
    outs.append(pltpu.make_async_copy(given.at[1], given_out, out_sems.at[2]))
    outs[-1].start()
    keys, diff_high = kq.at[0, top, :], uc.at[0, top, :]
    back_cot, hidden_cot = backward_hidden(
        keys, diff_high, low.at[0], right_pairs.at[0], hiddens[0], grams[0], cot_left, cot_right
    )
    backward_state(
        keys, diff_high, low.at[0], right_pairs.at[0], hiddens[0], back_cot, hidden_cot,
        cot, cot_left, cot_right, given.at[0],
    )
    sent[0:RANK, :] = cot_left[0:RANK, mine_cols]
    sent[RANK:, :] = cot_right[0:RANK, mine_cols]
    for copy in outs:
        copy.wait()


def first_call(pos, *arrays):
    width = arrays[0].shape[1]
    two = 2 * GROUP
    any_spec = pl.BlockSpec(memory_space=pl.ANY)
    vmem = pl.BlockSpec(memory_space=pltpu.VMEM)
    out_shape = (
        jax.ShapeDtypeStruct((2 * RANK, width // 2), bf16),
        jax.ShapeDtypeStruct((2, 2 * RANK, width), bf16),
        jax.ShapeDtypeStruct((2, RANK, width), f32),
        jax.ShapeDtypeStruct((2, GROUP, RANK), f32),
        jax.ShapeDtypeStruct((2, RANK, RANK), f32),
        jax.ShapeDtypeStruct((GROUP, RANK), f32),
        jax.ShapeDtypeStruct((RANK, width), f32),
    )
    one = pltpu.VMEM((2, GROUP, width), bf16)
    both = pltpu.VMEM((2, two, width), bf16)
    pair = pltpu.VMEM((2 * RANK, width), bf16)
    state = pltpu.VMEM((2, RANK, width), f32)
    return pl.pallas_call(
        first_kernel,
        out_shape=out_shape,
        in_specs=[pl.BlockSpec(memory_space=pltpu.SMEM)] + [any_spec] * len(arrays),
        out_specs=(vmem, any_spec, any_spec, vmem, vmem, vmem, any_spec),
        scratch_shapes=[
            both, both, one, one, one, one,
            state, pair, pltpu.VMEM((2, 2 * RANK, width), bf16),
            state, pair, pair, pltpu.VMEM((2, 2, RANK, width), f32), pltpu.VMEM((RANK, width), f32),
            pltpu.SemaphoreType.DMA((25,)), pltpu.SemaphoreType.DMA((4,)),
        ],
        compiler_params=pltpu.CompilerParams(vmem_limit_bytes=33 * 2**20),
        cost_estimate=pl.CostEstimate(flops=16 * 10**9, bytes_accessed=26 * 2**20, transcendentals=0),
    )(pos, *arrays)


def second_kernel(
    pos, got_mine, got_sib, keys_own, keys_sib, high_mine, high_got, low_mine, low_got, right_in, given_in, cots_own, cots_sib,
    hidden_in, gram_in,
    grad_out, power_out,
    k, high, low, right_pairs, given, received, cot, cot_left, cot_right, grad, sems, out_sems,
):
    core = pos[1]
    other = 1 - core
    width = keys_own.shape[-1]
    half = width // 2
    mine_cols = pl.ds(pl.multiple_of(core * half, half), half)
    sib_cols = pl.ds(pl.multiple_of(other * half, half), half)
    top, bottom = pl.ds(0, GROUP), pl.ds(GROUP, GROUP)
    def halves(mine, got, into, at):
        return [
            pltpu.make_async_copy(mine.at[top, :], into.at[core, :, mine_cols], sems.at[at + core]),
            pltpu.make_async_copy(mine.at[bottom, :], into.at[other, :, mine_cols], sems.at[at + other]),
            pltpu.make_async_copy(got.at[top, :], into.at[other, :, sib_cols], sems.at[at + 2 + other]),
            pltpu.make_async_copy(got.at[bottom, :], into.at[core, :, sib_cols], sems.at[at + 2 + core]),
        ]

    def wait_block(i):
        pltpu.make_async_copy(keys_own, k.at[i], sems.at[2 + i]).wait()
        pltpu.make_async_copy(right_in.at[i], right_pairs.at[i], sems.at[4 + i]).wait()
        for mine, into, at in ((high_mine, high, 6), (low_mine, low, 10)):
            for step, cols in ((0, mine_cols), (2, sib_cols)):
                pltpu.make_async_copy(mine.at[top, :], into.at[i, :, cols], sems.at[at + step + i]).wait()

    load_got = [
        pltpu.make_async_copy(got_mine, received.at[:, mine_cols], sems.at[0]),
        pltpu.make_async_copy(got_sib, received.at[:, sib_cols], sems.at[1]),
    ]
    load_blocks = (
        [
            pltpu.make_async_copy(keys_own, k.at[core], sems.at[2 + core]),
            pltpu.make_async_copy(keys_sib, k.at[other], sems.at[2 + other]),
            pltpu.make_async_copy(right_in.at[1], right_pairs.at[1], sems.at[5]),
        ]
        + halves(high_mine, high_got, high, 6)
        + halves(low_mine, low_got, low, 10)
        + [pltpu.make_async_copy(right_in.at[0], right_pairs.at[0], sems.at[4])]
    )
    load_later = [
        pltpu.make_async_copy(given_in, given, sems.at[14]),
        pltpu.make_async_copy(cots_own.at[:, mine_cols], grad.at[pl.ds(2 * GROUP, GROUP), :], sems.at[15]),
        pltpu.make_async_copy(cots_sib.at[:, mine_cols], grad.at[pl.ds(3 * GROUP, GROUP), :], sems.at[16]),
    ]
    for copy in load_got + load_blocks + load_later:
        copy.start()
    for copy in load_got:
        copy.wait()
    for cols in chunks(width):
        for part, pair in ((0, cot_left), (1, cot_right)):
            value = received[part * RANK : (part + 1) * RANK, cols]
            cot[part, :, cols] = value.astype(f32)
            pair[0:RANK, cols] = value
            pair[RANK:, cols] = jnp.zeros((RANK, CHUNK), bf16)
    peak = jnp.zeros((1, 1), f32)
    for i in (1, 0):
        wait_block(i)
        pair = right_pairs.at[i]
        hidden = hidden_in[i]
        back_cot, hidden_cot = backward_hidden(
            k.at[i], high.at[i], low.at[i], pair, hidden, gram_in[i], cot_left, cot_right
        )
        sh, sl = split(-RATE * hidden)
        bh, bl = split(back_cot)
        s_twice = jnp.concatenate([sh, sh], 1)
        b_twice = jnp.concatenate([bh, bh], 1)
        rows = pl.ds(pl.multiple_of(jnp.where(core == i, 0, GROUP), GROUP), GROUP)
        for j in range(0, half, CHUNK):
            cols = pl.ds(pl.multiple_of(core * half + j, CHUNK), CHUNK)
            value = (
                nn(s_twice, cot_right[:, cols])
                + nn(b_twice, pair[:, cols])
                + nn(sl, cot_right[0:RANK, cols])
                + nn(bl, pair[0:RANK, cols])
            )
            peak = jnp.maximum(peak, jnp.max(jnp.abs(value), axis=(0, 1), keepdims=True))
            grad[rows, j : j + CHUNK] = value.astype(bf16)
        if i == 1:
            for copy in load_later:
                copy.wait()
            backward_state(
                k.at[i], high.at[i], low.at[i], pair, hidden, back_cot, hidden_cot, cot, cot_left, cot_right, given
            )
    cots = jnp.max(jnp.abs(grad[2 * GROUP : 4 * GROUP, :].astype(f32)), axis=(0, 1), keepdims=True)
    bound = jnp.maximum(512.0 * (4.04 * peak + 6.0 * cots), 1e-26)
    power = jnp.clip(jnp.ceil(jnp.log2(jnp.broadcast_to(bound, (8, 128)))), -80.0, 127.0)
    power_out[...] = jnp.broadcast_to(power[0:1, 0:1], (EXTRA, half))
    scale = jnp.exp2(TOP - power[0:1, 0:1])
    outs = []
    for part in range(4):
        rows = pl.ds(part * GROUP, GROUP)
        grad[rows, :] = (grad[rows, :].astype(f32) * scale).astype(bf16)
        outs.append(pltpu.make_async_copy(grad.at[rows, :], grad_out.at[rows, :], out_sems.at[part]))
        outs[-1].start()
    for out in outs:
        out.wait()


def second_call(pos, *arrays):
    width = arrays[2].shape[1]
    half = width // 2
    any_spec = pl.BlockSpec(memory_space=pl.ANY)
    vmem = pl.BlockSpec(memory_space=pltpu.VMEM)
    one = pltpu.VMEM((2, GROUP, width), bf16)
    pair = pltpu.VMEM((2 * RANK, width), bf16)
    state = pltpu.VMEM((2, RANK, width), f32)
    return pl.pallas_call(
        second_kernel,
        out_shape=(jax.ShapeDtypeStruct((4 * GROUP, half), bf16), jax.ShapeDtypeStruct((EXTRA, half), f32)),
        in_specs=[pl.BlockSpec(memory_space=pltpu.SMEM)] + [any_spec] * (len(arrays) - 2) + [vmem] * 2,
        out_specs=(any_spec, vmem),
        scratch_shapes=[
            one, one, one, pltpu.VMEM((2, 2 * RANK, width), bf16), state, pair, state, pair, pair,
            pltpu.VMEM((4 * GROUP, half), bf16),
            pltpu.SemaphoreType.DMA((17,)), pltpu.SemaphoreType.DMA((4,)),
        ],
        compiler_params=pltpu.CompilerParams(vmem_limit_bytes=20 * 2**20),
        cost_estimate=pl.CostEstimate(flops=8 * 10**9, bytes_accessed=14 * 2**20, transcendentals=0),
    )(pos, *arrays)


EXTRA = 16


def permute_kernel(pos, keys_own, keys_sib, queries_own, queries_sib, *outs):
    core, along_x, along_z = pos[1], pos[2], pos[3]
    for first, out in enumerate(outs):
        for second in range(4):
            by_x = lax.rem(along_x + jnp.where(core == 0, first, second), 4)
            by_z = lax.rem(along_z + jnp.where(core == 0, second, first), 4)
            source = pl.ds(pl.multiple_of((by_x * 4 + by_z) * 128, 128), 128)
            for i, tokens in enumerate((keys_own, keys_sib, queries_own, queries_sib)):
                out[i * GROUP : (i + 1) * GROUP, 128 * second : 128 * (second + 1)] = tokens[:, source]


def permute_call(pos, *arrays):
    vmem = pl.BlockSpec(memory_space=pltpu.VMEM)
    return pl.pallas_call(
        permute_kernel,
        out_shape=(jax.ShapeDtypeStruct((4 * GROUP, 512), bf16),) * 4,
        in_specs=[pl.BlockSpec(memory_space=pltpu.SMEM)] + [vmem] * 4,
        out_specs=(vmem,) * 4,
        compiler_params=pltpu.CompilerParams(vmem_limit_bytes=14 * 2**20),
        cost_estimate=pl.CostEstimate(flops=0, bytes_accessed=8 * 2**20, transcendentals=0),
    )(pos, *arrays)


def assemble_kernel(pos, near, far1, far3, far2, out, sems):
    core, along_x, along_z = pos[1], pos[2], pos[3]
    copies = []
    for first, piece in ((0, near), (1, far1), (3, far3), (2, far2)):
        for second in range(4):
            by_x = lax.rem(along_x + jnp.where(core == 0, first, second), 4)
            by_z = lax.rem(along_z + jnp.where(core == 0, second, first), 4)
            rows = pl.ds(pl.multiple_of((by_x * 4 + by_z) * 128, 128), 128)
            copies.append(
                pltpu.make_async_copy(
                    piece.at[pl.ds(128 * second, 128), :], out.at[rows, :], sems.at[4 * first + second]
                )
            )
    for copy in copies:
        copy.start()
    for copy in copies:
        copy.wait()


def assemble_call(pos, *pieces):
    any_spec = pl.BlockSpec(memory_space=pl.ANY)
    rows, half = pieces[0].shape
    return pl.pallas_call(
        assemble_kernel,
        out_shape=jax.ShapeDtypeStruct((4 * rows, half), bf16),
        in_specs=[pl.BlockSpec(memory_space=pltpu.SMEM)] + [any_spec] * 4,
        out_specs=any_spec,
        scratch_shapes=[pltpu.SemaphoreType.DMA((16,))],
        compiler_params=pltpu.CompilerParams(vmem_limit_bytes=2 * 2**20),
        cost_estimate=pl.CostEstimate(flops=0, bytes_accessed=8 * 2**20, transcendentals=0),
    )(pos, *pieces)


DP = ("x", "z", "yh")
SEQ = ("yl", "c")
ALL = ("x", "z", "yh", "yl", "c")
SIZES = (4, 4, 2, 2, 2)


def swap_cores(value):
    return lax.ppermute(value, "c", [(0, 1), (1, 0)])


def ring_pairs(by, x_core):
    pairs = []
    for place in np.ndindex(*SIZES):
        there = list(place)
        axis = 0 if place[4] == x_core else 1
        there[axis] = (place[axis] + by) % 4
        pairs.append((int(np.ravel_multi_index(place, SIZES)), int(np.ravel_multi_index(there, SIZES))))
    return pairs


def first_axis(value, by):
    return lax.ppermute(value, ALL, ring_pairs(by, 0))


def second_axis(value, by):
    return lax.ppermute(value, ALL, ring_pairs(by, 1))


def across(value):
    return lax.ppermute(value, ("yh", "yl"), [(0, 3), (3, 0), (1, 2), (2, 1)])


def along(value):
    return lax.ppermute(value, "yl", [(0, 1), (1, 0)])


def after(value, *others):
    return lax.optimization_barrier((value, *others))[0]


def dot(left, right):
    return jnp.dot(left, right, preferred_element_type=f32)


def add_scaled(arrays, powers):
    power = powers[0]
    for other in powers[1:]:
        power = jnp.maximum(power, other)
    power = power + (2.0 if len(arrays) == 4 else 1.0)
    total = 0.0
    for array, other in zip(arrays, powers):
        total = total + array.astype(f32) * jnp.exp2(other - power)
    return total, power


def add_up(arrays, rows):
    return add_scaled(arrays, [a[rows : rows + 1].astype(f32) for a in arrays])


def in_one_order(keep, near, facing, opposite):
    first = lax.axis_index("yl") == 0
    mine, other = (keep, opposite), (near, facing)
    low_half = lax.axis_index("yh") == 0
    mine = [jnp.where(low_half, a, b) for a, b in (mine, mine[::-1])]
    other = [jnp.where(low_half, a, b) for a, b in (other, other[::-1])]
    ordered = [jnp.where(first, a, b) for a, b in zip(mine + other, other + mine)]
    return add_up(ordered, 64)


def packed(total, power):
    return jnp.concatenate([total, jnp.broadcast_to(power, (EXTRA, total.shape[1]))], 0).astype(f16)


def scatter_sum(lefts, right, power, beside):
    def product(left):
        return lax.dot_general(left, right, (((0,), (0,)), ((), ())), preferred_element_type=f32)

    power = power[:8]
    powers = [power] + [first_axis(power, by) for by in (2, 1, 3)]
    got = [first_axis(product(lefts[by]).astype(f16), by) for by in (2, 1, 3)]
    own = after(product(lefts[0]), beside)
    total, power = add_scaled([own] + got, [a[:1] for a in powers])
    send = {by: packed(total[128 * by : 128 * (by + 1)], power) for by in (2, 1, 3)}
    got = [second_axis(send[by], by) for by in (2, 1, 3)]
    total, power = add_up([packed(total[:128], power).astype(f32)] + got, 128)
    low_half = lax.axis_index("yh") == 0
    keep = packed(jnp.where(low_half, total[:64], total[64:128]), power)
    give = packed(jnp.where(low_half, total[64:128], total[:64]), power)
    opposite = lax.ppermute(give, "yh", [(0, 1), (1, 0)])
    total, power = in_one_order(keep, along(keep), across(give), opposite)
    own = total[:64] * jnp.exp2(power - TOP)
    other = swap_cores(own)
    return jnp.where(
        lax.axis_index("c") == 0, jnp.concatenate([own, other], 1), jnp.concatenate([other, own], 1)
    )


def per_device(key_tokens, value_tokens, query_tokens, cotangent, base_weight, factors):
    _, slice_len, width = key_tokens.shape
    half = width // 2
    core = lax.axis_index("c")
    place = jnp.stack([lax.axis_index(a) for a in ("yl", "c", "x", "z")]).astype(jnp.int32)

    def own_half(array):
        return lax.dynamic_slice_in_dim(array, core * half, half, 1)

    def other_half(array):
        return lax.dynamic_slice_in_dim(array, (1 - core) * half, half, 1)

    def join_halves(own, other):
        return jnp.where(
            core == 0, jnp.concatenate([own, other], 1), jnp.concatenate([other, own], 1)
        )

    keys, values, queries, cots = (a[0] for a in (key_tokens, value_tokens, query_tokens, cotangent))
    mine = own_half(base_weight)
    facing = across(mine)
    fkeys, fvalues = (lax.ppermute(a, "yl", [(0, 1)]) for a in (keys, values))
    near = jnp.where(
        lax.axis_index("yh") == 0,
        jnp.concatenate([mine, facing], 0),
        jnp.concatenate([facing, mine], 0),
    )
    near = jnp.concatenate([near] + [second_axis(near, by) for by in (3, 2, 1)], 0)
    factors_t = jnp.swapaxes(factors, 1, 2)
    near = after(near, factors_t)
    far1, far2, far3 = (first_axis(near, by) for by in (3, 2, 1))
    keys_sib, queries_sib, cots_sib = (swap_cores(a) for a in (keys, queries, cots))
    weight = assemble_call(place, near, far1, far3, far2)

    def diff(proj, subtract):
        whole = after(proj, weight) - subtract.astype(f32)
        high = lax.reduce_precision(whole, 8, 7)
        return high.astype(bf16), (whole - high).astype(bf16)

    fkeys_sib = swap_cores(fkeys)
    fvalues_half = jnp.concatenate([own_half(fvalues), swap_cores(other_half(fvalues))], 0)
    values_half = jnp.concatenate([own_half(values), swap_cores(other_half(values))], 0)
    fproj = dot(jnp.concatenate([fkeys, fkeys_sib], 0), weight)
    fhigh, flow = diff(fproj, fvalues_half)
    fhigh_got, flow_got = swap_cores(fhigh), swap_cores(flow)
    proj = dot(jnp.concatenate([keys, keys_sib], 0), after(weight, fhigh))
    high, low = diff(proj, values_half)
    high_got, low_got = swap_cores(high), swap_cores(low)
    qproj = dot(jnp.concatenate([queries, queries_sib], 0), after(weight, high))

    sent, right, given, hidden, grams, recall_hidden, recall_right = first_call(
        after(place, qproj), keys, keys_sib, queries, queries_sib, cots, cots_sib, fkeys, fkeys_sib,
        high, high_got, low, low_got, fhigh, fhigh_got, flow, flow_got, factors_t,
    )
    got = lax.ppermute(sent, "yl", [(1, 0)])
    lefts = permute_call(after(place, sent), keys, keys_sib, queries, queries_sib)
    got = after(got, *lefts)
    got_sib = swap_cores(got)
    grad, power = second_call(
        place, got, got_sib, keys, keys_sib, high, high_got, low, low_got, right, given, cots, cots_sib, hidden, grams
    )
    recalled = jnp.dot(recall_hidden, after(recall_right, grad), precision=lax.Precision.HIGHEST)
    recalled += join_halves(qproj[:slice_len], swap_cores(qproj[slice_len:]))
    recalled = recalled.astype(bf16)[None]
    return (recalled, scatter_sum(lefts, grad, power, recalled))


def solution(mesh):
    fine = Mesh(mesh.devices.reshape(SIZES), ALL)
    tokens = P(DP, SEQ, None)
    in_specs = (tokens, tokens, tokens, tokens, P(DP, None), P())
    out_specs = (tokens, P(DP, None))
    return jax.shard_map(
        per_device, mesh=fine, in_specs=in_specs, out_specs=out_specs, check_vma=False
    )
```
